32 devices in a mesh: section: 4 (over y, x), dp: 8 (over z, core).
Axes of the slice: x: 2, y: 2, z: 4, core: 2. Of those that a mesh axis runs over, the one named last changes fastest.
Arguments:
- tokens: bfloat16 [6400, 768], P(('dp', 'section')), may hold values from -6 to 6
- cotangent: bfloat16 [6400, 768], P(('dp', 'section')), may hold values from -6 to 6
- image_kind: int32 [16], P('dp'), may hold values from 0 to 2, as said below
- norm_one_gain: float32 [4, 768], P('section'), may hold values from 0.5 to 1.5
- norm_one_bias: float32 [4, 768], P('section'), may hold values from -1.8 to 1.8
- qkv_weight: bfloat16 [4, 768, 2304], P('section'), may hold values from -0.21875 to 0.21875
- qkv_bias: float32 [4, 2304], P('section'), may hold values from -1.8 to 1.8
- rotary_freq: float32 [4, 768], P('section'), may hold values from -1 to 1
- proj_weight: bfloat16 [4, 768, 768], P('section'), may hold values from -0.625 to 0.625
- proj_bias: float32 [4, 768], P('section'), may hold values from -1.8 to 1.8
- norm_two_gain: float32 [4, 768], P('section'), may hold values from 0.5 to 1.5
- norm_two_bias: float32 [4, 768], P('section'), may hold values from -1.8 to 1.8
- up_weight: bfloat16 [4, 768, 3072], P('section'), may hold values from -0.21875 to 0.21875
- up_bias: float32 [4, 3072], P('section'), may hold values from -1.8 to 1.8
- down_weight: bfloat16 [4, 3072, 768], P('section'), may hold values from -0.109375 to 0.109375
- down_bias: float32 [4, 768], P('section'), may hold values from -1.8 to 1.8
Outputs:
- block_out: bfloat16 [6400, 768], P(('dp', 'section'))
- grad_tokens: float32 [6400, 768], P(('dp', 'section'))
- grad_norm_one_gain: float32 [4, 768], P('section')
- grad_norm_one_bias: float32 [4, 768], P('section')
- grad_qkv_weight: float32 [4, 768, 2304], P('section')
- grad_qkv_bias: float32 [4, 2304], P('section')
- grad_rotary_freq: float32 [4, 768], P('section')
- grad_proj_weight: float32 [4, 768, 768], P('section')
- grad_proj_bias: float32 [4, 768], P('section')
- grad_norm_two_gain: float32 [4, 768], P('section')
- grad_norm_two_bias: float32 [4, 768], P('section')
- grad_up_weight: float32 [4, 768, 3072], P('section')
- grad_up_bias: float32 [4, 3072], P('section')
- grad_down_weight: float32 [4, 3072, 768], P('section')
- grad_down_bias: float32 [4, 768], P('section')
The draws below stay inside these ranges and needn't reach their ends.
Inputs may be any that keep to these rules, and one draw needn't show every extreme that they name: `image_kind`: 0: one image of 20 x 20 patches; 1: one image of 16 x 16; 2: two images of 14 x 14. Values 0 and 2 occur in every draw.
All inputs are finite; a program needn't handle non-finite values.
Results may differ from the reference program's by a relative error of at most 0.039.
Values may be sent and summed in bfloat16 or wider, within the bound.
No kernel may reach another device: no remote copies, remote signals or barrier semaphores. Data moves between devices by JAX's collectives and lax.ppermute only.
A program may use at most 448 MiB of HBM per device.

```python
import jax
import jax.numpy as jnp
from jax import lax

D = 768
HEADS = 12
FF = 3072
SIDE_LARGE = 20
SIDE_MID = 16
SIDE_SMALL = 14
ROWS = 400
LAYERS = 4
TOKENS = 6400
N_SECTION = 4


def draw_image_kind(key, part):
    key = jax.random.fold_in(key, 5)
    total_buffers = TOKENS // ROWS
    first_key, second_key, third_key = jax.random.split(key, 3)
    kind_list = jax.random.randint(first_key, (total_buffers,), 0, 3)
    first_place = jax.random.randint(second_key, (), 0, total_buffers)
    second_place = (first_place + 1 + jax.random.randint(third_key, (), 0, total_buffers - 1)) % total_buffers
    kind_list = kind_list.at[first_place].set(0).at[second_place].set(2)
    return kind_list.astype(jnp.int32)


def shard_levels(key, dims, pieces, least, largest):
    factor_of, own = 1.0, jax.random.fold_in(key, 6)
    for axis_at, parts in pieces:
        draws = jnp.exp(jax.random.uniform(jax.random.fold_in(own, axis_at), (parts,), jnp.float32, least / len(pieces), largest / len(pieces)))
        factor_of = factor_of * jnp.repeat(draws, dims[axis_at] // parts).reshape([-1 if axis == axis_at else 1 for axis in range(len(dims))])
    return factor_of


def scatter_about(own_key, dims, width, bound, pieces=(), held_as=jnp.bfloat16):
    values = width * jax.random.normal(own_key, dims, jnp.float32)
    if pieces:
        values = values * shard_levels(own_key, dims, pieces, -0.22, 0.18)
    return jnp.clip(values, -bound, bound).astype(held_as)


def setup_inputs(seed: int = 0) -> dict:
    keys = jax.random.split(jax.random.key(seed), 17)
    return {
        "tokens": scatter_about(keys[0], (TOKENS, D), 1.0, 6.0, ((0, 32),)),
        "cotangent": scatter_about(keys[1], (TOKENS, D), 1.0, 6.0, ((0, 32),)),
        "image_kind": draw_image_kind(jax.random.fold_in(keys[16], 71), 0),
        "norm_one_gain": jnp.clip(1.0 + 0.1 * jax.random.normal(keys[3], (LAYERS, D), jnp.float32), 0.5, 1.5),
        "norm_one_bias": scatter_about(keys[4], (LAYERS, D), 0.3, 1.8, ((0, 4),), jnp.float32),
        "qkv_weight": scatter_about(keys[5], (LAYERS, D, 3 * D), D ** -0.5, 0.21875, ((0, 4),)),
        "qkv_bias": scatter_about(keys[6], (LAYERS, 3 * D), 0.3, 1.8, ((0, 4),), jnp.float32),
        "rotary_freq": jnp.clip(jax.random.uniform(keys[7], (LAYERS, D), jnp.float32, -1.0, 1.0) * shard_levels(keys[7], (LAYERS, D), ((0, 4),), -0.4, 0.0), -1.0, 1.0),
        "proj_weight": scatter_about(keys[8], (LAYERS, D, D), (D // 8) ** -0.5, 0.625, ((0, 4),)),
        "proj_bias": scatter_about(keys[9], (LAYERS, D), 0.3, 1.8, ((0, 4),), jnp.float32),
        "norm_two_gain": jnp.clip(1.0 + 0.1 * jax.random.normal(keys[10], (LAYERS, D), jnp.float32), 0.5, 1.5),
        "norm_two_bias": scatter_about(keys[11], (LAYERS, D), 0.3, 1.8, ((0, 4),), jnp.float32),
        "up_weight": scatter_about(keys[12], (LAYERS, D, FF), D ** -0.5, 0.21875, ((0, 4),)),
        "up_bias": scatter_about(keys[13], (LAYERS, FF), 0.3, 1.8, ((0, 4),), jnp.float32),
        "down_weight": scatter_about(keys[14], (LAYERS, FF, D), FF ** -0.5, 0.109375, ((0, 4),)),
        "down_bias": scatter_about(keys[15], (LAYERS, D), 0.3, 1.8, ((0, 4),), jnp.float32),
    }


EPSILON = 1e-06
MASKED = -1e+30
HIGHEST = lax.Precision.HIGHEST

@jax.custom_vjp
def low(v):
    return lax.optimization_barrier(v.astype(jnp.bfloat16)).astype(jnp.float32)

@jax.custom_vjp
def low_back(v):
    return v

def low_keep(v):
    return (low(v), None)

def low_pass(kept, grad):
    return (grad,)

def back_keep(v):
    return (v, None)

def back_low(kept, grad):
    return (low(grad),)
low.defvjp(low_keep, low_pass)
low_back.defvjp(back_keep, back_low)

def geometry(kind_list):
    row_index = jnp.arange(ROWS, dtype=jnp.int32)[None, :]
    kind_col = kind_list[:, None]
    side_cells = jnp.where(kind_col == 0, SIDE_LARGE, jnp.where(kind_col == 1, SIDE_MID, SIDE_SMALL)).astype(jnp.int32)
    image_count = jnp.where(kind_col == 2, 2, 1).astype(jnp.int32)
    image_area = side_cells * side_cells
    image_index = row_index // image_area
    live_rows = image_index < image_count
    local_index = row_index - image_index * image_area
    patch_row = local_index // side_cells
    patch_col = local_index - patch_row * side_cells
    segment = jnp.where(live_rows, image_index, 3).astype(jnp.int32)
    patch_row = jnp.where(live_rows, patch_row, 0).astype(jnp.float32).reshape(-1)
    patch_col = jnp.where(live_rows, patch_col, 0).astype(jnp.float32).reshape(-1)
    return (patch_row, patch_col, segment, live_rows.astype(jnp.float32).reshape(-1))

def layer_norm(values):
    center = values - lax.optimization_barrier(jnp.mean(values, axis=-1, keepdims=True))
    return center * lax.rsqrt(lax.optimization_barrier(jnp.mean(center * center, axis=-1, keepdims=True)) + EPSILON)

def rotate(values, cosine, sine_part):
    half_dim = values.shape[-1] // 2
    first_half = values[..., :half_dim]
    second_half = values[..., half_dim:]
    return jnp.concatenate([first_half * cosine - second_half * sine_part, first_half * sine_part + second_half * cosine], axis=-1)

def attend(query, keys_in, value, segment):
    head_dim = query.shape[-1]
    scores = jnp.einsum('qhe,khe->hqk', query, keys_in, precision=HIGHEST) * head_dim ** (-0.5)
    scores = low_back(scores)
    same_image = segment[:, None] == segment[None, :]
    scores = jnp.where(same_image[None], scores, MASKED)
    attn_probs = low(jax.nn.softmax(scores, axis=-1))
    return jnp.einsum('hqk,khe->qhe', attn_probs, value, precision=HIGHEST)

def transformer_layer(hidden, weights, layout):
    gain_one, bias_one, qkv_weight, qkv_bias, frequency, proj_weight, proj_bias, gain_two, bias_two, up_weight, up_bias, down_weight, down_bias = weights
    patch_row, patch_col, segment, live_rows = layout
    model_width = hidden.shape[-1]
    head_dim = model_width // HEADS
    attn_in = low(layer_norm(hidden) * gain_one + bias_one)
    qkv_pre = low_back(jnp.dot(attn_in, qkv_weight, precision=HIGHEST) + qkv_bias)
    angles = (patch_row[:, None] * frequency[None, :model_width // 2] + patch_col[:, None] * frequency[None, model_width // 2:]).reshape(-1, HEADS, head_dim // 2)
    cosine = jnp.cos(angles)
    sine_part = jnp.sin(angles)
    query = low(rotate(qkv_pre[:, :model_width].reshape(-1, HEADS, head_dim), cosine, sine_part))
    keys_in = low(rotate(qkv_pre[:, model_width:2 * model_width].reshape(-1, HEADS, head_dim), cosine, sine_part))
    value = low(qkv_pre[:, 2 * model_width:].reshape(-1, HEADS, head_dim))
    attended = jax.checkpoint(attend)(query, keys_in, value, segment[0])
    attended = low(low_back(attended.reshape(-1, model_width)))
    middle = hidden + low_back(jnp.dot(attended, proj_weight, precision=HIGHEST) + proj_bias)
    mlp_in = low(layer_norm(middle) * gain_two + bias_two)
    up_pre = low_back(jnp.dot(mlp_in, up_weight, precision=HIGHEST) + up_bias)
    activated = low(jax.nn.gelu(up_pre, approximate=True))
    return middle + low_back(jnp.dot(activated, down_weight, precision=HIGHEST) + down_bias)

def reference(tokens, cotangent, image_kind, norm_one_gain, norm_one_bias, qkv_weight, qkv_bias, rotary_freq, proj_weight, proj_bias, norm_two_gain, norm_two_bias, up_weight, up_bias, down_weight, down_bias):
    params = tuple((item.astype(jnp.float32) for item in (norm_one_gain, norm_one_bias, qkv_weight, qkv_bias, rotary_freq, proj_weight, proj_bias, norm_two_gain, norm_two_bias, up_weight, up_bias, down_weight, down_bias)))
    model_width = tokens.shape[1]
    buffers = tokens.shape[0] // ROWS
    token_blocks = tokens.astype(jnp.float32).reshape(buffers, ROWS, model_width)
    cot_blocks = cotangent.astype(jnp.float32).reshape(buffers, ROWS, model_width)

    def one_buffer(totals, inputs):
        block_tokens, block_cot, kind_one = inputs
        layout = geometry(kind_one[None])

        def network(values, weights):
            hidden = values
            for layer_index in range(N_SECTION):
                if layer_index > 0:
                    hidden = low(low_back(hidden))
                hidden = transformer_layer(hidden, tuple((item[layer_index] for item in weights)), layout)
            return low(hidden)
        output, back_fn = jax.vjp(network, block_tokens, params)
        live_col = layout[3][:, None]
        grad_in, grad_params = back_fn(block_cot * live_col)
        totals = tuple((total + piece for total, piece in zip(totals, grad_params)))
        return (totals, (output * live_col, grad_in))
    zero_totals = tuple((jnp.zeros_like(item) for item in params))
    totals, (outputs, grads_in) = lax.scan(one_buffer, zero_totals, (token_blocks, cot_blocks, image_kind))
    g_one, b_one, w_qkv_g, b_qkv_g, freq_g, w_proj_g, b_proj_g, g_two, b_two, w_up_g, b_up_g, w_down_g, b_down_g = totals
    return (outputs.reshape(-1, model_width).astype(jnp.bfloat16), grads_in.reshape(-1, model_width), g_one, b_one, w_qkv_g, b_qkv_g, freq_g, w_proj_g, b_proj_g, g_two, b_two, w_up_g, b_up_g, w_down_g, b_down_g)
```

```python
from functools import partial
import math

import jax
import jax.numpy as jnp
import numpy as np
from jax import lax
from jax.experimental import pallas as pl
from jax.experimental.pallas import tpu as pltpu
from jax.sharding import PartitionSpec as P

HEADS = 12
SIDE_LARGE = 20
SIDE_MID = 16
SIDE_SMALL = 14
MICRO = 2
ROWS = 400
KEYS = 512
WIDTH = 768
HIDDEN = 3072
PAIRS = HEADS // 2
EPSILON = 1e-06
MASKED = -1e30
LOG2E = math.log2(math.e)
LN2 = math.log(2.0)
GELU_ONE = math.sqrt(2.0 / math.pi)
GELU_TWO = GELU_ONE * 0.044715

f32 = jnp.float32
bf16 = jnp.bfloat16
NT = (((1,), (1,)), ((), ()))

VEC_SIZES = (WIDTH, WIDTH, 3 * WIDTH, WIDTH, WIDTH, WIDTH, HIDDEN, WIDTH)
VEC_AT = tuple(int(v) for v in np.cumsum((0,) + VEC_SIZES))


def vec_part(vec_ref, index):
    return vec_ref[:, VEC_AT[index] : VEC_AT[index + 1]]


def swap_halves(values):
    lane = lax.broadcasted_iota(jnp.int32, values.shape, 1) % 64
    width = values.shape[1]
    return jnp.where(lane < 32, pltpu.roll(values, width - 32, 1), pltpu.roll(values, 32, 1))


def norm_parts(values):
    center = values - jnp.mean(values, axis=-1, keepdims=True)
    inverse = lax.rsqrt(jnp.mean(center * center, axis=-1, keepdims=True) + EPSILON)
    return center * inverse, inverse


def gelu_parts(pre):
    low = pre.astype(bf16)
    square = low * low
    tanh = jnp.tanh(low * (bf16(GELU_ONE) + bf16(GELU_TWO) * square))
    half = bf16(0.5) + bf16(0.5) * tanh
    value = low * half
    slope = half + (value - value * half) * (bf16(2 * GELU_ONE) + bf16(6 * GELU_TWO) * square)
    return value, slope


class Copies:
    def __init__(self, sems):
        self.sems = sems
        self.used = 0

    def start(self, source, target):
        copy = pltpu.make_async_copy(source, target, self.sems.at[self.used])
        self.used += 1
        copy.start()
        return copy


STATE_SHAPES = (
    ("x", (ROWS, WIDTH), bf16),
    ("a", (ROWS, WIDTH), bf16),
    ("qkv", (ROWS, 3 * WIDTH), bf16),
    ("e", (HEADS, ROWS, KEYS), bf16),
    ("linv", (ROWS, WIDTH), f32),
    ("o", (ROWS, WIDTH), bf16),
    ("n2", (ROWS, WIDTH), bf16),
    ("r2", (ROWS, 128), f32),
    ("c", (ROWS, WIDTH), bf16),
    ("g", (ROWS, HIDDEN), bf16),
    ("gp", (ROWS, HIDDEN), bf16),
)
STATES = tuple(name for name, _, _ in STATE_SHAPES)


def front_kernel(first, scal, *refs):
    ins, rest = refs[:8], refs[8:]
    x_in, vec_in, geo_in, cos_in, sin_in, wqkv_in, wp_in, wu_in = ins
    wd_in = rest[0]
    rest = rest[1:]
    if not first:
        rest = rest[len(STATES) :]
    out_ref = rest[0]
    state = dict(zip(STATES, rest[1 : 1 + len(STATES)]))
    (
        x_v, vec_v, geo_v, cos_v, sin_v, wqkv_v, wp_v, wu_v, wd_v,
        a_v, qkv_v, e_v, s_v, li_v, o_v, m_v, n2_v, r2_v, c_v, g_v, gp_v, qcode_v, kcode_v, out_v, sems,
    ) = rest[1 + len(STATES) :]

    @pl.when(scal[0] == 1)
    def _():
        slot = scal[1]
        copies = Copies(sems)
        get_x = copies.start(x_in, x_v)
        get_vec = copies.start(vec_in, vec_v)
        get_qkv = copies.start(wqkv_in, wqkv_v)
        get_cos = copies.start(cos_in.at[slot], cos_v)
        get_sin = copies.start(sin_in.at[slot], sin_v)
        get_geo = copies.start(geo_in.at[slot], geo_v)
        get_wp = copies.start(wp_in, wp_v)
        get_wu = copies.start(wu_in, wu_v)
        get_wd = copies.start(wd_in, wd_v)
        puts = []

        def put(source, name):
            puts.append(copies.start(source, state[name].at[slot]))

        get_x.wait()
        get_vec.wait()
        put(x_v, "x")
        normed, _ = norm_parts(x_v[...].astype(f32))
        a_v[...] = (normed * vec_part(vec_v, 0) + vec_part(vec_v, 1)).astype(bf16)
        put(a_v, "a")
        qkv_v[ROWS:KEYS, :] = jnp.zeros((KEYS - ROWS, 3 * WIDTH), bf16)
        get_geo.wait()
        segment = geo_v[:, 2:3]
        code = (lax.broadcasted_iota(jnp.int32, (KEYS, 128), 1) % 64).astype(f32)
        qcode_v[...] = jnp.where(segment[:ROWS] == code[:ROWS], 1.0, 0.0).astype(bf16)
        kcode_v[...] = jnp.where((segment != code) & (code < 4), MASKED, 0.0).astype(bf16)
        get_qkv.wait()
        get_cos.wait()
        get_sin.wait()
        for part in range(3):
            at = part * WIDTH
            acc = jnp.dot(a_v[...], wqkv_v[:, at : at + WIDTH], preferred_element_type=f32)
            acc = acc + vec_v[:, VEC_AT[2] + at : VEC_AT[2] + at + WIDTH]
            if part < 2:
                acc = acc * cos_v[...] + swap_halves(acc) * sin_v[...]
            if part == 0:
                acc = acc * (LOG2E / 8.0)
            qkv_v[:ROWS, at : at + WIDTH] = acc.astype(bf16)
        put(qkv_v.at[pl.ds(0, ROWS)], "qkv")

        def pair_step(pair, carry):
            lanes = pl.ds(pl.multiple_of(pair * 128, 128), 128)
            klanes = pl.ds(pl.multiple_of(pair * 128 + WIDTH, 128), 128)
            vlanes = pl.ds(pl.multiple_of(pair * 128 + 2 * WIDTH, 128), 128)
            q_two = qkv_v[:ROWS, lanes]
            k_two = qkv_v[:, klanes]
            v_two = qkv_v[:, vlanes]
            lane_q = lax.broadcasted_iota(jnp.int32, (ROWS, 128), 1) // 64
            lane_k = lax.broadcasted_iota(jnp.int32, (KEYS, 128), 1) // 64
            for head in range(2):
                q_one = jnp.where(lane_q == head, q_two, qcode_v[...])
                k_one = jnp.where(lane_k == head, k_two, kcode_v[...])
                s_v[head] = lax.dot_general(q_one, k_one, NT, preferred_element_type=f32)
            sums = []
            for head in range(2):
                v_one = jnp.where(lane_k == head, v_two, bf16(1.0))
                scores = s_v[head]
                peak = jnp.max(scores, axis=1, keepdims=True)
                e_v[2 * pair + head] = jnp.exp2(scores - peak).astype(bf16)
                sums.append(jnp.dot(e_v[2 * pair + head], v_one, preferred_element_type=f32))
            total = pltpu.roll(jnp.where(lane_q == 0, sums[1], sums[0]), 64, 1)
            inverse = 1.0 / total
            li_v[:, lanes] = inverse
            o_v[:, lanes] = (jnp.where(lane_q == 0, sums[0], sums[1]) * inverse).astype(bf16)
            return carry

        lax.fori_loop(0, PAIRS, pair_step, 0)
        put(e_v, "e")
        put(li_v, "linv")
        put(o_v, "o")
        get_wp.wait()
        middle = (
            x_v[...].astype(f32)
            + jnp.dot(o_v[...], wp_v[...], preferred_element_type=f32)
            + vec_part(vec_v, 3)
        )
        m_v[...] = middle
        normed, inverse = norm_parts(middle)
        n2_v[...] = normed.astype(bf16)
        r2_v[...] = jnp.broadcast_to(inverse, (ROWS, 128))
        c_v[...] = (normed * vec_part(vec_v, 4) + vec_part(vec_v, 5)).astype(bf16)
        put(n2_v, "n2")
        put(r2_v, "r2")
        put(c_v, "c")
        get_wu.wait()
        chunk = 1024

        def up_step(step, carry):
            lanes = pl.ds(pl.multiple_of(step * chunk, chunk), chunk)
            blanes = pl.ds(pl.multiple_of(step * chunk + VEC_AT[6], 128), chunk)
            pre = jnp.dot(c_v[...], wu_v[:, lanes], preferred_element_type=f32) + vec_v[:, blanes]
            value, slope = gelu_parts(pre)
            g_v[:, lanes] = value
            gp_v[:, lanes] = slope
            return carry

        lax.fori_loop(0, HIDDEN // chunk, up_step, 0)
        put(g_v, "g")
        put(gp_v, "gp")
        get_wd.wait()
        out = m_v[...] + jnp.dot(g_v[...], wd_v[...], preferred_element_type=f32) + vec_part(vec_v, 7)
        out_v[...] = out.astype(bf16)
        put_out = copies.start(out_v, out_ref)
        for copy in puts:
            copy.wait()
        put_out.wait()


ANY = pl.BlockSpec(memory_space=pl.ANY)
VMEM_LIMIT = 60 * 2**20


def vmem(*shape, dtype=bf16):
    return pltpu.VMEM(shape, dtype)


def front_call(scal, x, common, weights, states):
    vec, geo, cosine, sine = common
    wqkv, wp, wu, wd = weights
    first = states is None
    state_out = [jax.ShapeDtypeStruct((MICRO,) + shape, dtype) for _, shape, dtype in STATE_SHAPES]
    operands = [scal, x, vec, geo, cosine, sine, wqkv, wp, wu, wd] + ([] if first else list(states))
    scratch = [
        vmem(ROWS, WIDTH), vmem(1, VEC_AT[-1], dtype=f32), vmem(KEYS, 128, dtype=f32),
        vmem(ROWS, WIDTH, dtype=f32), vmem(ROWS, WIDTH, dtype=f32),
        vmem(WIDTH, 3 * WIDTH), vmem(WIDTH, WIDTH), vmem(WIDTH, HIDDEN), vmem(HIDDEN, WIDTH),
        vmem(ROWS, WIDTH), vmem(KEYS, 3 * WIDTH), vmem(HEADS, ROWS, KEYS), vmem(2, ROWS, KEYS, dtype=f32),
        vmem(ROWS, WIDTH, dtype=f32), vmem(ROWS, WIDTH), vmem(ROWS, WIDTH, dtype=f32),
        vmem(ROWS, WIDTH), vmem(ROWS, 128, dtype=f32), vmem(ROWS, WIDTH),
        vmem(ROWS, HIDDEN), vmem(ROWS, HIDDEN), vmem(ROWS, 128), vmem(KEYS, 128), vmem(ROWS, WIDTH),
        pltpu.SemaphoreType.DMA((24,)),
    ]
    results = pl.pallas_call(
        partial(front_kernel, first),
        out_shape=[jax.ShapeDtypeStruct((ROWS, WIDTH), bf16)] + state_out,
        in_specs=[pl.BlockSpec(memory_space=pltpu.SMEM)] + [ANY] * (len(operands) - 1),
        out_specs=[ANY] * (1 + len(STATES)),
        scratch_shapes=scratch,
        input_output_aliases={} if first else {10 + i: 1 + i for i in range(len(STATES))},
        compiler_params=pltpu.CompilerParams(vmem_limit_bytes=VMEM_LIMIT),
        name="layer_front",
    )(*operands)
    return results[0], tuple(results[1:])


BACK_SHAPES = (
    ("du", (ROWS, HIDDEN), bf16),
    ("dz", (ROWS, WIDTH), bf16),
    ("dy", (ROWS, WIDTH), bf16),
    ("small_two", (8, WIDTH), f32),
)
BACKS = tuple(name for name, _, _ in BACK_SHAPES)


def branch_kernel(first, scal, dy_in, vec_in, wd_in, wu_in, wp_in, gp_in, n2_in, r2_in, linv_in, *rest):
    if not first:
        rest = rest[len(BACKS) :]
    dm_ref, dop_ref = rest[:2]
    state = dict(zip(BACKS, rest[2 : 2 + len(BACKS)]))
    (
        dy_v, vec_v, wd_v, wu_v, wp_v, gp_v, n2_v, r2_v, li_v, du_v, dz_v, dm_v, dop_v, small_v, sems,
    ) = rest[2 + len(BACKS) :]

    @pl.when(scal[0] == 1)
    def _():
        slot = scal[1]
        copies = Copies(sems)
        get_dy = copies.start(dy_in, dy_v)
        get_wd = copies.start(wd_in, wd_v)
        get_gp = copies.start(gp_in.at[slot], gp_v)
        get_wu = copies.start(wu_in, wu_v)
        get_wp = copies.start(wp_in, wp_v)
        later = [
            copies.start(vec_in, vec_v),
            copies.start(n2_in.at[slot], n2_v),
            copies.start(r2_in.at[slot], r2_v),
            copies.start(linv_in.at[slot], li_v),
        ]
        puts = []

        def put(source, name):
            puts.append(copies.start(source, state[name].at[slot]))

        get_dy.wait()
        put(dy_v, "dy")
        get_wd.wait()
        get_gp.wait()
        chunk = 1024

        def act_step(step, carry):
            part = pl.ds(pl.multiple_of(step * chunk, chunk), chunk)
            act = lax.dot_general(dy_v[...], wd_v[part, :], NT, preferred_element_type=f32)
            du_v[:, part] = act.astype(bf16) * gp_v[:, part]
            return carry

        lax.fori_loop(0, HIDDEN // chunk, act_step, 0)
        put(du_v, "du")
        get_wu.wait()
        dc = lax.dot_general(du_v[...], wu_v[...], NT, preferred_element_type=f32)
        for copy in later:
            copy.wait()
        normed = n2_v[...].astype(f32)
        small_v[0:1, :] = jnp.sum(dc * normed, axis=0, keepdims=True)
        small_v[1:2, :] = jnp.sum(dc, axis=0, keepdims=True)
        put(small_v, "small_two")
        hat = dc * vec_part(vec_v, 4)
        dm = dy_v[...].astype(f32) + r2_v[:, 0:1] * (
            hat
            - jnp.mean(hat, axis=-1, keepdims=True)
            - normed * jnp.mean(hat * normed, axis=-1, keepdims=True)
        )
        dm_v[...] = dm
        dz_v[...] = dm.astype(bf16)
        put(dz_v, "dz")
        put_dm = copies.start(dm_v, dm_ref)
        get_wp.wait()
        do = lax.dot_general(dz_v[...], wp_v[...], NT, preferred_element_type=f32)
        dop_v[...] = (do * li_v[...]).astype(bf16)
        put_do = copies.start(dop_v, dop_ref)
        for copy in puts + [put_dm, put_do]:
            copy.wait()


def branch_call(scal, dy, vec, weights, fronts, backs):
    wqkv, wp, wu, wd = weights
    first = backs is None
    back_out = [jax.ShapeDtypeStruct((MICRO,) + shape, dtype) for _, shape, dtype in BACK_SHAPES]
    operands = [scal, dy, vec, wd, wu, wp, fronts["gp"], fronts["n2"], fronts["r2"], fronts["linv"]]
    count = len(operands)
    operands += [] if first else list(backs)
    scratch = [
        vmem(ROWS, WIDTH), vmem(1, VEC_AT[-1], dtype=f32), vmem(HIDDEN, WIDTH), vmem(WIDTH, HIDDEN), vmem(WIDTH, WIDTH),
        vmem(ROWS, HIDDEN), vmem(ROWS, WIDTH), vmem(ROWS, 128, dtype=f32), vmem(ROWS, WIDTH, dtype=f32),
        vmem(ROWS, HIDDEN), vmem(ROWS, WIDTH), vmem(ROWS, WIDTH, dtype=f32), vmem(ROWS, WIDTH), vmem(8, WIDTH, dtype=f32),
        pltpu.SemaphoreType.DMA((16,)),
    ]
    results = pl.pallas_call(
        partial(branch_kernel, first),
        out_shape=[jax.ShapeDtypeStruct((ROWS, WIDTH), f32), jax.ShapeDtypeStruct((ROWS, WIDTH), bf16)] + back_out,
        in_specs=[pl.BlockSpec(memory_space=pltpu.SMEM)] + [ANY] * (len(operands) - 1),
        out_specs=[ANY] * (2 + len(BACKS)),
        scratch_shapes=scratch,
        input_output_aliases={} if first else {count + i: 2 + i for i in range(len(BACKS))},
        compiler_params=pltpu.CompilerParams(vmem_limit_bytes=VMEM_LIMIT),
        name="branch_back",
    )(*operands)
    return results[0], results[1], tuple(results[2:])


LAST_SHAPES = (
    ("dqkv", (ROWS, 3 * WIDTH), bf16),
    ("small_one", (8, WIDTH), f32),
)
LASTS = tuple(name for name, _, _ in LAST_SHAPES)


def attention_kernel(
    first, scal, dm_in, dop_in, vec_in, geo_in, cos_in, sin_in, wqkv_in, qkv_in, e_in, o_in, x_in, *rest
):
    if not first:
        rest = rest[len(LASTS) :]
    dx_ref = rest[0]
    state = dict(zip(LASTS, rest[1 : 1 + len(LASTS)]))
    (
        dm_v, dop_v, vec_v, geo_v, cos_v, sin_v, wqkv_v, qkv_v, e_v, o_v, x_v,
        qt_v, dot_v, dq_v, dkt_v, dvt_v, dqkv_v, small_v, dx_v, sems,
    ) = rest[1 + len(LASTS) :]

    @pl.when(scal[0] == 1)
    def _():
        slot = scal[1]
        copies = Copies(sems)
        get_dop = copies.start(dop_in, dop_v)
        get_qkv = copies.start(qkv_in.at[slot], qkv_v.at[pl.ds(0, ROWS)])
        get_o = copies.start(o_in.at[slot], o_v)
        get_e = copies.start(e_in.at[slot], e_v)
        get_x = copies.start(x_in.at[slot], x_v)
        later = [
            copies.start(cos_in.at[slot], cos_v),
            copies.start(sin_in.at[slot], sin_v),
            copies.start(geo_in.at[slot], geo_v),
            copies.start(vec_in, vec_v),
            copies.start(dm_in, dm_v),
        ]
        get_w = copies.start(wqkv_in, wqkv_v)
        puts = []

        def put(source, name):
            puts.append(copies.start(source, state[name].at[slot]))

        qkv_v[ROWS:KEYS, :] = jnp.zeros((KEYS - ROWS, 3 * WIDTH), bf16)
        get_dop.wait()
        dot_v[...] = dop_v[...].T
        get_qkv.wait()
        qt_v[...] = qkv_v[:ROWS, :WIDTH].T
        get_o.wait()
        get_e.wait()

        def pair_step(pair, carry):
            lanes = pl.ds(pl.multiple_of(pair * 128, 128), 128)
            klanes = pl.ds(pl.multiple_of(pair * 128 + WIDTH, 128), 128)
            vlanes = pl.ds(pl.multiple_of(pair * 128 + 2 * WIDTH, 128), 128)
            do_two = dop_v[:, lanes]
            k_two = qkv_v[:, klanes]
            v_two = qkv_v[:, vlanes]
            prod = do_two.astype(f32) * o_v[:, lanes].astype(f32)
            lane = lax.broadcasted_iota(jnp.int32, (ROWS, 128), 1) // 64
            dqs = []
            for head in range(2):
                rows = pl.ds(pl.multiple_of(pair * 128 + head * 64, 64), 64)
                do_one = jnp.where(lane == head, do_two, bf16(0.0))
                dp = lax.dot_general(do_one, v_two, NT, preferred_element_type=f32)
                delta = jnp.sum(jnp.where(lane == head, prod, 0.0), axis=1, keepdims=True)
                probs = e_v[2 * pair + head]
                ds = probs * (dp - delta).astype(bf16)
                dqs.append(jnp.dot(ds, k_two, preferred_element_type=f32))
                dkt_v[rows, :] = jnp.dot(qt_v[rows, :], ds, preferred_element_type=f32)
                dvt_v[rows, :] = jnp.dot(dot_v[rows, :], probs, preferred_element_type=f32).astype(bf16)
            dq_v[:, lanes] = jnp.where(lane == 0, dqs[0], dqs[1])
            return carry

        lax.fori_loop(0, PAIRS, pair_step, 0)
        for copy in later:
            copy.wait()
        dqkv_v[:, 2 * WIDTH :] = dvt_v[...].T[:ROWS]
        dk = dkt_v[...].T[:ROWS]
        dq = dq_v[...]
        turn = dq * swap_halves(qkv_v[:ROWS, :WIDTH].astype(f32)) + dk * swap_halves(
            qkv_v[:ROWS, WIDTH : 2 * WIDTH].astype(f32)
        )
        small_v[2:3, :] = LN2 * jnp.sum(turn * geo_v[:ROWS, 0:1], axis=0, keepdims=True)
        small_v[3:4, :] = LN2 * jnp.sum(turn * geo_v[:ROWS, 1:2], axis=0, keepdims=True)
        dqkv_v[:, :WIDTH] = (0.125 * (dq * cos_v[...] - swap_halves(dq) * sin_v[...])).astype(bf16)
        dqkv_v[:, WIDTH : 2 * WIDTH] = (LN2 * (dk * cos_v[...] - swap_halves(dk) * sin_v[...])).astype(bf16)
        put(dqkv_v, "dqkv")
        get_x.wait()
        normed, inverse = norm_parts(x_v[...].astype(f32))
        get_w.wait()
        da = lax.dot_general(dqkv_v[...], wqkv_v[...], NT, preferred_element_type=f32)
        small_v[0:1, :] = jnp.sum(da * normed, axis=0, keepdims=True)
        small_v[1:2, :] = jnp.sum(da, axis=0, keepdims=True)
        put(small_v, "small_one")
        hat = da * vec_part(vec_v, 0)
        dx = dm_v[...] + inverse * (
            hat
            - jnp.mean(hat, axis=-1, keepdims=True)
            - normed * jnp.mean(hat * normed, axis=-1, keepdims=True)
        )
        dx_v[...] = dx.astype(bf16)
        put_dx = copies.start(dx_v, dx_ref)
        for copy in puts + [put_dx]:
            copy.wait()


def attention_call(scal, dm, dop, common, weights, fronts, lasts):
    vec, geo, cosine, sine = common
    first = lasts is None
    last_out = [jax.ShapeDtypeStruct((MICRO,) + shape, dtype) for _, shape, dtype in LAST_SHAPES]
    operands = [
        scal, dm, dop, vec, geo, cosine, sine, weights[0],
        fronts["qkv"], fronts["e"], fronts["o"], fronts["x"],
    ]
    count = len(operands)
    operands += [] if first else list(lasts)
    scratch = [
        vmem(ROWS, WIDTH, dtype=f32), vmem(ROWS, WIDTH), vmem(1, VEC_AT[-1], dtype=f32), vmem(KEYS, 128, dtype=f32),
        vmem(ROWS, WIDTH, dtype=f32), vmem(ROWS, WIDTH, dtype=f32), vmem(WIDTH, 3 * WIDTH),
        vmem(KEYS, 3 * WIDTH), vmem(HEADS, ROWS, KEYS), vmem(ROWS, WIDTH), vmem(ROWS, WIDTH),
        vmem(WIDTH, ROWS), vmem(WIDTH, ROWS), vmem(ROWS, WIDTH, dtype=f32),
        vmem(WIDTH, KEYS, dtype=f32), vmem(WIDTH, KEYS), vmem(ROWS, 3 * WIDTH), vmem(8, WIDTH, dtype=f32), vmem(ROWS, WIDTH),
        pltpu.SemaphoreType.DMA((16,)),
    ]
    results = pl.pallas_call(
        partial(attention_kernel, first),
        out_shape=[jax.ShapeDtypeStruct((ROWS, WIDTH), bf16)] + last_out,
        in_specs=[pl.BlockSpec(memory_space=pltpu.SMEM)] + [ANY] * (len(operands) - 1),
        out_specs=[ANY] * (1 + len(LASTS)),
        scratch_shapes=scratch,
        input_output_aliases={} if first else {count + i: 1 + i for i in range(len(LASTS))},
        compiler_params=pltpu.CompilerParams(vmem_limit_bytes=VMEM_LIMIT),
        name="attention_back",
    )(*operands)
    return results[0], tuple(results[1:])


def geometry(kind_list):
    row_index = jnp.arange(KEYS, dtype=jnp.int32)[None, :]
    kind_col = kind_list[:, None]
    side_cells = jnp.where(
        kind_col == 0, SIDE_LARGE, jnp.where(kind_col == 1, SIDE_MID, SIDE_SMALL)
    ).astype(jnp.int32)
    image_count = jnp.where(kind_col == 2, 2, 1).astype(jnp.int32)
    image_area = side_cells * side_cells
    image_index = row_index // image_area
    live_rows = (image_index < image_count) & (row_index < ROWS)
    local_index = row_index - image_index * image_area
    patch_row = local_index // side_cells
    patch_col = local_index - patch_row * side_cells
    segment = jnp.where(live_rows, image_index, jnp.where(row_index < ROWS, 3, 2)).astype(f32)
    patch_row = jnp.where(live_rows, patch_row, 0).astype(f32)
    patch_col = jnp.where(live_rows, patch_col, 0).astype(f32)
    return patch_row, patch_col, segment, live_rows.astype(f32)


def tables(kinds, frequency):
    patch_row, patch_col, segment, live = geometry(kinds)
    lane = jnp.arange(128)[None, None, :]
    geo = jnp.where(
        lane == 0, patch_row[..., None], jnp.where(lane == 1, patch_col[..., None], segment[..., None])
    )
    half = WIDTH // 2
    spread = lambda row: jnp.broadcast_to(row.reshape(HEADS, 1, 32), (HEADS, 2, 32)).reshape(1, 1, WIDTH)
    angles = patch_row[:, :ROWS, None] * spread(frequency[:half]) + patch_col[:, :ROWS, None] * spread(frequency[half:])
    sign = jnp.where((jnp.arange(WIDTH) % 64) < 32, -1.0, 1.0)[None, None, :]
    return geo, jnp.cos(angles), jnp.sin(angles) * sign, live[:, :ROWS]


def send(value, source, target):
    return lax.ppermute(value, "section", [(source, target)])


def gathered(part, target, sections):
    section = lax.axis_index("section")
    pieces = []
    for source in range(sections):
        pieces.append(part if source == target else send(part, source, target))
    return jnp.concatenate(pieces, axis=0)


def handed_out(whole, source, sections):
    section = lax.axis_index("section")
    share = whole.shape[0] // sections
    result = whole[source * share : (source + 1) * share]
    for target in range(sections):
        if target != source:
            piece = send(whole[target * share : (target + 1) * share], source, target)
            result = jnp.where(section == target, piece, result)
    return result


def rows_product(left, right):
    left = left.reshape(-1, left.shape[-1])
    right = right.reshape(-1, right.shape[-1])
    return jnp.einsum("rd,re->de", left, right, preferred_element_type=f32).astype(bf16)


def column_sum(values):
    return jnp.sum(values.reshape(-1, values.shape[-1]).astype(f32), axis=0)


def summed_over_images(part):
    own = lax.psum_scatter(part, "dp", scatter_dimension=0, tiled=True)
    return lax.all_gather(own, "dp", axis=0, tiled=True)


SMALL_ROWS = 128


def per_device(
    tokens,
    cotangent,
    image_kind,
    norm_one_gain,
    norm_one_bias,
    qkv_weight,
    qkv_bias,
    rotary_freq,
    proj_weight,
    proj_bias,
    norm_two_gain,
    norm_two_bias,
    up_weight,
    up_bias,
    down_weight,
    down_bias,
):
    sections = lax.axis_size("section")
    section = lax.axis_index("section")
    last = sections - 1
    geo, cosine, sine, live = tables(image_kind, rotary_freq[0])
    vec = jnp.concatenate(
        [
            norm_one_gain[0], norm_one_bias[0], qkv_bias[0], proj_bias[0],
            norm_two_gain[0], norm_two_bias[0], up_bias[0], down_bias[0],
        ]
    )[None]
    common = (vec, geo, cosine, sine)
    weights = (qkv_weight[0], proj_weight[0], up_weight[0], down_weight[0])
    first_in = gathered(tokens, 0, sections)
    last_in = gathered(cotangent, last, sections)
    live_rows = live.reshape(-1, 1)
    last_in = jnp.where(live_rows > 0, last_in, bf16(0.0))

    def scalars(layer, micro):
        return jnp.stack([(section == layer).astype(jnp.int32), jnp.int32(micro)])

    states = None
    values = [first_in[m * ROWS : (m + 1) * ROWS] for m in range(MICRO)]
    for layer in range(sections):
        for micro in range(MICRO):
            out, states = front_call(scalars(layer, micro), values[micro], common, weights, states)
            values[micro] = send(out, layer, layer + 1) if layer < last else out
    final = jnp.where(live_rows > 0, jnp.concatenate(values, axis=0), bf16(0.0))
    block_out = handed_out(final, last, sections)
    fronts = dict(zip(STATES, states))
    backs = lasts = None
    grads = [last_in[m * ROWS : (m + 1) * ROWS] for m in range(MICRO)]
    for layer in reversed(range(sections)):
        for micro in range(MICRO):
            scal = scalars(layer, micro)
            dm, dop, backs = branch_call(scal, grads[micro], vec, weights, fronts, backs)
            dx, lasts = attention_call(scal, dm, dop, common, weights, fronts, lasts)
            grads[micro] = send(dx, layer, layer - 1) if layer > 0 else dx
    grad_tokens = handed_out(jnp.concatenate(grads, axis=0), 0, sections)
    backs = dict(zip(BACKS, backs))
    lasts = dict(zip(LASTS, lasts))
    grad_down = rows_product(fronts["g"], backs["dy"])
    grad_up = rows_product(fronts["c"], backs["du"])
    grad_proj = rows_product(fronts["o"], backs["dz"])
    grad_qkv = rows_product(fronts["a"], lasts["dqkv"])
    one = jnp.sum(lasts["small_one"], axis=0)
    two = jnp.sum(backs["small_two"], axis=0)
    turns = one[2:4].reshape(2, HEADS, 2, 32)
    small = jnp.concatenate(
        [
            one[0], one[1], column_sum(lasts["dqkv"]), (turns[:, :, 1] - turns[:, :, 0]).reshape(-1),
            column_sum(backs["dz"]), two[0], two[1], column_sum(backs["du"]), column_sum(backs["dy"]),
        ]
    )
    small = jnp.pad(small.astype(bf16).reshape(-1, WIDTH), ((0, SMALL_ROWS - small.shape[0] // WIDTH), (0, 0)))
    grad_down = summed_over_images(grad_down).astype(f32)
    grad_up = summed_over_images(grad_up).astype(f32)
    grad_proj = summed_over_images(jnp.concatenate([grad_proj, small], axis=0)).astype(f32)
    grad_qkv = summed_over_images(grad_qkv).astype(f32)
    small = grad_proj[WIDTH:].reshape(-1)
    sizes = (WIDTH, WIDTH, 3 * WIDTH, WIDTH, WIDTH, WIDTH, WIDTH, HIDDEN, WIDTH)
    ends = np.cumsum((0,) + sizes)
    g_one, b_one, b_qkv, freq, b_proj, g_two, b_two, b_up, b_down = (
        small[int(ends[i]) : int(ends[i + 1])][None] for i in range(len(sizes))
    )
    return (
        block_out, grad_tokens.astype(f32), g_one, b_one, grad_qkv[None], b_qkv, freq,
        grad_proj[:WIDTH][None], b_proj, g_two, b_two, grad_up[None], b_up, grad_down[None], b_down,
    )


def solution(mesh):
    row = P(("dp", "section"), None)
    vector = P("section", None)
    matrix = P("section", None, None)
    params = (
        vector, vector, matrix, vector, vector, matrix, vector, vector, vector, matrix, vector, matrix, vector,
    )
    return jax.shard_map(
        per_device,
        mesh=mesh,
        in_specs=(row, row, P("dp")) + params,
        out_specs=(row, row) + params,
        check_vma=False,
    )
```

```python
from functools import partial
import math

import jax
import jax.numpy as jnp
import numpy as np
from jax import lax
from jax.experimental import pallas as pl
from jax.experimental.pallas import tpu as pltpu
from jax.sharding import PartitionSpec as P

HEADS = 12
SIDE_LARGE = 20
SIDE_MID = 16
SIDE_SMALL = 14
MICRO = 2
ROWS = 400
KEYS = 512
WIDTH = 768
HIDDEN = 3072
PAIRS = HEADS // 2
EPSILON = 1e-06
MASKED = -1e30
LOG2E = math.log2(math.e)
LN2 = math.log(2.0)
GELU_ONE = math.sqrt(2.0 / math.pi)
GELU_TWO = GELU_ONE * 0.044715

f32 = jnp.float32
bf16 = jnp.bfloat16
NT = (((1,), (1,)), ((), ()))
TN = (((0,), (0,)), ((), ()))

VEC_SIZES = (WIDTH, WIDTH, 3 * WIDTH, WIDTH, WIDTH, WIDTH, HIDDEN, WIDTH)
VEC_AT = tuple(int(v) for v in np.cumsum((0,) + VEC_SIZES))


def vec_part(vec_ref, index):
    return vec_ref[:, VEC_AT[index] : VEC_AT[index + 1]]


def swap_halves(values):
    lane = lax.broadcasted_iota(jnp.int32, values.shape, 1) % 64
    width = values.shape[1]
    return jnp.where(lane < 32, pltpu.roll(values, width - 32, 1), pltpu.roll(values, 32, 1))


def norm_parts(values):
    center = values - jnp.mean(values, axis=-1, keepdims=True)
    inverse = lax.rsqrt(jnp.mean(center * center, axis=-1, keepdims=True) + EPSILON)
    return center * inverse, inverse


def gelu_parts(pre):
    low = pre.astype(bf16)
    square = low * low
    tanh = jnp.tanh(low * (bf16(GELU_ONE) + bf16(GELU_TWO) * square))
    half = bf16(0.5) + bf16(0.5) * tanh
    value = low * half
    slope = half + (value - value * half) * (bf16(2 * GELU_ONE) + bf16(6 * GELU_TWO) * square)
    return value, slope


class Copies:
    def __init__(self, sems):
        self.sems = sems
        self.open = []
        self.used = 0

    def start(self, source, target):
        copy = pltpu.make_async_copy(source, target, self.sems.at[self.used])
        self.used += 1
        copy.start()
        self.open.append(copy)
        return copy

    def wait(self, *copies):
        for copy in copies:
            self.open = [other for other in self.open if other is not copy]
            copy.wait()

    def finish(self):
        self.wait(*list(self.open))


STATE_SHAPES = (
    ("x", (ROWS, WIDTH), bf16),
    ("a", (ROWS, WIDTH), bf16),
    ("qkv", (ROWS, 3 * WIDTH), bf16),
    ("e", (HEADS, ROWS, KEYS), bf16),
    ("linv", (ROWS, WIDTH), f32),
    ("o", (ROWS, WIDTH), bf16),
    ("n2", (ROWS, WIDTH), bf16),
    ("r2", (ROWS, 128), f32),
    ("c", (ROWS, WIDTH), bf16),
    ("g", (ROWS, HIDDEN), bf16),
    ("gp", (ROWS, HIDDEN), bf16),
)
STATES = tuple(name for name, _, _ in STATE_SHAPES)


def front_kernel(first, scal, layer, *refs):
    x_in, geo_in, cos_in, sin_in, wqkv_in, wp_in, wu_in, wd_in = refs[:8]
    vec_in, rest = refs[8:16], refs[16:]
    if not first:
        rest = rest[len(STATES) :]
    out_ref = rest[0]
    state = dict(zip(STATES, rest[1 : 1 + len(STATES)]))
    (
        x_v, vec_v, geo_v, cos_v, sin_v, wqkv_v, wp_v, wu_v, wd_v,
        a_v, qkv_v, e_v, s_v, li_v, o_v, m_v, n2_v, r2_v, c_v, g_v, gp_v, qcode_v, kcode_v, out_v, sems,
    ) = rest[1 + len(STATES) :]

    @pl.when(scal[0] == layer[0])
    def _():
        slot = layer[1]
        copies = Copies(sems)
        wait = copies.wait
        get_x = copies.start(x_in, x_v)
        get_vec = [
            copies.start(part, vec_v.at[:, pl.ds(at, size)]) for part, at, size in zip(vec_in, VEC_AT, VEC_SIZES)
        ]
        get_geo = copies.start(geo_in.at[slot], geo_v)
        get_qkv = [
            copies.start(wqkv_in.at[:, pl.ds(at, WIDTH)], wqkv_v.at[:, pl.ds(at, WIDTH)])
            for at in range(0, 3 * WIDTH, WIDTH)
        ]
        get_cos = copies.start(cos_in.at[slot], cos_v)
        get_sin = copies.start(sin_in.at[slot], sin_v)

        def put(source, name):
            copies.start(source, state[name].at[slot])

        qkv_v[ROWS:KEYS, :] = jnp.zeros((KEYS - ROWS, 3 * WIDTH), bf16)
        wait(get_x, get_geo, *get_vec)
        normed, _ = norm_parts(x_v[...].astype(f32))
        a_v[...] = (normed * vec_part(vec_v, 0) + vec_part(vec_v, 1)).astype(bf16)
        segment = geo_v[:, 2:3]
        code = (lax.broadcasted_iota(jnp.int32, (KEYS, 128), 1) % 64).astype(f32)
        qcode_v[...] = jnp.where(segment[:ROWS] == code[:ROWS], 1.0, 0.0).astype(bf16)
        kcode_v[...] = jnp.where((segment != code) & (code < 4), MASKED, 0.0).astype(bf16)
        for part in range(3):
            at = part * WIDTH
            wait(get_qkv[part])
            if part == 0:
                wait(get_cos, get_sin)
                get_wp = copies.start(wp_in, wp_v)
                get_wu = copies.start(wu_in, wu_v)
                get_wd = copies.start(wd_in, wd_v)
            acc = jnp.dot(a_v[...], wqkv_v[:, at : at + WIDTH], preferred_element_type=f32)
            acc = acc + vec_v[:, VEC_AT[2] + at : VEC_AT[2] + at + WIDTH]
            if part < 2:
                acc = acc * cos_v[...] + swap_halves(acc) * sin_v[...]
            if part == 0:
                acc = acc * (LOG2E / 8.0)
            qkv_v[:ROWS, at : at + WIDTH] = acc.astype(bf16)

        for pair in range(PAIRS):
            lanes = pl.ds(pair * 128, 128)
            klanes = pl.ds(pair * 128 + WIDTH, 128)
            vlanes = pl.ds(pair * 128 + 2 * WIDTH, 128)
            q_two = qkv_v[:ROWS, lanes]
            k_two = qkv_v[:, klanes]
            v_two = qkv_v[:, vlanes]
            lane_q = lax.broadcasted_iota(jnp.int32, (ROWS, 128), 1) // 64
            lane_k = lax.broadcasted_iota(jnp.int32, (KEYS, 128), 1) // 64
            for head in range(2):
                q_one = jnp.where(lane_q == head, q_two, qcode_v[...])
                k_one = jnp.where(lane_k == head, k_two, kcode_v[...])
                s_v[2 * (pair % 2) + head] = lax.dot_general(q_one, k_one, NT, preferred_element_type=f32)
            sums = []
            for head in range(2):
                v_one = jnp.where(lane_k == head, v_two, bf16(1.0))
                scores = s_v[2 * (pair % 2) + head]
                peak = jnp.max(scores, axis=1, keepdims=True)
                e_v[2 * pair + head] = jnp.exp2(scores - peak).astype(bf16)
                sums.append(jnp.dot(e_v[2 * pair + head], v_one, preferred_element_type=f32))
            total = pltpu.roll(jnp.where(lane_q == 0, sums[1], sums[0]), 64, 1)
            inverse = 1.0 / total
            li_v[:, lanes] = inverse
            o_v[:, lanes] = (jnp.where(lane_q == 0, sums[0], sums[1]) * inverse).astype(bf16)
        put(x_v, "x")
        put(a_v, "a")
        put(qkv_v.at[pl.ds(0, ROWS)], "qkv")
        put(e_v, "e")
        put(li_v, "linv")
        put(o_v, "o")
        wait(get_wp)
        middle = (
            x_v[...].astype(f32)
            + jnp.dot(o_v[...], wp_v[...], preferred_element_type=f32)
            + vec_part(vec_v, 3)
        )
        m_v[...] = middle
        normed, inverse = norm_parts(middle)
        n2_v[...] = normed.astype(bf16)
        r2_v[...] = jnp.broadcast_to(inverse, (ROWS, 128))
        c_v[...] = (normed * vec_part(vec_v, 4) + vec_part(vec_v, 5)).astype(bf16)
        put(n2_v, "n2")
        put(r2_v, "r2")
        put(c_v, "c")
        wait(get_wu)
        chunk = 1024

        def up_step(step, carry):
            lanes = pl.ds(pl.multiple_of(step * chunk, chunk), chunk)
            blanes = pl.ds(pl.multiple_of(step * chunk + VEC_AT[6], 128), chunk)
            pre = jnp.dot(c_v[...], wu_v[:, lanes], preferred_element_type=f32) + vec_v[:, blanes]
            value, slope = gelu_parts(pre)
            g_v[:, lanes] = value
            gp_v[:, lanes] = slope
            return carry

        lax.fori_loop(0, HIDDEN // chunk, up_step, 0)
        put(gp_v, "gp")
        put(g_v, "g")
        wait(get_wd)
        for at in range(0, WIDTH, 256):
            part = pl.ds(at, 256)
            out = jnp.dot(g_v[...], wd_v[:, part], preferred_element_type=f32)
            out = out + m_v[:, part] + vec_v[:, VEC_AT[7] + at : VEC_AT[7] + at + 256]
            out_v[:, part] = out.astype(bf16)
            copies.start(out_v.at[:, part], out_ref.at[:, part])
        copies.finish()


ANY = pl.BlockSpec(memory_space=pl.ANY)
VMEM_LIMIT = 60 * 2**20


def vmem(*shape, dtype=bf16):
    return pltpu.VMEM(shape, dtype)


def call_states(kernel, first, operands, smem, states, plain_out, shapes, scratch, name):
    count = len(operands)
    state_out = [jax.ShapeDtypeStruct((MICRO,) + shape, dtype) for _, shape, dtype in shapes]
    operands = list(operands) + ([] if first else list(states))
    results = pl.pallas_call(
        partial(kernel, first),
        out_shape=list(plain_out) + state_out,
        in_specs=[pl.BlockSpec(memory_space=pltpu.SMEM)] * smem + [ANY] * (len(operands) - smem),
        out_specs=[ANY] * (len(plain_out) + len(shapes)),
        scratch_shapes=scratch,
        input_output_aliases={} if first else {count + i: len(plain_out) + i for i in range(len(shapes))},
        compiler_params=pltpu.CompilerParams(vmem_limit_bytes=VMEM_LIMIT),
        name=name,
    )(*operands)
    return results[0], tuple(results[1:])


def front_call(scal, layer, x, common, weights, vecs, states):
    scratch = [
        vmem(ROWS, WIDTH), vmem(1, VEC_AT[-1], dtype=f32), vmem(KEYS, 128, dtype=f32),
        vmem(ROWS, WIDTH, dtype=f32), vmem(ROWS, WIDTH, dtype=f32),
        vmem(WIDTH, 3 * WIDTH), vmem(WIDTH, WIDTH), vmem(WIDTH, HIDDEN), vmem(HIDDEN, WIDTH),
        vmem(ROWS, WIDTH), vmem(KEYS, 3 * WIDTH), vmem(HEADS, ROWS, KEYS), vmem(4, ROWS, KEYS, dtype=f32),
        vmem(ROWS, WIDTH, dtype=f32), vmem(ROWS, WIDTH), vmem(ROWS, WIDTH, dtype=f32),
        vmem(ROWS, WIDTH), vmem(ROWS, 128, dtype=f32), vmem(ROWS, WIDTH),
        vmem(ROWS, HIDDEN), vmem(ROWS, HIDDEN), vmem(ROWS, 128), vmem(KEYS, 128), vmem(ROWS, WIDTH),
        pltpu.SemaphoreType.DMA((36,)),
    ]
    operands = [scal, layer, x, *common, *weights, *vecs]
    out = jax.ShapeDtypeStruct((ROWS, WIDTH), bf16)
    return call_states(front_kernel, states is None, operands, 2, states, [out], STATE_SHAPES, scratch, "layer_front")


BACK_SHAPES = (
    ("du", (ROWS, HIDDEN), bf16),
    ("dz", (ROWS, WIDTH), bf16),
    ("dqkv", (ROWS, 3 * WIDTH), bf16),
    ("small", (8, WIDTH), f32),
)
BACKS = tuple(name for name, _, _ in BACK_SHAPES)


def back_kernel(first, scal, layer, *refs):
    dy_in, geo_in, cos_in, sin_in, wqkv_in, wp_in, wu_in, wd_in, gain_one_in, gain_two_in = refs[:10]
    saved = dict(zip(KEPT, refs[10 : 10 + len(KEPT)]))
    rest = refs[10 + len(KEPT) :]
    if not first:
        rest = rest[len(BACKS) :]
    dx_ref = rest[0]
    state = dict(zip(BACKS, rest[1 : 1 + len(BACKS)]))
    (
        dy_v, geo_v, cos_v, sin_v, wqkv_v, wp_v, wu_v, wd_v, gains_v,
        gp_v, n2_v, r2_v, li_v, qkv_v, e_v, o_v, x_v,
        du_v, dz_v, dm_v, dop_v, qt_v, dot_v, dq_v, dkt_v, dvt_v, dqkv_v, small_v, dx_v, sems,
    ) = rest[1 + len(BACKS) :]

    @pl.when(scal[0] == layer[0])
    def _():
        slot = layer[1]
        copies = Copies(sems)
        wait = copies.wait
        chunk = 1024
        steps = HIDDEN // chunk
        get_dy = copies.start(dy_in, dy_v)
        get_wd, get_gp = [], []
        for step in range(steps):
            part = pl.ds(step * chunk, chunk)
            get_wd.append(copies.start(wd_in.at[part], wd_v.at[part]))
            get_gp.append(copies.start(saved["gp"].at[slot, :, part], gp_v.at[:, part]))
        get_wu = copies.start(wu_in, wu_v)
        get_norm = [
            copies.start(saved["n2"].at[slot], n2_v),
            copies.start(saved["r2"].at[slot], r2_v),
            copies.start(gain_one_in, gains_v.at[pl.ds(0, 1)]),
            copies.start(gain_two_in, gains_v.at[pl.ds(8, 1)]),
        ]

        def put(source, name):
            copies.start(source, state[name].at[slot])

        qkv_v[ROWS:KEYS, :] = jnp.zeros((KEYS - ROWS, 3 * WIDTH), bf16)
        wait(get_dy)
        for step in range(steps):
            part = slice(step * chunk, (step + 1) * chunk)
            wait(get_wd[step], get_gp[step])
            act = lax.dot_general(dy_v[...], wd_v[part, :], NT, preferred_element_type=f32)
            du_v[:, part] = act.astype(bf16) * gp_v[:, part]
        get_wp = copies.start(wp_in, wp_v)
        get_li = copies.start(saved["linv"].at[slot], li_v)
        get_qkv = copies.start(saved["qkv"].at[slot], qkv_v.at[pl.ds(0, ROWS)])
        get_o = copies.start(saved["o"].at[slot], o_v)
        get_e = copies.start(saved["e"].at[slot], e_v)
        get_turn = [
            copies.start(cos_in.at[slot], cos_v),
            copies.start(sin_in.at[slot], sin_v),
            copies.start(geo_in.at[slot], geo_v),
        ]
        get_x = copies.start(saved["x"].at[slot], x_v)
        get_wqkv = copies.start(wqkv_in, wqkv_v)
        put(du_v, "du")
        wait(get_wu)
        dc = lax.dot_general(du_v[...], wu_v[...], NT, preferred_element_type=f32)
        wait(*get_norm)
        normed = n2_v[...].astype(f32)
        small_v[0:1, :] = jnp.sum(dc * normed, axis=0, keepdims=True)
        small_v[1:2, :] = jnp.sum(dc, axis=0, keepdims=True)
        hat = dc * gains_v[8:9, :]
        dm = dy_v[...].astype(f32) + r2_v[:, 0:1] * (
            hat
            - jnp.mean(hat, axis=-1, keepdims=True)
            - normed * jnp.mean(hat * normed, axis=-1, keepdims=True)
        )
        dm_v[...] = dm
        dz_v[...] = dm.astype(bf16)
        put(dz_v, "dz")
        wait(get_wp, get_li)
        do = lax.dot_general(dz_v[...], wp_v[...], NT, preferred_element_type=f32)
        dop_v[...] = (do * li_v[...]).astype(bf16)
        dot_v[...] = dop_v[...].T
        wait(get_qkv)
        qt_v[...] = qkv_v[:ROWS, :WIDTH].T
        wait(get_o, get_e)

        def pair_step(step, carry):
            for pair in [step * 2 + i for i in range(2)]:
                lanes = pl.ds(pl.multiple_of(pair * 128, 128), 128)
                klanes = pl.ds(pl.multiple_of(pair * 128 + WIDTH, 128), 128)
                vlanes = pl.ds(pl.multiple_of(pair * 128 + 2 * WIDTH, 128), 128)
                do_two = dop_v[:, lanes]
                k_two = qkv_v[:, klanes]
                v_two = qkv_v[:, vlanes]
                prod = do_two.astype(f32) * o_v[:, lanes].astype(f32)
                lane = lax.broadcasted_iota(jnp.int32, (ROWS, 128), 1) // 64
                dqs = []
                for head in range(2):
                    rows = pl.ds(pl.multiple_of(pair * 128 + head * 64, 64), 64)
                    do_one = jnp.where(lane == head, do_two, bf16(0.0))
                    dp = lax.dot_general(do_one, v_two, NT, preferred_element_type=f32)
                    delta = jnp.sum(jnp.where(lane == head, prod, 0.0), axis=1, keepdims=True)
                    probs = e_v[2 * pair + head]
                    ds = probs * (dp - delta).astype(bf16)
                    dqs.append(jnp.dot(ds, k_two, preferred_element_type=f32))
                    dkt_v[rows, :] = jnp.dot(qt_v[rows, :], ds, preferred_element_type=f32)
                    dvt_v[rows, :] = jnp.dot(dot_v[rows, :], probs, preferred_element_type=f32).astype(bf16)
                dq_v[:, lanes] = jnp.where(lane == 0, dqs[0], dqs[1])
            return carry

        lax.fori_loop(0, PAIRS // 2, pair_step, 0)
        wait(*get_turn)
        dqkv_v[:, 2 * WIDTH :] = dvt_v[...].T[:ROWS]
        dk = dkt_v[...].T[:ROWS]
        dq = dq_v[...]
        turn = dq * swap_halves(qkv_v[:ROWS, :WIDTH].astype(f32)) + dk * swap_halves(
            qkv_v[:ROWS, WIDTH : 2 * WIDTH].astype(f32)
        )
        small_v[4:5, :] = LN2 * jnp.sum(turn * geo_v[:ROWS, 0:1], axis=0, keepdims=True)
        small_v[5:6, :] = LN2 * jnp.sum(turn * geo_v[:ROWS, 1:2], axis=0, keepdims=True)
        dqkv_v[:, :WIDTH] = (0.125 * (dq * cos_v[...] - swap_halves(dq) * sin_v[...])).astype(bf16)
        dqkv_v[:, WIDTH : 2 * WIDTH] = (LN2 * (dk * cos_v[...] - swap_halves(dk) * sin_v[...])).astype(bf16)
        put(dqkv_v, "dqkv")
        wait(get_x)
        normed, inverse = norm_parts(x_v[...].astype(f32))
        wait(get_wqkv)
        da = lax.dot_general(dqkv_v[...], wqkv_v[...], NT, preferred_element_type=f32)
        small_v[2:3, :] = jnp.sum(da * normed, axis=0, keepdims=True)
        small_v[3:4, :] = jnp.sum(da, axis=0, keepdims=True)
        put(small_v, "small")
        hat = da * gains_v[0:1, :]
        dx = dm_v[...] + inverse * (
            hat
            - jnp.mean(hat, axis=-1, keepdims=True)
            - normed * jnp.mean(hat * normed, axis=-1, keepdims=True)
        )
        dx_v[...] = dx.astype(bf16)
        copies.start(dx_v, dx_ref)
        copies.finish()


KEPT = ("gp", "n2", "r2", "linv", "qkv", "e", "o", "x")


def back_call(scal, layer, dy, common, weights, vecs, fronts, backs):
    scratch = [
        vmem(ROWS, WIDTH), vmem(KEYS, 128, dtype=f32), vmem(ROWS, WIDTH, dtype=f32), vmem(ROWS, WIDTH, dtype=f32),
        vmem(WIDTH, 3 * WIDTH), vmem(WIDTH, WIDTH), vmem(WIDTH, HIDDEN), vmem(HIDDEN, WIDTH), vmem(16, WIDTH, dtype=f32),
        vmem(ROWS, HIDDEN), vmem(ROWS, WIDTH), vmem(ROWS, 128, dtype=f32), vmem(ROWS, WIDTH, dtype=f32),
        vmem(KEYS, 3 * WIDTH), vmem(HEADS, ROWS, KEYS), vmem(ROWS, WIDTH), vmem(ROWS, WIDTH),
        vmem(ROWS, HIDDEN), vmem(ROWS, WIDTH), vmem(ROWS, WIDTH, dtype=f32), vmem(ROWS, WIDTH),
        vmem(WIDTH, ROWS), vmem(WIDTH, ROWS), vmem(ROWS, WIDTH, dtype=f32),
        vmem(WIDTH, KEYS, dtype=f32), vmem(WIDTH, KEYS), vmem(ROWS, 3 * WIDTH), vmem(8, WIDTH, dtype=f32), vmem(ROWS, WIDTH),
        pltpu.SemaphoreType.DMA((36,)),
    ]
    operands = [scal, layer, dy, *common, *weights, vecs[0], vecs[4], *(fronts[name] for name in KEPT)]
    out = jax.ShapeDtypeStruct((ROWS, WIDTH), bf16)
    return call_states(back_kernel, backs is None, operands, 2, backs, [out], BACK_SHAPES, scratch, "layer_back")


def side_of(kind):
    return jnp.where(kind == 0, float(SIDE_LARGE), jnp.where(kind == 1, float(SIDE_MID), float(SIDE_SMALL)))


def places(kind, rows):
    side = side_of(kind)
    area = side * side
    images = jnp.where(kind == 2, 2.0, 1.0)
    image = (rows >= area).astype(f32) + (rows >= 2 * area).astype(f32)
    live = (image < images) & (rows < ROWS)
    local = rows - image * area
    patch_row = jnp.floor((local + 0.5) / side)
    patch_col = local - patch_row * side
    zero = jnp.zeros_like(rows)
    segment = jnp.where(live, image, jnp.where(rows < ROWS, 3.0, 2.0))
    return jnp.where(live, patch_row, zero), jnp.where(live, patch_col, zero), segment, live


def split_low(values):
    high = values.astype(bf16)
    return jnp.concatenate([high, (values - high.astype(f32)).astype(bf16)], axis=0)


def tables_kernel(first, turn_ref, kind_ref, freq_in, *refs):
    if not first:
        refs = refs[4:]
    geo_ref, cos_ref, sin_ref, freq_v, geo_v, cos_v, sin_v, sems = refs

    @pl.when(turn_ref[0] == 1)
    def _():
        micro = turn_ref[1]
        copies = Copies(sems)
        copies.wait(copies.start(freq_in, freq_v))
        step = lax.broadcasted_iota(jnp.int32, (32, WIDTH // 2), 0).astype(f32)
        angles = [step * freq_v[:, at : at + WIDTH // 2] for at in (0, WIDTH // 2)]
        waves = [split_low(jnp.concatenate([jnp.cos(angle), jnp.sin(angle)], axis=1)) for angle in angles]
        sixteen = lax.broadcasted_iota(jnp.int32, (ROWS, 64), 1) % 32
        rows = lax.broadcasted_iota(jnp.int32, (KEYS, 128), 0).astype(f32)
        lane = lax.broadcasted_iota(jnp.int32, (KEYS, 128), 1)
        patch_row, patch_col, segment, _ = places(kind_ref[micro], rows)
        geo_v[...] = jnp.where(lane == 0, patch_row, jnp.where(lane == 1, patch_col, segment))
        picks = [
            jnp.where(sixteen.astype(f32) == patch[:ROWS, :64], 1.0, 0.0).astype(bf16)
            for patch in (patch_row, patch_col)
        ]
        row_wave, col_wave = (
            jnp.dot(pick, wave, preferred_element_type=f32) for pick, wave in zip(picks, waves)
        )
        half = WIDTH // 2
        row_cos, row_sin = row_wave[:, :half], row_wave[:, half:]
        col_cos, col_sin = col_wave[:, :half], col_wave[:, half:]
        cosine = row_cos * col_cos - row_sin * col_sin
        sine = row_sin * col_cos + row_cos * col_sin
        lane = lax.broadcasted_iota(jnp.int32, (ROWS, 128), 1)
        for part in range(half // 128):
            for pair in range(2):
                at = (2 * part + pair) * 128
                cos_v[:, at : at + 128] = spread(cosine[:, part * 128 : part * 128 + 128], pair, lane)
                values = spread(sine[:, part * 128 : part * 128 + 128], pair, lane)
                sin_v[:, at : at + 128] = jnp.where(lane % 64 < 32, -values, values)
        copies.start(geo_v, geo_ref.at[micro])
        copies.start(cos_v, cos_ref.at[micro])
        copies.start(sin_v, sin_ref.at[micro])
        copies.finish()


def spread(values, pair, lane):
    base = values if pair == 0 else pltpu.roll(values, 64, 1)
    by_one = pltpu.roll(base, 32, 1)
    by_two = pltpu.roll(base, 64, 1)
    return jnp.where(lane < 32, base, jnp.where(lane < 96, by_one, by_two))


def tables(turn, kinds, frequency, earlier=None, held=None):
    shapes = [(KEYS, 128), (ROWS, WIDTH), (ROWS, WIDTH)]
    first = held is None
    operands = [turn, kinds, frequency] + ([] if first else [earlier, *held])
    return pl.pallas_call(
        partial(tables_kernel, first),
        out_shape=[jax.ShapeDtypeStruct((MICRO,) + shape, f32) for shape in shapes],
        in_specs=[pl.BlockSpec(memory_space=pltpu.SMEM)] * 2 + [ANY] * (len(operands) - 2),
        out_specs=[ANY] * 3,
        scratch_shapes=[vmem(1, WIDTH, dtype=f32)]
        + [vmem(*shape, dtype=f32) for shape in shapes]
        + [pltpu.SemaphoreType.DMA((8,))],
        input_output_aliases={} if first else {4: 0, 5: 1, 6: 2},
        compiler_params=pltpu.CompilerParams(vmem_limit_bytes=VMEM_LIMIT),
        name="tables",
    )(*operands)


def live_rows_of(kinds):
    rows = jnp.broadcast_to(jnp.arange(ROWS, dtype=jnp.int32).astype(f32)[None, :], (MICRO, ROWS))
    return places(kinds[:, None], rows)[3].reshape(-1, 1)


def product_kernel(
    offset, block, core_ref, left_in, right_in, other_ref, own_ref, sums_ref,
    other_v, own_v, right_v, other_out, own_out, sums_out, sems,
):
    copies = Copies(sems)
    core = core_ref[0]
    half = left_in.shape[1] // 2
    rows = other_v.shape[1]
    get_right = copies.start(right_in, right_v)
    get_other = copies.start(left_in.at[:, pl.ds(pl.multiple_of((1 - core) * half + offset, 128), rows)], other_v)
    get_own = copies.start(left_in.at[:, pl.ds(pl.multiple_of(core * half + offset, 128), rows)], own_v)
    copies.wait(get_right)
    for get, part_v, part_out, ref in (
        (get_other, other_v, other_out, other_ref),
        (get_own, own_v, own_out, own_ref),
    ):
        copies.wait(get)

        for at in range(0, rows, block):
            lanes = pl.ds(at, block)
            part_out[lanes, :] = lax.dot_general(
                part_v[:, lanes], right_v[...], TN, preferred_element_type=f32
            ).astype(bf16)
            copies.start(part_out.at[lanes], ref.at[lanes])
    sums_out[...] = jnp.dot(jnp.ones((16, right_v.shape[0]), bf16), right_v[...], preferred_element_type=f32)[:8]
    copies.start(sums_out, sums_ref)
    copies.finish()


def product_call(core, left, right, offset, rows):
    left = left.reshape(MICRO * ROWS, left.shape[-1])
    right = right.reshape(MICRO * ROWS, right.shape[-1])
    count, width = right.shape
    block = 512 if rows % 512 == 0 else 384
    return pl.pallas_call(
        partial(product_kernel, offset, block),
        out_shape=[jax.ShapeDtypeStruct((rows, width), bf16)] * 2 + [jax.ShapeDtypeStruct((8, width), f32)],
        in_specs=[pl.BlockSpec(memory_space=pltpu.SMEM), ANY, ANY],
        out_specs=[ANY] * 3,
        scratch_shapes=[
            vmem(count, rows), vmem(count, rows), vmem(count, width), vmem(rows, width), vmem(rows, width),
            vmem(8, width, dtype=f32), pltpu.SemaphoreType.DMA((16,)),
        ],
        compiler_params=pltpu.CompilerParams(vmem_limit_bytes=VMEM_LIMIT),
        name="weight_grad",
    )(core, left, right)


def send(value, source, target):
    return lax.ppermute(value, "section", [(source, target)])


def gathered(part, target, sections):
    pieces = [part if source == target else send(part, source, target) for source in range(sections)]
    return jnp.concatenate(pieces, axis=0)


def handed_out(whole, source, sections):
    section = lax.axis_index("section")
    share = whole.shape[0] // sections
    result = whole[source * share : (source + 1) * share]
    for target in range(sections):
        if target != source:
            piece = send(whole[target * share : (target + 1) * share], source, target)
            result = jnp.where(section == target, piece, result)
    return result


def added(one, other):
    return (one.astype(f32) + other.astype(f32)).astype(bf16)


def both_cores(pairs):
    return [(2 * a + core, 2 * b + core) for a, b in pairs for core in range(2)]


def core_swap():
    return [(i, i ^ 1) for i in range(lax.axis_size("dp"))]


class Relay:
    LAG = 3

    def __init__(self):
        self.chunks, self.sums, self.totals = [], [], []
        self.flying, self.joined, self.clock = [], [], 0

    def start(self, value, pairs, then, keep):
        self.flying.append((self.clock, lax.ppermute(value, "dp", pairs), then, keep))

    def step(self, *gate, every=False):
        ready = [f for f in self.flying if every or f[0] + self.LAG <= self.clock]
        self.flying = [f for f in self.flying if not (every or f[0] + self.LAG <= self.clock)]
        even = self.clock % 2 == 0
        fresh = self.chunks.pop(0) if even and self.chunks else None
        arrays, keeps = [f[1] for f in ready], [f[3] for f in ready]
        new = [] if fresh is None else [fresh[0]]
        joined, self.joined = self.joined, []
        results = [item.result for item in joined]
        arrays, keeps, new, gate, results = lax.optimization_barrier((arrays, keeps, new, gate, results))
        for item, result in zip(joined, results):
            item.result = result
        for (_, _, then, _), array, keep in zip(ready, arrays, keeps):
            then(array, keep)
        if even:
            self.outer_step((new[0],) + fresh[1:] if fresh else None, self.totals.pop(0) if self.totals else None)
        elif self.sums:
            both, done = self.sums.pop(0)
            pairs = both_cores([(1, 2), (2, 1)])
            self.start(both, pairs, lambda array, keep: self.totals.append((added(keep, array), done)), both)
        self.clock += 1
        return gate[0] if len(gate) == 1 else gate

    def outer_step(self, chunk, total):
        inward, outward = both_cores([(0, 1), (3, 2)]), both_cores([(1, 0), (2, 3)])
        chip = lax.axis_index("dp") // 2
        outer = (chip == 0) | (chip == 3)

        def inner_sum(array, own):
            self.sums.append((added(own, array), chunk[1]))

        def result(array, own):
            total[1](jnp.where(outer, array, own))

        if chunk and total and chunk[0].shape == total[0].shape:
            def land(array, keep):
                inner_sum(array, keep[0])
                result(array, keep[1])

            value = jnp.where(outer, chunk[0], total[0])
            self.start(value, inward + outward, land, (chunk[0], total[0]))
        else:
            if total:
                self.start(total[0], outward, result, total[0])
            if chunk:
                self.start(chunk[0], inward, inner_sum, chunk[0])

    def finish(self):
        while self.chunks or self.sums or self.totals or self.flying:
            self.step()


class LineSum:
    def __init__(self, relay, axis):
        self.relay, self.axis, self.count = relay, axis, 0
        self.totals, self.result = {}, None

    def add(self, other, mine, pieces):
        half = added(mine, lax.ppermute(other, "dp", core_swap()))
        for chunk in jnp.split(half, pieces, axis=self.axis):
            self.relay.chunks.append((chunk, partial(self.landed, self.count)))
            self.count += 1

    def landed(self, index, total):
        self.totals[index] = total
        if len(self.totals) == self.count:
            mine = jnp.concatenate([self.totals[i] for i in range(self.count)], axis=self.axis)
            self.relay.start(mine, core_swap(), self.join, mine)

    def join(self, other, mine):
        core = lax.axis_index("dp") % 2
        low, high = jnp.where(core == 0, mine, other), jnp.where(core == 0, other, mine)
        self.result = jnp.concatenate([low, high], axis=0).astype(f32)
        self.relay.joined.append(self)


def summed_by_compiler(part):
    count, rows = lax.axis_size("dp"), part.shape[0]
    part = jnp.pad(part, ((0, -rows % count), (0, 0)))
    own = lax.psum_scatter(part, "dp", scatter_dimension=0, tiled=True)
    return lax.all_gather(own, "dp", axis=0, tiled=True)[:rows].astype(f32)


SMALL_ROWS = 32


def per_device(
    tokens,
    cotangent,
    image_kind,
    norm_one_gain,
    norm_one_bias,
    qkv_weight,
    qkv_bias,
    rotary_freq,
    proj_weight,
    proj_bias,
    norm_two_gain,
    norm_two_bias,
    up_weight,
    up_bias,
    down_weight,
    down_bias,
):
    sections = lax.axis_size("section")
    section = lax.axis_index("section")
    last = sections - 1
    by_line = lax.axis_size("dp") == 8
    scal = section.astype(jnp.int32).reshape(1)
    core = (lax.axis_index("dp") % 2).astype(jnp.int32).reshape(1)
    low = core[0] == 0
    micros = jnp.arange(MICRO, dtype=jnp.int32)
    whole = tables(jnp.array([1, 0], jnp.int32), image_kind, rotary_freq)
    common = tables(jnp.stack([core[0], micros[1]]), image_kind, rotary_freq, tokens, whole)
    weights = (qkv_weight[0], proj_weight[0], up_weight[0], down_weight[0])
    vecs = (
        norm_one_gain, norm_one_bias, qkv_bias, proj_bias, norm_two_gain, norm_two_bias, up_bias, down_bias,
    )
    first_in = gathered(tokens, 0, sections)
    live_rows = live_rows_of(image_kind)
    last_in = gathered(cotangent, last, sections)
    last_in = jnp.where(live_rows > 0, last_in, bf16(0.0))

    def turn(layer, micro):
        return jnp.array([layer, micro], jnp.int32)

    states = None
    values = [first_in[m * ROWS : (m + 1) * ROWS] for m in range(MICRO)]
    for layer in range(sections):
        if layer == 2:
            values[0], last_in = lax.optimization_barrier((values[0], last_in))
        for micro in range(MICRO):
            out, states = front_call(scal, turn(layer, micro), values[micro], common, weights, vecs, states)
            if layer == 0 and micro == 0:
                common = tables(jnp.stack([1 - core[0], micros[1]]), image_kind, rotary_freq, out, common)
            values[micro] = send(out, layer, layer + 1) if layer < last else out
    fronts = dict(zip(STATES, states))
    backs = None
    grads = [last_in[m * ROWS : (m + 1) * ROWS] for m in range(MICRO)]
    out_grads = list(grads)
    relay = Relay()
    sums = [LineSum(relay, axis) for axis in (1, 0, 1, 0)]
    plain = [[], [], [], []]

    def to_sum(index, other, mine, pieces):
        if by_line:
            sums[index].add(other, mine, pieces)
        else:
            plain[index].append((jnp.where(low, mine, other), jnp.where(low, other, mine)))

    for layer in reversed(range(sections)):
        if 0 < layer < last:
            out_grads = [jnp.where(section == layer, new, old) for new, old in zip(grads, out_grads)]
        if layer == 0:
            received = grads[0]
        for micro in range(MICRO):
            end = layer == 0 and micro == MICRO - 1
            if end:
                grads[0], grads[1], out_grads = lax.optimization_barrier((grads[0], grads[1], out_grads))
                out_grads = [jnp.where(section == 0, new, old) for new, old in zip((received, grads[1]), out_grads)]
                all_grads = jnp.concatenate(out_grads, axis=0)
                for offset in (0, 768):
                    other, mine, b_down = product_call(core, fronts["g"], all_grads, offset, 768)
                    to_sum(3, other, mine, 2)
                relay.step()
                relay.step()
                grads[1] = relay.step(grads[1])
            dx, backs = back_call(scal, turn(layer, micro), grads[micro], common, weights, vecs, fronts, backs)
            if end:
                dx, backs = relay.step(dx, backs, every=True)
            grads[micro] = send(dx, layer, layer - 1) if layer > 0 else dx
    relay.step()
    backs = dict(zip(BACKS, relay.step(*backs)))
    other, mine, b_up = product_call(core, fronts["c"], backs["du"], 0, WIDTH // 2)
    to_sum(2, other, mine, 4)
    relay.step()
    dqkv = relay.step(backs["dqkv"])
    other, mine, b_qkv = product_call(core, fronts["a"], dqkv, 0, WIDTH // 2)
    to_sum(0, other, mine, 3)
    relay.step()
    o_kept, dz, small = relay.step(fronts["o"], backs["dz"], backs["small"])
    other, mine, b_proj = product_call(core, o_kept, dz, 0, WIDTH // 2)
    small = jnp.sum(small, axis=0)
    turns = small[4:6].reshape(2, HEADS, 2, 32)
    freq = (turns[:, :, 1] - turns[:, :, 0]).reshape(-1)
    small = jnp.concatenate(
        [small[2], small[3], b_qkv[0], freq, b_proj[0], small[0], small[1], b_up[0], b_down[0]]
    )
    small = small.astype(bf16).reshape(-1, WIDTH)
    small = jnp.pad(small, ((0, SMALL_ROWS - small.shape[0]), (0, 0)))
    half = SMALL_ROWS // 2
    mine = jnp.concatenate([mine, jnp.where(low, small[:half], small[half:])], axis=0)
    other = jnp.concatenate([other, jnp.where(low, small[half:], small[:half])], axis=0)
    to_sum(1, other, mine, 1)
    relay.step()
    values = relay.step(*values)
    final = jnp.where(live_rows > 0, jnp.concatenate(values, axis=0), bf16(0.0))
    block_out = handed_out(final, last, sections)
    relay.step()
    relay.step()
    relay.step()
    relay.step()
    grads[0], grads[1], block_out = relay.step(*grads, block_out)
    grad_tokens = handed_out(jnp.concatenate(grads, axis=0), 0, sections)
    relay.step()
    relay.step()
    relay.step()
    grad_tokens = relay.step(grad_tokens)
    relay.finish()
    if by_line:
        grad_qkv, grad_proj, grad_up, grad_down = (item.result for item in sums)
    else:
        grad_qkv, grad_proj, grad_up, grad_down = (
            summed_by_compiler(jnp.concatenate([part[side] for side in range(2) for part in parts], axis=0))
            for parts in plain
        )
    middle = WIDTH // 2
    small = jnp.concatenate([grad_proj[middle : middle + half], grad_proj[middle + half + middle :]], axis=0).reshape(-1)
    grad_proj = jnp.concatenate([grad_proj[:middle], grad_proj[middle + half : middle + half + middle]], axis=0)
    sizes = (WIDTH, WIDTH, 3 * WIDTH, WIDTH, WIDTH, WIDTH, WIDTH, HIDDEN, WIDTH)
    ends = np.cumsum((0,) + sizes)
    g_one, b_one, b_qkv, freq, b_proj, g_two, b_two, b_up, b_down = (
        small[int(ends[i]) : int(ends[i + 1])][None] for i in range(len(sizes))
    )
    return (
        block_out, grad_tokens.astype(f32), g_one, b_one, grad_qkv[None], b_qkv, freq,
        grad_proj[None], b_proj, g_two, b_two, grad_up[None], b_up, grad_down[None], b_down,
    )


def solution(mesh):
    row = P(("dp", "section"), None)
    vector = P("section", None)
    matrix = P("section", None, None)
    params = (
        vector, vector, matrix, vector, vector, matrix, vector, vector, vector, matrix, vector, matrix, vector,
    )
    return jax.shard_map(
        per_device,
        mesh=mesh,
        in_specs=(row, row, P("dp")) + params,
        out_specs=(row, row) + params,
        check_vma=False,
    )
```

```python
from functools import partial
import math

import jax
import jax.numpy as jnp
import numpy as np
from jax import lax
from jax.experimental import pallas as pl
from jax.experimental.pallas import tpu as pltpu
from jax.sharding import PartitionSpec as P

HEADS = 12
SIDE_LARGE = 20
SIDE_MID = 16
SIDE_SMALL = 14
MICRO = 2
ROWS = 400
KEYS = 512
WIDTH = 768
HIDDEN = 3072
PAIRS = HEADS // 2
EPSILON = 1e-06
MASKED = -1e30
LOG2E = math.log2(math.e)
LN2 = math.log(2.0)
GELU_ONE = math.sqrt(2.0 / math.pi)
GELU_TWO = GELU_ONE * 0.044715

f32 = jnp.float32
bf16 = jnp.bfloat16
NT = (((1,), (1,)), ((), ()))
TN = (((0,), (0,)), ((), ()))

VEC_SIZES = (WIDTH, WIDTH, 3 * WIDTH, WIDTH, WIDTH, WIDTH, HIDDEN, WIDTH)
VEC_AT = tuple(int(v) for v in np.cumsum((0,) + VEC_SIZES))


def vec_part(vec_ref, index):
    return vec_ref[:, VEC_AT[index] : VEC_AT[index + 1]]


def swap_halves(values):
    lane = lax.broadcasted_iota(jnp.int32, values.shape, 1) % 64
    width = values.shape[1]
    return jnp.where(lane < 32, pltpu.roll(values, width - 32, 1), pltpu.roll(values, 32, 1))


def norm_parts(values):
    center = values - jnp.mean(values, axis=-1, keepdims=True)
    inverse = lax.rsqrt(jnp.mean(center * center, axis=-1, keepdims=True) + EPSILON)
    return center * inverse, inverse


def gelu_parts(pre):
    low = pre.astype(bf16)
    square = low * low
    tanh = jnp.tanh(low * (bf16(GELU_ONE) + bf16(GELU_TWO) * square))
    half = bf16(0.5) + bf16(0.5) * tanh
    value = low * half
    slope = half + (value - value * half) * (bf16(2 * GELU_ONE) + bf16(6 * GELU_TWO) * square)
    return value, slope


class Copies:
    def __init__(self, sems):
        self.sems = sems
        self.open = []
        self.used = 0

    def start(self, source, target):
        copy = pltpu.make_async_copy(source, target, self.sems.at[self.used])
        self.used += 1
        copy.start()
        self.open.append(copy)
        return copy

    def wait(self, *copies):
        for copy in copies:
            self.open = [other for other in self.open if other is not copy]
            copy.wait()

    def finish(self):
        self.wait(*list(self.open))


STATE_SHAPES = (
    ("x", (ROWS, WIDTH), bf16),
    ("a", (ROWS, WIDTH), bf16),
    ("qkv", (ROWS, 3 * WIDTH), bf16),
    ("e", (HEADS, ROWS, KEYS), bf16),
    ("linv", (ROWS, WIDTH), f32),
    ("o", (ROWS, WIDTH), bf16),
    ("n2", (ROWS, WIDTH), bf16),
    ("r2", (ROWS, 128), f32),
    ("c", (ROWS, WIDTH), bf16),
    ("g", (ROWS, HIDDEN), bf16),
    ("gp", (ROWS, HIDDEN), bf16),
)
STATES = tuple(name for name, _, _ in STATE_SHAPES)


def front_kernel(first, scal, layer, *refs):
    x_in, geo_in, cos_in, sin_in, wqkv_in, wp_in, wu_in, wd_in = refs[:8]
    vec_in, rest = refs[8:16], refs[17:]
    if not first:
        rest = rest[len(STATES) :]
    out_ref = rest[0]
    state = dict(zip(STATES, rest[1 : 1 + len(STATES)]))
    (
        x_v, vec_v, geo_v, cos_v, sin_v, wqkv_v, wp_v, wu_v, wd_v,
        a_v, qkv_v, e_v, s_v, li_v, o_v, m_v, n2_v, r2_v, c_v, g_v, gp_v, qcode_v, kcode_v, out_v, sems,
    ) = rest[1 + len(STATES) :]

    @pl.when(scal[0] == layer[0])
    def _():
        slot = layer[1]
        copies = Copies(sems)
        wait = copies.wait
        get_x = copies.start(x_in, x_v)
        get_vec = [
            copies.start(part, vec_v.at[:, pl.ds(at, size)]) for part, at, size in zip(vec_in, VEC_AT, VEC_SIZES)
        ]
        get_geo = copies.start(geo_in.at[slot], geo_v)
        get_qkv = [
            copies.start(wqkv_in.at[:, pl.ds(at, WIDTH)], wqkv_v.at[:, pl.ds(at, WIDTH)])
            for at in range(0, 3 * WIDTH, WIDTH)
        ]
        get_cos = copies.start(cos_in.at[slot], cos_v)
        get_sin = copies.start(sin_in.at[slot], sin_v)

        def put(source, name):
            copies.start(source, state[name].at[slot])

        qkv_v[ROWS:KEYS, :] = jnp.zeros((KEYS - ROWS, 3 * WIDTH), bf16)
        wait(get_x, get_geo, *get_vec)
        normed, _ = norm_parts(x_v[...].astype(f32))
        a_v[...] = (normed * vec_part(vec_v, 0) + vec_part(vec_v, 1)).astype(bf16)
        segment = geo_v[:, 2:3]
        code = (lax.broadcasted_iota(jnp.int32, (KEYS, 128), 1) % 64).astype(f32)
        qcode_v[...] = jnp.where(segment[:ROWS] == code[:ROWS], 1.0, 0.0).astype(bf16)
        kcode_v[...] = jnp.where((segment != code) & (code < 4), MASKED, 0.0).astype(bf16)
        for part in range(3):
            at = part * WIDTH
            wait(get_qkv[part])
            if part == 0:
                wait(get_cos, get_sin)
                get_wp = copies.start(wp_in, wp_v)
                get_wu = copies.start(wu_in, wu_v)
                get_wd = copies.start(wd_in, wd_v)
            acc = jnp.dot(a_v[...], wqkv_v[:, at : at + WIDTH], preferred_element_type=f32)
            acc = acc + vec_v[:, VEC_AT[2] + at : VEC_AT[2] + at + WIDTH]
            if part < 2:
                acc = acc * cos_v[...] + swap_halves(acc) * sin_v[...]
            if part == 0:
                acc = acc * (LOG2E / 8.0)
            qkv_v[:ROWS, at : at + WIDTH] = acc.astype(bf16)

        for pair in range(PAIRS):
            lanes = pl.ds(pair * 128, 128)
            klanes = pl.ds(pair * 128 + WIDTH, 128)
            vlanes = pl.ds(pair * 128 + 2 * WIDTH, 128)
            q_two = qkv_v[:ROWS, lanes]
            k_two = qkv_v[:, klanes]
            v_two = qkv_v[:, vlanes]
            lane_q = lax.broadcasted_iota(jnp.int32, (ROWS, 128), 1) // 64
            lane_k = lax.broadcasted_iota(jnp.int32, (KEYS, 128), 1) // 64
            for head in range(2):
                q_one = jnp.where(lane_q == head, q_two, qcode_v[...])
                k_one = jnp.where(lane_k == head, k_two, kcode_v[...])
                s_v[2 * (pair % 2) + head] = lax.dot_general(q_one, k_one, NT, preferred_element_type=f32)
            sums = []
            for head in range(2):
                v_one = jnp.where(lane_k == head, v_two, bf16(1.0))
                scores = s_v[2 * (pair % 2) + head]
                peak = jnp.max(scores, axis=1, keepdims=True)
                e_v[2 * pair + head] = jnp.exp2(scores - peak).astype(bf16)
                sums.append(jnp.dot(e_v[2 * pair + head], v_one, preferred_element_type=f32))
            total = pltpu.roll(jnp.where(lane_q == 0, sums[1], sums[0]), 64, 1)
            inverse = 1.0 / total
            li_v[:, lanes] = inverse
            o_v[:, lanes] = (jnp.where(lane_q == 0, sums[0], sums[1]) * inverse).astype(bf16)
        put(x_v, "x")
        put(a_v, "a")
        put(qkv_v.at[pl.ds(0, ROWS)], "qkv")
        put(e_v, "e")
        put(li_v, "linv")
        put(o_v, "o")
        wait(get_wp)
        middle = (
            x_v[...].astype(f32)
            + jnp.dot(o_v[...], wp_v[...], preferred_element_type=f32)
            + vec_part(vec_v, 3)
        )
        m_v[...] = middle
        normed, inverse = norm_parts(middle)
        n2_v[...] = normed.astype(bf16)
        r2_v[...] = jnp.broadcast_to(inverse, (ROWS, 128))
        c_v[...] = (normed * vec_part(vec_v, 4) + vec_part(vec_v, 5)).astype(bf16)
        put(n2_v, "n2")
        put(r2_v, "r2")
        put(c_v, "c")
        wait(get_wu)
        chunk = 1024

        def up_step(step, carry):
            lanes = pl.ds(pl.multiple_of(step * chunk, chunk), chunk)
            blanes = pl.ds(pl.multiple_of(step * chunk + VEC_AT[6], 128), chunk)
            pre = jnp.dot(c_v[...], wu_v[:, lanes], preferred_element_type=f32) + vec_v[:, blanes]
            value, slope = gelu_parts(pre)
            g_v[:, lanes] = value
            gp_v[:, lanes] = slope
            return carry

        lax.fori_loop(0, HIDDEN // chunk, up_step, 0)
        put(gp_v, "gp")
        put(g_v, "g")
        wait(get_wd)
        for at in range(0, WIDTH, 256):
            part = pl.ds(at, 256)
            out = jnp.dot(g_v[...], wd_v[:, part], preferred_element_type=f32)
            out = out + m_v[:, part] + vec_v[:, VEC_AT[7] + at : VEC_AT[7] + at + 256]
            out_v[:, part] = out.astype(bf16)
            copies.start(out_v.at[:, part], out_ref.at[:, part])
        copies.finish()


ANY = pl.BlockSpec(memory_space=pl.ANY)
VMEM_LIMIT = 60 * 2**20


def vmem(*shape, dtype=bf16):
    return pltpu.VMEM(shape, dtype)


def call_states(kernel, first, operands, smem, states, plain_out, shapes, scratch, name):
    count = len(operands)
    state_out = [jax.ShapeDtypeStruct((MICRO,) + shape, dtype) for _, shape, dtype in shapes]
    operands = list(operands) + ([] if first else list(states))
    results = pl.pallas_call(
        partial(kernel, first),
        out_shape=list(plain_out) + state_out,
        in_specs=[pl.BlockSpec(memory_space=pltpu.SMEM)] * smem + [ANY] * (len(operands) - smem),
        out_specs=[ANY] * (len(plain_out) + len(shapes)),
        scratch_shapes=scratch,
        input_output_aliases={} if first else {count + i: len(plain_out) + i for i in range(len(shapes))},
        compiler_params=pltpu.CompilerParams(vmem_limit_bytes=VMEM_LIMIT),
        name=name,
    )(*operands)
    return results[0], tuple(results[1:])


def front_call(scal, layer, x, common, weights, vecs, states, earlier):
    scratch = [
        vmem(ROWS, WIDTH), vmem(1, VEC_AT[-1], dtype=f32), vmem(KEYS, 128, dtype=f32),
        vmem(ROWS, WIDTH, dtype=f32), vmem(ROWS, WIDTH, dtype=f32),
        vmem(WIDTH, 3 * WIDTH), vmem(WIDTH, WIDTH), vmem(WIDTH, HIDDEN), vmem(HIDDEN, WIDTH),
        vmem(ROWS, WIDTH), vmem(KEYS, 3 * WIDTH), vmem(HEADS, ROWS, KEYS), vmem(4, ROWS, KEYS, dtype=f32),
        vmem(ROWS, WIDTH, dtype=f32), vmem(ROWS, WIDTH), vmem(ROWS, WIDTH, dtype=f32),
        vmem(ROWS, WIDTH), vmem(ROWS, 128, dtype=f32), vmem(ROWS, WIDTH),
        vmem(ROWS, HIDDEN), vmem(ROWS, HIDDEN), vmem(ROWS, 128), vmem(KEYS, 128), vmem(ROWS, WIDTH),
        pltpu.SemaphoreType.DMA((36,)),
    ]
    operands = [scal, layer, x, *common, *weights, *vecs, earlier]
    out = jax.ShapeDtypeStruct((ROWS, WIDTH), bf16)
    return call_states(front_kernel, states is None, operands, 2, states, [out], STATE_SHAPES, scratch, "layer_front")


BACK_SHAPES = (
    ("du", (ROWS, HIDDEN), bf16),
    ("dz", (ROWS, WIDTH), bf16),
    ("dqkv", (ROWS, 3 * WIDTH), bf16),
    ("small", (8, WIDTH), f32),
)
BACKS = tuple(name for name, _, _ in BACK_SHAPES)


def back_kernel(first, scal, layer, *refs):
    dy_in, geo_in, cos_in, sin_in, wqkv_in, wp_in, wu_in, wd_in, gain_one_in, gain_two_in = refs[:10]
    saved = dict(zip(KEPT, refs[10 : 10 + len(KEPT)]))
    rest = refs[10 + len(KEPT) :]
    if not first:
        rest = rest[len(BACKS) :]
    dx_ref = rest[0]
    state = dict(zip(BACKS, rest[1 : 1 + len(BACKS)]))
    (
        dy_v, geo_v, cos_v, sin_v, wqkv_v, wp_v, wu_v, wd_v, gains_v,
        gp_v, n2_v, r2_v, li_v, qkv_v, e_v, o_v, x_v,
        du_v, dz_v, dm_v, dop_v, qt_v, dot_v, dq_v, dkt_v, dvt_v, dqkv_v, small_v, dx_v, sems,
    ) = rest[1 + len(BACKS) :]

    @pl.when(scal[0] == layer[0])
    def _():
        slot = layer[1]
        copies = Copies(sems)
        wait = copies.wait
        chunk = 1024
        steps = HIDDEN // chunk
        get_dy = copies.start(dy_in, dy_v)
        get_wd, get_gp = [], []
        for step in range(steps):
            part = pl.ds(step * chunk, chunk)
            get_wd.append(copies.start(wd_in.at[part], wd_v.at[part]))
            get_gp.append(copies.start(saved["gp"].at[slot, :, part], gp_v.at[:, part]))
        get_wu = copies.start(wu_in, wu_v)
        get_norm = [
            copies.start(saved["n2"].at[slot], n2_v),
            copies.start(saved["r2"].at[slot], r2_v),
            copies.start(gain_one_in, gains_v.at[pl.ds(0, 1)]),
            copies.start(gain_two_in, gains_v.at[pl.ds(8, 1)]),
        ]

        def put(source, name):
            copies.start(source, state[name].at[slot])

        qkv_v[ROWS:KEYS, :] = jnp.zeros((KEYS - ROWS, 3 * WIDTH), bf16)
        wait(get_dy)
        for step in range(steps):
            part = slice(step * chunk, (step + 1) * chunk)
            wait(get_wd[step], get_gp[step])
            act = lax.dot_general(dy_v[...], wd_v[part, :], NT, preferred_element_type=f32)
            du_v[:, part] = act.astype(bf16) * gp_v[:, part]
        get_wp = copies.start(wp_in, wp_v)
        get_li = copies.start(saved["linv"].at[slot], li_v)
        get_qkv = copies.start(saved["qkv"].at[slot], qkv_v.at[pl.ds(0, ROWS)])
        get_o = copies.start(saved["o"].at[slot], o_v)
        get_e = copies.start(saved["e"].at[slot], e_v)
        get_turn = [
            copies.start(cos_in.at[slot], cos_v),
            copies.start(sin_in.at[slot], sin_v),
            copies.start(geo_in.at[slot], geo_v),
        ]
        get_x = copies.start(saved["x"].at[slot], x_v)
        get_wqkv = copies.start(wqkv_in, wqkv_v)
        put(du_v, "du")
        wait(get_wu)
        dc = lax.dot_general(du_v[...], wu_v[...], NT, preferred_element_type=f32)
        wait(*get_norm)
        normed = n2_v[...].astype(f32)
        small_v[0:1, :] = jnp.sum(dc * normed, axis=0, keepdims=True)
        small_v[1:2, :] = jnp.sum(dc, axis=0, keepdims=True)
        hat = dc * gains_v[8:9, :]
        dm = dy_v[...].astype(f32) + r2_v[:, 0:1] * (
            hat
            - jnp.mean(hat, axis=-1, keepdims=True)
            - normed * jnp.mean(hat * normed, axis=-1, keepdims=True)
        )
        dm_v[...] = dm
        dz_v[...] = dm.astype(bf16)
        put(dz_v, "dz")
        wait(get_wp, get_li)
        do = lax.dot_general(dz_v[...], wp_v[...], NT, preferred_element_type=f32)
        dop_v[...] = (do * li_v[...]).astype(bf16)
        dot_v[...] = dop_v[...].T
        wait(get_qkv)
        qt_v[...] = qkv_v[:ROWS, :WIDTH].T
        wait(get_o, get_e)

        def pair_step(step, carry):
            for pair in [step * 2 + i for i in range(2)]:
                lanes = pl.ds(pl.multiple_of(pair * 128, 128), 128)
                klanes = pl.ds(pl.multiple_of(pair * 128 + WIDTH, 128), 128)
                vlanes = pl.ds(pl.multiple_of(pair * 128 + 2 * WIDTH, 128), 128)
                do_two = dop_v[:, lanes]
                k_two = qkv_v[:, klanes]
                v_two = qkv_v[:, vlanes]
                prod = do_two.astype(f32) * o_v[:, lanes].astype(f32)
                lane = lax.broadcasted_iota(jnp.int32, (ROWS, 128), 1) // 64
                dqs = []
                for head in range(2):
                    rows = pl.ds(pl.multiple_of(pair * 128 + head * 64, 64), 64)
                    do_one = jnp.where(lane == head, do_two, bf16(0.0))
                    dp = lax.dot_general(do_one, v_two, NT, preferred_element_type=f32)
                    delta = jnp.sum(jnp.where(lane == head, prod, 0.0), axis=1, keepdims=True)
                    probs = e_v[2 * pair + head]
                    ds = probs * (dp - delta).astype(bf16)
                    dqs.append(jnp.dot(ds, k_two, preferred_element_type=f32))
                    dkt_v[rows, :] = jnp.dot(qt_v[rows, :], ds, preferred_element_type=f32)
                    dvt_v[rows, :] = jnp.dot(dot_v[rows, :], probs, preferred_element_type=f32).astype(bf16)
                dq_v[:, lanes] = jnp.where(lane == 0, dqs[0], dqs[1])
            return carry

        lax.fori_loop(0, PAIRS // 2, pair_step, 0)
        wait(*get_turn)
        dqkv_v[:, 2 * WIDTH :] = dvt_v[...].T[:ROWS]
        dk = dkt_v[...].T[:ROWS]
        dq = dq_v[...]
        turn = dq * swap_halves(qkv_v[:ROWS, :WIDTH].astype(f32)) + dk * swap_halves(
            qkv_v[:ROWS, WIDTH : 2 * WIDTH].astype(f32)
        )
        small_v[4:5, :] = LN2 * jnp.sum(turn * geo_v[:ROWS, 0:1], axis=0, keepdims=True)
        small_v[5:6, :] = LN2 * jnp.sum(turn * geo_v[:ROWS, 1:2], axis=0, keepdims=True)
        dqkv_v[:, :WIDTH] = (0.125 * (dq * cos_v[...] - swap_halves(dq) * sin_v[...])).astype(bf16)
        dqkv_v[:, WIDTH : 2 * WIDTH] = (LN2 * (dk * cos_v[...] - swap_halves(dk) * sin_v[...])).astype(bf16)
        put(dqkv_v, "dqkv")
        wait(get_x)
        normed, inverse = norm_parts(x_v[...].astype(f32))
        wait(get_wqkv)
        da = lax.dot_general(dqkv_v[...], wqkv_v[...], NT, preferred_element_type=f32)
        small_v[2:3, :] = jnp.sum(da * normed, axis=0, keepdims=True)
        small_v[3:4, :] = jnp.sum(da, axis=0, keepdims=True)
        put(small_v, "small")
        hat = da * gains_v[0:1, :]
        dx = dm_v[...] + inverse * (
            hat
            - jnp.mean(hat, axis=-1, keepdims=True)
            - normed * jnp.mean(hat * normed, axis=-1, keepdims=True)
        )
        dx_v[...] = dx.astype(bf16)
        copies.start(dx_v, dx_ref)
        copies.finish()


KEPT = ("gp", "n2", "r2", "linv", "qkv", "e", "o", "x")


def back_call(scal, layer, dy, common, weights, vecs, fronts, backs):
    scratch = [
        vmem(ROWS, WIDTH), vmem(KEYS, 128, dtype=f32), vmem(ROWS, WIDTH, dtype=f32), vmem(ROWS, WIDTH, dtype=f32),
        vmem(WIDTH, 3 * WIDTH), vmem(WIDTH, WIDTH), vmem(WIDTH, HIDDEN), vmem(HIDDEN, WIDTH), vmem(16, WIDTH, dtype=f32),
        vmem(ROWS, HIDDEN), vmem(ROWS, WIDTH), vmem(ROWS, 128, dtype=f32), vmem(ROWS, WIDTH, dtype=f32),
        vmem(KEYS, 3 * WIDTH), vmem(HEADS, ROWS, KEYS), vmem(ROWS, WIDTH), vmem(ROWS, WIDTH),
        vmem(ROWS, HIDDEN), vmem(ROWS, WIDTH), vmem(ROWS, WIDTH, dtype=f32), vmem(ROWS, WIDTH),
        vmem(WIDTH, ROWS), vmem(WIDTH, ROWS), vmem(ROWS, WIDTH, dtype=f32),
        vmem(WIDTH, KEYS, dtype=f32), vmem(WIDTH, KEYS), vmem(ROWS, 3 * WIDTH), vmem(8, WIDTH, dtype=f32), vmem(ROWS, WIDTH),
        pltpu.SemaphoreType.DMA((36,)),
    ]
    operands = [scal, layer, dy, *common, *weights, vecs[0], vecs[4], *(fronts[name] for name in KEPT)]
    out = jax.ShapeDtypeStruct((ROWS, WIDTH), bf16)
    return call_states(back_kernel, backs is None, operands, 2, backs, [out], BACK_SHAPES, scratch, "layer_back")


def side_of(kind):
    return jnp.where(kind == 0, float(SIDE_LARGE), jnp.where(kind == 1, float(SIDE_MID), float(SIDE_SMALL)))


def places(kind, rows):
    side = side_of(kind)
    area = side * side
    images = jnp.where(kind == 2, 2.0, 1.0)
    image = (rows >= area).astype(f32) + (rows >= 2 * area).astype(f32)
    live = (image < images) & (rows < ROWS)
    local = rows - image * area
    patch_row = jnp.floor((local + 0.5) / side)
    patch_col = local - patch_row * side
    zero = jnp.zeros_like(rows)
    segment = jnp.where(live, image, jnp.where(rows < ROWS, 3.0, 2.0))
    return jnp.where(live, patch_row, zero), jnp.where(live, patch_col, zero), segment, live


def split_low(values):
    high = values.astype(bf16)
    return jnp.concatenate([high, (values - high.astype(f32)).astype(bf16)], axis=0)


def tables_kernel(kind_ref, freq_in, geo_ref, cos_ref, sin_ref, freq_v, geo_v, cos_v, sin_v, sems):
    copies = Copies(sems)
    copies.wait(copies.start(freq_in, freq_v))
    step = lax.broadcasted_iota(jnp.int32, (32, WIDTH // 2), 0).astype(f32)
    angles = [step * freq_v[:, at : at + WIDTH // 2] for at in (0, WIDTH // 2)]
    waves = [split_low(jnp.concatenate([jnp.cos(angle), jnp.sin(angle)], axis=1)) for angle in angles]
    sixteen = lax.broadcasted_iota(jnp.int32, (ROWS, 64), 1) % 32
    for micro in range(MICRO):
        rows = lax.broadcasted_iota(jnp.int32, (KEYS, 128), 0).astype(f32)
        lane = lax.broadcasted_iota(jnp.int32, (KEYS, 128), 1)
        patch_row, patch_col, segment, _ = places(kind_ref[micro], rows)
        geo_v[micro] = jnp.where(lane == 0, patch_row, jnp.where(lane == 1, patch_col, segment))
        picks = [
            jnp.where(sixteen.astype(f32) == patch[:ROWS, :64], 1.0, 0.0).astype(bf16)
            for patch in (patch_row, patch_col)
        ]
        row_wave, col_wave = (
            jnp.dot(pick, wave, preferred_element_type=f32) for pick, wave in zip(picks, waves)
        )
        half = WIDTH // 2
        row_cos, row_sin = row_wave[:, :half], row_wave[:, half:]
        col_cos, col_sin = col_wave[:, :half], col_wave[:, half:]
        cosine = row_cos * col_cos - row_sin * col_sin
        sine = row_sin * col_cos + row_cos * col_sin
        lane = lax.broadcasted_iota(jnp.int32, (ROWS, 128), 1)
        for part in range(half // 128):
            for pair in range(2):
                at = (2 * part + pair) * 128
                cos_v[micro, :, at : at + 128] = spread(cosine[:, part * 128 : part * 128 + 128], pair, lane)
                values = spread(sine[:, part * 128 : part * 128 + 128], pair, lane)
                sin_v[micro, :, at : at + 128] = jnp.where(lane % 64 < 32, -values, values)
        copies.start(geo_v.at[micro], geo_ref.at[micro])
        copies.start(cos_v.at[micro], cos_ref.at[micro])
        copies.start(sin_v.at[micro], sin_ref.at[micro])
    copies.finish()


def spread(values, pair, lane):
    base = values if pair == 0 else pltpu.roll(values, 64, 1)
    by_one = pltpu.roll(base, 32, 1)
    by_two = pltpu.roll(base, 64, 1)
    return jnp.where(lane < 32, base, jnp.where(lane < 96, by_one, by_two))


def tables(kinds, frequency):
    shapes = [(MICRO, KEYS, 128), (MICRO, ROWS, WIDTH), (MICRO, ROWS, WIDTH)]
    return pl.pallas_call(
        tables_kernel,
        out_shape=[jax.ShapeDtypeStruct(shape, f32) for shape in shapes],
        in_specs=[pl.BlockSpec(memory_space=pltpu.SMEM), ANY],
        out_specs=[ANY] * 3,
        scratch_shapes=[vmem(1, WIDTH, dtype=f32)]
        + [vmem(*shape, dtype=f32) for shape in shapes]
        + [pltpu.SemaphoreType.DMA((8,))],
        compiler_params=pltpu.CompilerParams(vmem_limit_bytes=VMEM_LIMIT),
        name="tables",
    )(kinds, frequency)


def live_rows_of(kinds):
    rows = jnp.broadcast_to(jnp.arange(ROWS, dtype=jnp.int32).astype(f32)[None, :], (MICRO, ROWS))
    return places(kinds[:, None], rows)[3].reshape(-1, 1)


def product_kernel(
    offset, block, core_ref, left_in, right_in, other_ref, own_ref, sums_ref,
    other_v, own_v, right_v, other_out, own_out, sums_out, sems,
):
    copies = Copies(sems)
    core = core_ref[0]
    half = left_in.shape[1] // 2
    rows = other_v.shape[1]
    get_right = copies.start(right_in, right_v)
    get_other = copies.start(left_in.at[:, pl.ds(pl.multiple_of((1 - core) * half + offset, 128), rows)], other_v)
    get_own = copies.start(left_in.at[:, pl.ds(pl.multiple_of(core * half + offset, 128), rows)], own_v)
    copies.wait(get_right)
    for get, part_v, part_out, ref in (
        (get_other, other_v, other_out, other_ref),
        (get_own, own_v, own_out, own_ref),
    ):
        copies.wait(get)

        for at in range(0, rows, block):
            lanes = pl.ds(at, block)
            part_out[lanes, :] = lax.dot_general(
                part_v[:, lanes], right_v[...], TN, preferred_element_type=f32
            ).astype(bf16)
            copies.start(part_out.at[lanes], ref.at[lanes])
    sums_out[...] = jnp.dot(jnp.ones((16, right_v.shape[0]), bf16), right_v[...], preferred_element_type=f32)[:8]
    copies.start(sums_out, sums_ref)
    copies.finish()


def product_call(core, left, right, offset, rows):
    left = left.reshape(MICRO * ROWS, left.shape[-1])
    right = right.reshape(MICRO * ROWS, right.shape[-1])
    count, width = right.shape
    block = 512 if rows % 512 == 0 else 384
    return pl.pallas_call(
        partial(product_kernel, offset, block),
        out_shape=[jax.ShapeDtypeStruct((rows, width), bf16)] * 2 + [jax.ShapeDtypeStruct((8, width), f32)],
        in_specs=[pl.BlockSpec(memory_space=pltpu.SMEM), ANY, ANY],
        out_specs=[ANY] * 3,
        scratch_shapes=[
            vmem(count, rows), vmem(count, rows), vmem(count, width), vmem(rows, width), vmem(rows, width),
            vmem(8, width, dtype=f32), pltpu.SemaphoreType.DMA((16,)),
        ],
        compiler_params=pltpu.CompilerParams(vmem_limit_bytes=VMEM_LIMIT),
        name="weight_grad",
    )(core, left, right)


SMALL_AT = (WIDTH, WIDTH, 3 * WIDTH, WIDTH, WIDTH, WIDTH, WIDTH, WIDTH, HIDDEN, WIDTH)
SMALL_ROWS = 32


def small_kernel(small_in, qkv_in, proj_in, up_in, down_in, low_ref, high_ref, *scratch):
    small_v, qkv_v, proj_v, up_v, down_v, rows_v, low_v, high_v, sems = scratch
    copies = Copies(sems)
    for source, target in ((small_in, small_v), (qkv_in, qkv_v), (proj_in, proj_v), (up_in, up_v), (down_in, down_v)):
        copies.start(source, target)
    copies.finish()
    rows_v[...] = jnp.zeros_like(rows_v)
    small = small_v[0] + small_v[1]
    parts = [small[2:3], small[3:4]]
    parts += [qkv_v[0:1, at : at + WIDTH] for at in range(0, 3 * WIDTH, WIDTH)]
    parts += [small[4:5], small[5:6], proj_v[0:1, :], small[0:1], small[1:2]]
    parts += [up_v[0:1, at : at + WIDTH] for at in range(0, HIDDEN, WIDTH)]
    parts += [down_v[0:1, :]]
    for index, part in enumerate(parts):
        rows_v[index : index + 1, :] = part
    half = SMALL_ROWS // 2
    low_v[...] = rows_v[:half, :].astype(bf16)
    high_v[...] = rows_v[half:, :].astype(bf16)
    copies.start(low_v, low_ref)
    copies.start(high_v, high_ref)
    copies.finish()


def small_call(small, qkv, proj, up, down):
    half = (SMALL_ROWS // 2, WIDTH)
    return pl.pallas_call(
        small_kernel,
        out_shape=[jax.ShapeDtypeStruct(half, bf16)] * 2,
        in_specs=[ANY] * 5,
        out_specs=[ANY] * 2,
        scratch_shapes=[
            vmem(MICRO, 8, WIDTH, dtype=f32), vmem(8, 3 * WIDTH, dtype=f32), vmem(8, WIDTH, dtype=f32),
            vmem(8, HIDDEN, dtype=f32), vmem(8, WIDTH, dtype=f32), vmem(SMALL_ROWS, WIDTH, dtype=f32),
            vmem(*half), vmem(*half), pltpu.SemaphoreType.DMA((8,)),
        ],
        name="small_grads",
    )(small, qkv, proj, up, down)


def send(value, source, target):
    return lax.ppermute(value, "section", [(source, target)])


def gathered(part, target, sections):
    pieces = [part if source == target else send(part, source, target) for source in range(sections)]
    return jnp.concatenate(pieces, axis=0)


def handed_out(whole, source, sections):
    section = lax.axis_index("section")
    share = whole.shape[0] // sections
    result = whole[source * share : (source + 1) * share]
    for target in range(sections):
        if target != source:
            piece = send(whole[target * share : (target + 1) * share], source, target)
            result = jnp.where(section == target, piece, result)
    return result


def added(one, other):
    return (one.astype(f32) + other.astype(f32)).astype(bf16)


def both_cores(pairs):
    return [(2 * a + core, 2 * b + core) for a, b in pairs for core in range(2)]


def core_swap():
    return [(i, i ^ 1) for i in range(lax.axis_size("dp"))]


class Relay:
    def __init__(self):
        self.chunks, self.sums, self.totals = [], [], []
        self.flying, self.joined, self.clock = [], [], 0

    def start(self, value, pairs, then, keep):
        self.flying.append((self.clock, lax.ppermute(value, "dp", pairs), then, keep))

    def step(self, *gate, outer=0, inner=0, age=3):
        ready = [f for f in self.flying if f[0] + age <= self.clock]
        self.flying = [f for f in self.flying if f[0] + age > self.clock]
        fresh, self.chunks = self.chunks[:outer], self.chunks[outer:]
        arrays, keeps = [f[1] for f in ready], [f[3] for f in ready]
        new = [value for value, _ in fresh]
        joined, self.joined = self.joined, []
        results = [item.result for item in joined]
        arrays, keeps, new, gate, results = lax.optimization_barrier((arrays, keeps, new, gate, results))
        for item, result in zip(joined, results):
            item.result = result
        for (_, _, then, _), array, keep in zip(ready, arrays, keeps):
            then(array, keep)
        fresh = [(value, done) for value, (_, done) in zip(new, fresh)]
        for _ in range(outer):
            self.outer_start(fresh.pop(0) if fresh else None, self.totals.pop(0) if self.totals else None)
        for _ in range(min(inner, len(self.sums))):
            self.inner_start(*self.sums.pop(0))
        self.clock += 1
        return gate[0] if len(gate) == 1 else gate

    def inner_start(self, both, done):
        pairs = both_cores([(1, 2), (2, 1)])
        self.start(both, pairs, lambda array, keep: self.totals.append((added(keep, array), done)), both)

    def outer_start(self, chunk, total):
        inward, outward = both_cores([(0, 1), (3, 2)]), both_cores([(1, 0), (2, 3)])
        chip = lax.axis_index("dp") // 2
        outer = (chip == 0) | (chip == 3)

        def inner_sum(array, own):
            self.sums.append((added(own, array), chunk[1]))

        def result(array, own):
            total[1](jnp.where(outer, array, own))

        if chunk and total and chunk[0].shape == total[0].shape:
            def land(array, keep):
                inner_sum(array, keep[0])
                result(array, keep[1])

            value = jnp.where(outer, chunk[0], total[0])
            self.start(value, inward + outward, land, (chunk[0], total[0]))
        else:
            if total:
                self.start(total[0], outward, result, total[0])
            if chunk:
                self.start(chunk[0], inward, inner_sum, chunk[0])

    def finish(self):
        while self.chunks or self.sums or self.totals or self.flying:
            self.pulse()

    def pulse(self, *gate):
        most = 1 if self.chunks else 4
        return self.step(*gate, inner=most * (self.clock % 2), outer=most * (1 - self.clock % 2))


class LineSum:
    def __init__(self, relay, axis):
        self.relay, self.axis, self.count = relay, axis, 0
        self.totals, self.result = {}, None

    def add(self, other, mine, ends):
        half = added(mine, lax.ppermute(other, "dp", core_swap()))
        for chunk in jnp.split(half, ends, axis=self.axis):
            self.relay.chunks.append((chunk, partial(self.landed, self.count)))
            self.count += 1

    def landed(self, index, total):
        self.totals[index] = total
        if len(self.totals) == self.count:
            mine = jnp.concatenate([self.totals[i] for i in range(self.count)], axis=self.axis)
            self.relay.start(mine, core_swap(), self.join, mine)

    def join(self, other, mine):
        core = lax.axis_index("dp") % 2
        low, high = jnp.where(core == 0, mine, other), jnp.where(core == 0, other, mine)
        self.result = jnp.concatenate([low, high], axis=0).astype(f32)
        self.relay.joined.append(self)


def summed_by_compiler(part):
    count, rows = lax.axis_size("dp"), part.shape[0]
    part = jnp.pad(part, ((0, -rows % count), (0, 0)))
    own = lax.psum_scatter(part, "dp", scatter_dimension=0, tiled=True)
    return lax.all_gather(own, "dp", axis=0, tiled=True)[:rows].astype(f32)


def per_device(
    tokens,
    cotangent,
    image_kind,
    norm_one_gain,
    norm_one_bias,
    qkv_weight,
    qkv_bias,
    rotary_freq,
    proj_weight,
    proj_bias,
    norm_two_gain,
    norm_two_bias,
    up_weight,
    up_bias,
    down_weight,
    down_bias,
):
    sections = lax.axis_size("section")
    section = lax.axis_index("section")
    last = sections - 1
    by_line = lax.axis_size("dp") == 8
    scal = section.astype(jnp.int32).reshape(1)
    core = (lax.axis_index("dp") % 2).astype(jnp.int32).reshape(1)
    low = core[0] == 0
    common = tables(image_kind, rotary_freq)
    weights = (qkv_weight[0], proj_weight[0], up_weight[0], down_weight[0])
    vecs = (
        norm_one_gain, norm_one_bias, qkv_bias, proj_bias, norm_two_gain, norm_two_bias, up_bias, down_bias,
    )
    first_in = gathered(tokens, 0, sections)
    live_rows = live_rows_of(image_kind)
    last_in = gathered(cotangent, last, sections)
    last_in = jnp.where(live_rows > 0, last_in, bf16(0.0))

    def turn(layer, micro):
        return jnp.array([layer, micro], jnp.int32)

    states = None
    values = [first_in[m * ROWS : (m + 1) * ROWS] for m in range(MICRO)]
    backs, out_grads = None, None
    for layer in range(sections):
        for micro in range(MICRO):
            earlier = tokens
            if layer == last and micro == 1:
                fronts = dict(zip(STATES, states))
                turned, backs = back_call(scal, turn(last, 0), grads[0], common, weights, vecs, fronts, None)
                earlier = turned
            out, states = front_call(scal, turn(layer, micro), values[micro], common, weights, vecs, states, earlier)
            values[micro] = send(out, layer, layer + 1) if layer < last else out
        if layer == 1:
            values[0], last_in = lax.optimization_barrier((values[0], last_in))
            grads = [last_in[m * ROWS : (m + 1) * ROWS] for m in range(MICRO)]
            out_grads = list(grads)
    fronts = dict(zip(STATES, states))
    relay = Relay()
    sums = [LineSum(relay, axis) for axis in (1, 0, 1, 0)]
    plain = [[], [], [], []]

    def to_sum(index, other, mine, ends):
        if by_line:
            sums[index].add(other, mine, ends)
        else:
            plain[index].append((jnp.where(low, mine, other), jnp.where(low, other, mine)))

    for layer in reversed(range(sections)):
        if 0 < layer < last:
            out_grads = [jnp.where(section == layer, new, old) for new, old in zip(grads, out_grads)]
        if layer == 0:
            received = grads[0]
        for micro in range(MICRO):
            end = layer == 0 and micro == MICRO - 1
            if end:
                grads[0], grads[1], out_grads = lax.optimization_barrier((grads[0], grads[1], out_grads))
                out_grads = [jnp.where(section == 0, new, old) for new, old in zip((received, grads[1]), out_grads)]
                all_grads = jnp.concatenate(out_grads, axis=0)
                for offset in (0, 768):
                    other, mine, b_down = product_call(core, fronts["g"], all_grads, offset, 768)
                    to_sum(3, other, mine, [384])
                grads[1] = relay.step(grads[1], outer=2)
            if layer == last and micro == 0:
                dx = turned
            else:
                dx, backs = back_call(scal, turn(layer, micro), grads[micro], common, weights, vecs, fronts, backs)
            if end:
                values[0], values[1], dx, backs = relay.step(*values, dx, backs, outer=1, inner=1, age=1)
            grads[micro] = send(dx, layer, layer - 1) if layer > 0 else dx
    backs = dict(zip(BACKS, backs))
    other, mine, b_up = product_call(core, fronts["c"], backs["du"], 0, WIDTH // 2)
    to_sum(2, other, mine, [768, 1536, 2304])
    final = jnp.where(live_rows > 0, jnp.concatenate(values, axis=0), bf16(0.0))
    block_out = handed_out(final, last, sections)
    grad_tokens = handed_out(jnp.concatenate(grads, axis=0), 0, sections)
    b_up, block_out, grad_tokens, dqkv = relay.step(
        b_up, block_out, grad_tokens, backs["dqkv"], outer=1, inner=1, age=1
    )
    other, mine, b_qkv = product_call(core, fronts["a"], dqkv, 0, WIDTH // 2)
    to_sum(0, other, mine, [768, 1536])
    b_qkv, dz, small = relay.step(b_qkv, backs["dz"], backs["small"], outer=1, inner=1, age=1)
    other, mine, b_proj = product_call(core, fronts["o"], dz, 0, WIDTH // 2)
    lows, highs = small_call(small, b_qkv, b_proj, b_up, b_down)
    mine = jnp.concatenate([mine, jnp.where(low, lows, highs)], axis=0)
    other = jnp.concatenate([other, jnp.where(low, highs, lows)], axis=0)
    mine, other = relay.step(mine, other, outer=1, inner=1, age=1)
    to_sum(1, other, mine, [])
    relay.clock += relay.clock % 2
    relay.finish()
    if by_line:
        grad_qkv, grad_proj, grad_up, grad_down = (item.result for item in sums)
    else:
        grad_qkv, grad_proj, grad_up, grad_down = (
            summed_by_compiler(jnp.concatenate([part[side] for side in range(2) for part in parts], axis=0))
            for parts in plain
        )
    middle, half = WIDTH // 2, SMALL_ROWS // 2
    small = jnp.concatenate([grad_proj[middle : middle + half], grad_proj[middle + half + middle :]], axis=0)
    grad_proj = jnp.concatenate([grad_proj[:middle], grad_proj[middle + half : middle + half + middle]], axis=0)
    turns = small[5:7].reshape(2, HEADS, 2, 32)
    freq = (turns[:, :, 1] - turns[:, :, 0]).reshape(1, WIDTH)
    g_one, b_one, b_proj, g_two, b_two, b_down = (small[i : i + 1] for i in (0, 1, 7, 8, 9, 14))
    b_qkv, b_up = small[2:5].reshape(1, -1), small[10:14].reshape(1, -1)
    return (
        block_out, grad_tokens.astype(f32), g_one, b_one, grad_qkv[None], b_qkv, freq,
        grad_proj[None], b_proj, g_two, b_two, grad_up[None], b_up, grad_down[None], b_down,
    )


def solution(mesh):
    row = P(("dp", "section"), None)
    vector = P("section", None)
    matrix = P("section", None, None)
    params = (
        vector, vector, matrix, vector, vector, matrix, vector, vector, vector, matrix, vector, matrix, vector,
    )
    return jax.shard_map(
        per_device,
        mesh=mesh,
        in_specs=(row, row, P("dp")) + params,
        out_specs=(row, row) + params,
        check_vma=False,
    )
```

```python
from functools import partial
import math

import jax
import jax.numpy as jnp
import numpy as np
from jax import lax
from jax.experimental import pallas as pl
from jax.experimental.pallas import tpu as pltpu
from jax.sharding import PartitionSpec as P

HEADS = 12
SIDE_LARGE = 20
SIDE_MID = 16
SIDE_SMALL = 14
MICRO = 2
ROWS = 400
KEYS = 512
WIDTH = 768
HIDDEN = 3072
PAIRS = HEADS // 2
EPSILON = 1e-06
MASKED = -1e30
LOG2E = math.log2(math.e)
LN2 = math.log(2.0)
GELU_ONE = math.sqrt(2.0 / math.pi)
GELU_TWO = GELU_ONE * 0.044715

f32 = jnp.float32
bf16 = jnp.bfloat16
NT = (((1,), (1,)), ((), ()))
TN = (((0,), (0,)), ((), ()))

VEC_SIZES = (WIDTH, WIDTH, 3 * WIDTH, WIDTH, WIDTH, WIDTH, HIDDEN, WIDTH)
VEC_AT = tuple(int(v) for v in np.cumsum((0,) + VEC_SIZES))


def vec_part(vec_ref, index):
    return vec_ref[:, VEC_AT[index] : VEC_AT[index + 1]]


def swap_halves(values):
    lane = lax.broadcasted_iota(jnp.int32, values.shape, 1) % 64
    width = values.shape[1]
    return jnp.where(lane < 32, pltpu.roll(values, width - 32, 1), pltpu.roll(values, 32, 1))


def norm_parts(values):
    center = values - jnp.mean(values, axis=-1, keepdims=True)
    inverse = lax.rsqrt(jnp.mean(center * center, axis=-1, keepdims=True) + EPSILON)
    return center * inverse, inverse


def gelu_parts(pre):
    low = pre.astype(bf16)
    square = low * low
    tanh = jnp.tanh(low * (bf16(GELU_ONE) + bf16(GELU_TWO) * square))
    half = bf16(0.5) + bf16(0.5) * tanh
    value = low * half
    slope = half + (value - value * half) * (bf16(2 * GELU_ONE) + bf16(6 * GELU_TWO) * square)
    return value, slope


class Copies:
    def __init__(self, sems):
        self.sems = sems
        self.open = []
        self.used = 0

    def start(self, source, target):
        copy = pltpu.make_async_copy(source, target, self.sems.at[self.used])
        self.used += 1
        copy.start()
        self.open.append(copy)
        return copy

    def wait(self, *copies):
        for copy in copies:
            self.open = [other for other in self.open if other is not copy]
            copy.wait()

    def finish(self):
        self.wait(*list(self.open))


STATE_SHAPES = (
    ("x", (ROWS, WIDTH), bf16),
    ("a", (ROWS, WIDTH), bf16),
    ("qkv", (ROWS, 3 * WIDTH), bf16),
    ("e", (HEADS, ROWS, KEYS), bf16),
    ("linv", (ROWS, WIDTH), f32),
    ("o", (ROWS, WIDTH), bf16),
    ("n2", (ROWS, WIDTH), bf16),
    ("r2", (ROWS, 128), f32),
    ("c", (ROWS, WIDTH), bf16),
    ("g", (ROWS, HIDDEN), bf16),
    ("gp", (ROWS, HIDDEN), bf16),
)
STATES = tuple(name for name, _, _ in STATE_SHAPES)


def front_kernel(first, scal, layer, *refs):
    x_in, geo_in, cos_in, sin_in, wqkv_in, wp_in, wu_in, wd_in = refs[:8]
    vec_in, rest = refs[8:16], refs[17:]
    if not first:
        rest = rest[len(STATES) :]
    out_ref = rest[0]
    state = dict(zip(STATES, rest[1 : 1 + len(STATES)]))
    (
        x_v, vec_v, geo_v, cos_v, sin_v, wqkv_v, wp_v, wu_v, wd_v,
        a_v, qkv_v, e_v, s_v, li_v, o_v, m_v, n2_v, r2_v, c_v, g_v, gp_v, qcode_v, kcode_v, out_v, sems,
    ) = rest[1 + len(STATES) :]

    @pl.when(scal[0] == layer[0])
    def _():
        slot = layer[1]
        copies = Copies(sems)
        wait = copies.wait
        get_x = copies.start(x_in, x_v)
        get_vec = [
            copies.start(part, vec_v.at[:, pl.ds(at, size)]) for part, at, size in zip(vec_in, VEC_AT, VEC_SIZES)
        ]
        get_geo = copies.start(geo_in.at[slot], geo_v)
        get_qkv = [copies.start(wqkv_in.at[:, pl.ds(0, WIDTH)], wqkv_v.at[:, pl.ds(0, WIDTH)])]

        def put(source, name):
            copies.start(source, state[name].at[slot])

        qkv_v[ROWS:KEYS, :] = jnp.zeros((KEYS - ROWS, 3 * WIDTH), bf16)
        wait(get_x, *get_vec)
        get_cos = copies.start(cos_in.at[slot], cos_v)
        get_sin = copies.start(sin_in.at[slot], sin_v)
        for at in (WIDTH, 2 * WIDTH):
            get_qkv.append(copies.start(wqkv_in.at[:, pl.ds(at, WIDTH)], wqkv_v.at[:, pl.ds(at, WIDTH)]))
        normed, _ = norm_parts(x_v[...].astype(f32))
        a_v[...] = (normed * vec_part(vec_v, 0) + vec_part(vec_v, 1)).astype(bf16)
        wait(get_geo)
        segment = geo_v[:, 2:3]
        code = (lax.broadcasted_iota(jnp.int32, (KEYS, 128), 1) % 64).astype(f32)
        qcode_v[...] = jnp.where(segment[:ROWS] == code[:ROWS], 1.0, 0.0).astype(bf16)
        kcode_v[...] = jnp.where((segment != code) & (code < 4), MASKED, 0.0).astype(bf16)
        for part in range(3):
            at = part * WIDTH
            wait(get_qkv[part])
            if part == 0:
                wait(get_cos, get_sin)
                get_wp = copies.start(wp_in, wp_v)
                get_wu = copies.start(wu_in, wu_v)
                get_wd = copies.start(wd_in, wd_v)
            acc = jnp.dot(a_v[...], wqkv_v[:, at : at + WIDTH], preferred_element_type=f32)
            acc = acc + vec_v[:, VEC_AT[2] + at : VEC_AT[2] + at + WIDTH]
            if part < 2:
                acc = acc * cos_v[...] + swap_halves(acc) * sin_v[...]
            if part == 0:
                acc = acc * (LOG2E / 8.0)
            qkv_v[:ROWS, at : at + WIDTH] = acc.astype(bf16)

        lane_q = lax.broadcasted_iota(jnp.int32, (ROWS, 128), 1) // 64
        lane_k = lax.broadcasted_iota(jnp.int32, (KEYS, 128), 1) // 64

        def scores(index):
            pair, head = divmod(index, 2)
            q_one = jnp.where(lane_q == head, qkv_v[:ROWS, pair * 128 : pair * 128 + 128], qcode_v[...])
            k_at = WIDTH + pair * 128
            k_one = jnp.where(lane_k == head, qkv_v[:, k_at : k_at + 128], kcode_v[...])
            s_v[index % 4] = lax.dot_general(q_one, k_one, NT, preferred_element_type=f32)

        scores(0)
        sums = []
        for index in range(HEADS):
            pair, head = divmod(index, 2)
            if index + 1 < HEADS:
                scores(index + 1)
            v_at = 2 * WIDTH + pair * 128
            v_one = jnp.where(lane_k == head, qkv_v[:, v_at : v_at + 128], bf16(1.0))
            peak = jnp.max(s_v[index % 4], axis=1, keepdims=True)
            e_v[index] = jnp.exp2(s_v[index % 4] - peak).astype(bf16)
            sums.append(jnp.dot(e_v[index], v_one, preferred_element_type=f32))
            if head == 1:
                lanes = pl.ds(pair * 128, 128)
                inverse = 1.0 / pltpu.roll(jnp.where(lane_q == 0, sums[index], sums[index - 1]), 64, 1)
                li_v[:, lanes] = inverse
                o_v[:, lanes] = (jnp.where(lane_q == 0, sums[index - 1], sums[index]) * inverse).astype(bf16)
        put(x_v, "x")
        put(a_v, "a")
        put(qkv_v.at[pl.ds(0, ROWS)], "qkv")
        put(e_v, "e")
        put(li_v, "linv")
        put(o_v, "o")
        wait(get_wp)
        middle = (
            x_v[...].astype(f32)
            + jnp.dot(o_v[...], wp_v[...], preferred_element_type=f32)
            + vec_part(vec_v, 3)
        )
        m_v[...] = middle
        normed, inverse = norm_parts(middle)
        n2_v[...] = normed.astype(bf16)
        r2_v[...] = jnp.broadcast_to(inverse, (ROWS, 128))
        c_v[...] = (normed * vec_part(vec_v, 4) + vec_part(vec_v, 5)).astype(bf16)
        put(n2_v, "n2")
        put(r2_v, "r2")
        put(c_v, "c")
        wait(get_wu)
        chunk = 1024

        def up_step(step, carry):
            lanes = pl.ds(pl.multiple_of(step * chunk, chunk), chunk)
            blanes = pl.ds(pl.multiple_of(step * chunk + VEC_AT[6], 128), chunk)
            pre = jnp.dot(c_v[...], wu_v[:, lanes], preferred_element_type=f32) + vec_v[:, blanes]
            value, slope = gelu_parts(pre)
            g_v[:, lanes] = value
            gp_v[:, lanes] = slope
            return carry

        lax.fori_loop(0, HIDDEN // chunk, up_step, 0)
        put(gp_v, "gp")
        put(g_v, "g")
        wait(get_wd)
        for at in range(0, WIDTH, 256):
            part = pl.ds(at, 256)
            out = jnp.dot(g_v[...], wd_v[:, part], preferred_element_type=f32)
            out = out + m_v[:, part] + vec_v[:, VEC_AT[7] + at : VEC_AT[7] + at + 256]
            out_v[:, part] = out.astype(bf16)
            copies.start(out_v.at[:, part], out_ref.at[:, part])
        copies.finish()


ANY = pl.BlockSpec(memory_space=pl.ANY)
VMEM_LIMIT = 60 * 2**20


def vmem(*shape, dtype=bf16):
    return pltpu.VMEM(shape, dtype)


def call_states(kernel, first, operands, smem, states, plain_out, shapes, scratch, name):
    count = len(operands)
    state_out = [jax.ShapeDtypeStruct((MICRO,) + shape, dtype) for _, shape, dtype in shapes]
    operands = list(operands) + ([] if first else list(states))
    results = pl.pallas_call(
        partial(kernel, first),
        out_shape=list(plain_out) + state_out,
        in_specs=[pl.BlockSpec(memory_space=pltpu.SMEM)] * smem + [ANY] * (len(operands) - smem),
        out_specs=[ANY] * (len(plain_out) + len(shapes)),
        scratch_shapes=scratch,
        input_output_aliases={} if first else {count + i: len(plain_out) + i for i in range(len(shapes))},
        compiler_params=pltpu.CompilerParams(vmem_limit_bytes=VMEM_LIMIT),
        name=name,
    )(*operands)
    return results[0], tuple(results[1:])


def front_call(scal, layer, x, common, weights, vecs, states, earlier):
    scratch = [
        vmem(ROWS, WIDTH), vmem(1, VEC_AT[-1], dtype=f32), vmem(KEYS, 128, dtype=f32),
        vmem(ROWS, WIDTH, dtype=f32), vmem(ROWS, WIDTH, dtype=f32),
        vmem(WIDTH, 3 * WIDTH), vmem(WIDTH, WIDTH), vmem(WIDTH, HIDDEN), vmem(HIDDEN, WIDTH),
        vmem(ROWS, WIDTH), vmem(KEYS, 3 * WIDTH), vmem(HEADS, ROWS, KEYS), vmem(4, ROWS, KEYS, dtype=f32),
        vmem(ROWS, WIDTH, dtype=f32), vmem(ROWS, WIDTH), vmem(ROWS, WIDTH, dtype=f32),
        vmem(ROWS, WIDTH), vmem(ROWS, 128, dtype=f32), vmem(ROWS, WIDTH),
        vmem(ROWS, HIDDEN), vmem(ROWS, HIDDEN), vmem(ROWS, 128), vmem(KEYS, 128), vmem(ROWS, WIDTH),
        pltpu.SemaphoreType.DMA((36,)),
    ]
    operands = [scal, layer, x, *common, *weights, *vecs, earlier]
    out = jax.ShapeDtypeStruct((ROWS, WIDTH), bf16)
    return call_states(front_kernel, states is None, operands, 2, states, [out], STATE_SHAPES, scratch, "layer_front")


BACK_SHAPES = (
    ("du", (ROWS, HIDDEN), bf16),
    ("dz", (ROWS, WIDTH), bf16),
    ("dqkv", (ROWS, 3 * WIDTH), bf16),
    ("small", (8, WIDTH), f32),
)
BACKS = tuple(name for name, _, _ in BACK_SHAPES)


def back_kernel(first, scal, layer, *refs):
    dy_in, geo_in, cos_in, sin_in, wqkv_in, wp_in, wu_in, wd_in, gain_one_in, gain_two_in = refs[:10]
    saved = dict(zip(KEPT, refs[10 : 10 + len(KEPT)]))
    rest = refs[10 + len(KEPT) :]
    if not first:
        rest = rest[len(BACKS) :]
    dx_ref = rest[0]
    state = dict(zip(BACKS, rest[1 : 1 + len(BACKS)]))
    (
        dy_v, geo_v, cos_v, sin_v, wqkv_v, wp_v, wu_v, wd_v, gains_v,
        gp_v, n2_v, r2_v, li_v, qkv_v, e_v, o_v, x_v,
        du_v, dz_v, dm_v, dop_v, qt_v, dot_v, dq_v, dkt_v, dvt_v, dqkv_v, small_v, dx_v, sems,
    ) = rest[1 + len(BACKS) :]

    @pl.when(scal[0] == layer[0])
    def _():
        slot = layer[1]
        copies = Copies(sems)
        wait = copies.wait
        chunk = 1024
        steps = HIDDEN // chunk
        get_dy = copies.start(dy_in, dy_v)
        get_wd, get_gp = [], []
        for step in range(steps):
            part = pl.ds(step * chunk, chunk)
            get_wd.append(copies.start(wd_in.at[part], wd_v.at[part]))
            get_gp.append(copies.start(saved["gp"].at[slot, :, part], gp_v.at[:, part]))
        get_wu = copies.start(wu_in, wu_v)
        get_norm = [
            copies.start(saved["n2"].at[slot], n2_v),
            copies.start(saved["r2"].at[slot], r2_v),
            copies.start(gain_one_in, gains_v.at[pl.ds(0, 1)]),
            copies.start(gain_two_in, gains_v.at[pl.ds(8, 1)]),
        ]

        def put(source, name):
            copies.start(source, state[name].at[slot])

        qkv_v[ROWS:KEYS, :] = jnp.zeros((KEYS - ROWS, 3 * WIDTH), bf16)
        wait(get_dy)
        for step in range(steps):
            part = slice(step * chunk, (step + 1) * chunk)
            wait(get_wd[step], get_gp[step])
            act = lax.dot_general(dy_v[...], wd_v[part, :], NT, preferred_element_type=f32)
            du_v[:, part] = act.astype(bf16) * gp_v[:, part]
        get_wp = copies.start(wp_in, wp_v)
        get_li = copies.start(saved["linv"].at[slot], li_v)
        get_qkv = copies.start(saved["qkv"].at[slot], qkv_v.at[pl.ds(0, ROWS)])
        get_o = copies.start(saved["o"].at[slot], o_v)
        get_e = copies.start(saved["e"].at[slot], e_v)
        get_turn = [
            copies.start(cos_in.at[slot], cos_v),
            copies.start(sin_in.at[slot], sin_v),
            copies.start(geo_in.at[slot], geo_v),
        ]
        get_x = copies.start(saved["x"].at[slot], x_v)
        get_wqkv = copies.start(wqkv_in, wqkv_v)
        put(du_v, "du")
        wait(get_wu)
        dc = lax.dot_general(du_v[...], wu_v[...], NT, preferred_element_type=f32)
        wait(*get_norm)
        normed = n2_v[...].astype(f32)
        small_v[0:1, :] = jnp.sum(dc * normed, axis=0, keepdims=True)
        small_v[1:2, :] = jnp.sum(dc, axis=0, keepdims=True)
        hat = dc * gains_v[8:9, :]
        dm = dy_v[...].astype(f32) + r2_v[:, 0:1] * (
            hat
            - jnp.mean(hat, axis=-1, keepdims=True)
            - normed * jnp.mean(hat * normed, axis=-1, keepdims=True)
        )
        dm_v[...] = dm
        dz_v[...] = dm.astype(bf16)
        put(dz_v, "dz")
        wait(get_wp, get_li)
        do = lax.dot_general(dz_v[...], wp_v[...], NT, preferred_element_type=f32)
        dop_v[...] = (do * li_v[...]).astype(bf16)
        dot_v[...] = dop_v[...].T
        wait(get_qkv)
        qt_v[...] = qkv_v[:ROWS, :WIDTH].T
        wait(get_o, get_e)

        def pair_step(step, carry):
            for pair in [step * 2 + i for i in range(2)]:
                lanes = pl.ds(pl.multiple_of(pair * 128, 128), 128)
                klanes = pl.ds(pl.multiple_of(pair * 128 + WIDTH, 128), 128)
                vlanes = pl.ds(pl.multiple_of(pair * 128 + 2 * WIDTH, 128), 128)
                do_two = dop_v[:, lanes]
                k_two = qkv_v[:, klanes]
                v_two = qkv_v[:, vlanes]
                prod = do_two.astype(f32) * o_v[:, lanes].astype(f32)
                lane = lax.broadcasted_iota(jnp.int32, (ROWS, 128), 1) // 64
                dqs = []
                for head in range(2):
                    rows = pl.ds(pl.multiple_of(pair * 128 + head * 64, 64), 64)
                    do_one = jnp.where(lane == head, do_two, bf16(0.0))
                    dp = lax.dot_general(do_one, v_two, NT, preferred_element_type=f32)
                    delta = jnp.sum(jnp.where(lane == head, prod, 0.0), axis=1, keepdims=True)
                    probs = e_v[2 * pair + head]
                    ds = probs * (dp - delta).astype(bf16)
                    dqs.append(jnp.dot(ds, k_two, preferred_element_type=f32))
                    dkt_v[rows, :] = jnp.dot(qt_v[rows, :], ds, preferred_element_type=f32)
                    dvt_v[rows, :] = jnp.dot(dot_v[rows, :], probs, preferred_element_type=f32).astype(bf16)
                dq_v[:, lanes] = jnp.where(lane == 0, dqs[0], dqs[1])
            return carry

        lax.fori_loop(0, PAIRS // 2, pair_step, 0)
        wait(*get_turn)
        dqkv_v[:, 2 * WIDTH :] = dvt_v[...].T[:ROWS]
        dk = dkt_v[...].T[:ROWS]
        dq = dq_v[...]
        turn = dq * swap_halves(qkv_v[:ROWS, :WIDTH].astype(f32)) + dk * swap_halves(
            qkv_v[:ROWS, WIDTH : 2 * WIDTH].astype(f32)
        )
        small_v[4:5, :] = LN2 * jnp.sum(turn * geo_v[:ROWS, 0:1], axis=0, keepdims=True)
        small_v[5:6, :] = LN2 * jnp.sum(turn * geo_v[:ROWS, 1:2], axis=0, keepdims=True)
        dqkv_v[:, :WIDTH] = (0.125 * (dq * cos_v[...] - swap_halves(dq) * sin_v[...])).astype(bf16)
        dqkv_v[:, WIDTH : 2 * WIDTH] = (LN2 * (dk * cos_v[...] - swap_halves(dk) * sin_v[...])).astype(bf16)
        put(dqkv_v, "dqkv")
        wait(get_x)
        normed, inverse = norm_parts(x_v[...].astype(f32))
        wait(get_wqkv)
        da = lax.dot_general(dqkv_v[...], wqkv_v[...], NT, preferred_element_type=f32)
        small_v[2:3, :] = jnp.sum(da * normed, axis=0, keepdims=True)
        small_v[3:4, :] = jnp.sum(da, axis=0, keepdims=True)
        put(small_v, "small")
        hat = da * gains_v[0:1, :]
        dx = dm_v[...] + inverse * (
            hat
            - jnp.mean(hat, axis=-1, keepdims=True)
            - normed * jnp.mean(hat * normed, axis=-1, keepdims=True)
        )
        dx_v[...] = dx.astype(bf16)
        copies.start(dx_v, dx_ref)
        copies.finish()


KEPT = ("gp", "n2", "r2", "linv", "qkv", "e", "o", "x")


def back_call(scal, layer, dy, common, weights, vecs, fronts, backs):
    scratch = [
        vmem(ROWS, WIDTH), vmem(KEYS, 128, dtype=f32), vmem(ROWS, WIDTH, dtype=f32), vmem(ROWS, WIDTH, dtype=f32),
        vmem(WIDTH, 3 * WIDTH), vmem(WIDTH, WIDTH), vmem(WIDTH, HIDDEN), vmem(HIDDEN, WIDTH), vmem(16, WIDTH, dtype=f32),
        vmem(ROWS, HIDDEN), vmem(ROWS, WIDTH), vmem(ROWS, 128, dtype=f32), vmem(ROWS, WIDTH, dtype=f32),
        vmem(KEYS, 3 * WIDTH), vmem(HEADS, ROWS, KEYS), vmem(ROWS, WIDTH), vmem(ROWS, WIDTH),
        vmem(ROWS, HIDDEN), vmem(ROWS, WIDTH), vmem(ROWS, WIDTH, dtype=f32), vmem(ROWS, WIDTH),
        vmem(WIDTH, ROWS), vmem(WIDTH, ROWS), vmem(ROWS, WIDTH, dtype=f32),
        vmem(WIDTH, KEYS, dtype=f32), vmem(WIDTH, KEYS), vmem(ROWS, 3 * WIDTH), vmem(8, WIDTH, dtype=f32), vmem(ROWS, WIDTH),
        pltpu.SemaphoreType.DMA((36,)),
    ]
    operands = [scal, layer, dy, *common, *weights, vecs[0], vecs[4], *(fronts[name] for name in KEPT)]
    out = jax.ShapeDtypeStruct((ROWS, WIDTH), bf16)
    return call_states(back_kernel, backs is None, operands, 2, backs, [out], BACK_SHAPES, scratch, "layer_back")


def side_of(kind):
    return jnp.where(kind == 0, float(SIDE_LARGE), jnp.where(kind == 1, float(SIDE_MID), float(SIDE_SMALL)))


def places(kind, rows):
    side = side_of(kind)
    area = side * side
    images = jnp.where(kind == 2, 2.0, 1.0)
    image = (rows >= area).astype(f32) + (rows >= 2 * area).astype(f32)
    live = (image < images) & (rows < ROWS)
    local = rows - image * area
    patch_row = jnp.floor((local + 0.5) / side)
    patch_col = local - patch_row * side
    zero = jnp.zeros_like(rows)
    segment = jnp.where(live, image, jnp.where(rows < ROWS, 3.0, 2.0))
    return jnp.where(live, patch_row, zero), jnp.where(live, patch_col, zero), segment, live


def split_low(values):
    high = values.astype(bf16)
    return jnp.concatenate([high, (values - high.astype(f32)).astype(bf16)], axis=0)


def tables_kernel(kind_ref, freq_in, geo_ref, cos_ref, sin_ref, freq_v, geo_v, cos_v, sin_v, sems):
    copies = Copies(sems)
    copies.wait(copies.start(freq_in, freq_v))
    step = lax.broadcasted_iota(jnp.int32, (32, WIDTH // 2), 0).astype(f32)
    angles = [step * freq_v[:, at : at + WIDTH // 2] for at in (0, WIDTH // 2)]
    waves = [split_low(jnp.concatenate([jnp.cos(angle), jnp.sin(angle)], axis=1)) for angle in angles]
    sixteen = lax.broadcasted_iota(jnp.int32, (ROWS, 64), 1) % 32
    for micro in range(MICRO):
        rows = lax.broadcasted_iota(jnp.int32, (KEYS, 128), 0).astype(f32)
        lane = lax.broadcasted_iota(jnp.int32, (KEYS, 128), 1)
        patch_row, patch_col, segment, _ = places(kind_ref[micro], rows)
        geo_v[micro] = jnp.where(lane == 0, patch_row, jnp.where(lane == 1, patch_col, segment))
        picks = [
            jnp.where(sixteen.astype(f32) == patch[:ROWS, :64], 1.0, 0.0).astype(bf16)
            for patch in (patch_row, patch_col)
        ]
        row_wave, col_wave = (
            jnp.dot(pick, wave, preferred_element_type=f32) for pick, wave in zip(picks, waves)
        )
        half = WIDTH // 2
        row_cos, row_sin = row_wave[:, :half], row_wave[:, half:]
        col_cos, col_sin = col_wave[:, :half], col_wave[:, half:]
        cosine = row_cos * col_cos - row_sin * col_sin
        sine = row_sin * col_cos + row_cos * col_sin
        lane = lax.broadcasted_iota(jnp.int32, (ROWS, 128), 1)
        for part in range(half // 128):
            for pair in range(2):
                at = (2 * part + pair) * 128
                cos_v[micro, :, at : at + 128] = spread(cosine[:, part * 128 : part * 128 + 128], pair, lane)
                values = spread(sine[:, part * 128 : part * 128 + 128], pair, lane)
                sin_v[micro, :, at : at + 128] = jnp.where(lane % 64 < 32, -values, values)
        copies.start(geo_v.at[micro], geo_ref.at[micro])
        copies.start(cos_v.at[micro], cos_ref.at[micro])
        copies.start(sin_v.at[micro], sin_ref.at[micro])
    copies.finish()


def spread(values, pair, lane):
    base = values if pair == 0 else pltpu.roll(values, 64, 1)
    by_one = pltpu.roll(base, 32, 1)
    by_two = pltpu.roll(base, 64, 1)
    return jnp.where(lane < 32, base, jnp.where(lane < 96, by_one, by_two))


def tables(kinds, frequency):
    shapes = [(MICRO, KEYS, 128), (MICRO, ROWS, WIDTH), (MICRO, ROWS, WIDTH)]
    return pl.pallas_call(
        tables_kernel,
        out_shape=[jax.ShapeDtypeStruct(shape, f32) for shape in shapes],
        in_specs=[pl.BlockSpec(memory_space=pltpu.SMEM), ANY],
        out_specs=[ANY] * 3,
        scratch_shapes=[vmem(1, WIDTH, dtype=f32)]
        + [vmem(*shape, dtype=f32) for shape in shapes]
        + [pltpu.SemaphoreType.DMA((8,))],
        compiler_params=pltpu.CompilerParams(vmem_limit_bytes=VMEM_LIMIT),
        name="tables",
    )(kinds, frequency)


def live_rows_of(kinds):
    rows = jnp.broadcast_to(jnp.arange(ROWS, dtype=jnp.int32).astype(f32)[None, :], (MICRO, ROWS))
    return places(kinds[:, None], rows)[3].reshape(-1, 1)


def product_kernel(
    offset, block, core_ref, left_in, right_in, other_ref, own_ref, sums_ref,
    other_v, own_v, right_v, other_out, own_out, sums_out, sems,
):
    copies = Copies(sems)
    core = core_ref[0]
    half = left_in.shape[1] // 2
    rows = other_v.shape[1]
    get_right = copies.start(right_in, right_v)
    get_other = copies.start(left_in.at[:, pl.ds(pl.multiple_of((1 - core) * half + offset, 128), rows)], other_v)
    get_own = copies.start(left_in.at[:, pl.ds(pl.multiple_of(core * half + offset, 128), rows)], own_v)
    copies.wait(get_right)
    for get, part_v, part_out, ref in (
        (get_other, other_v, other_out, other_ref),
        (get_own, own_v, own_out, own_ref),
    ):
        copies.wait(get)

        for at in range(0, rows, block):
            lanes = pl.ds(at, block)
            part_out[lanes, :] = lax.dot_general(
                part_v[:, lanes], right_v[...], TN, preferred_element_type=f32
            ).astype(bf16)
            copies.start(part_out.at[lanes], ref.at[lanes])
    sums_out[...] = jnp.dot(jnp.ones((16, right_v.shape[0]), bf16), right_v[...], preferred_element_type=f32)[:8]
    copies.start(sums_out, sums_ref)
    copies.finish()


def product_call(core, left, right, offset, rows):
    left = left.reshape(MICRO * ROWS, left.shape[-1])
    right = right.reshape(MICRO * ROWS, right.shape[-1])
    count, width = right.shape
    block = 512 if rows % 512 == 0 else 384
    return pl.pallas_call(
        partial(product_kernel, offset, block),
        out_shape=[jax.ShapeDtypeStruct((rows, width), bf16)] * 2 + [jax.ShapeDtypeStruct((8, width), f32)],
        in_specs=[pl.BlockSpec(memory_space=pltpu.SMEM), ANY, ANY],
        out_specs=[ANY] * 3,
        scratch_shapes=[
            vmem(count, rows), vmem(count, rows), vmem(count, width), vmem(rows, width), vmem(rows, width),
            vmem(8, width, dtype=f32), pltpu.SemaphoreType.DMA((16,)),
        ],
        compiler_params=pltpu.CompilerParams(vmem_limit_bytes=VMEM_LIMIT),
        name="weight_grad",
    )(core, left, right)


SMALL_AT = (WIDTH, WIDTH, 3 * WIDTH, WIDTH, WIDTH, WIDTH, WIDTH, WIDTH, HIDDEN, WIDTH)
SMALL_ROWS = 32


def small_kernel(small_in, qkv_in, proj_in, up_in, down_in, low_ref, high_ref, *scratch):
    small_v, qkv_v, proj_v, up_v, down_v, rows_v, low_v, high_v, sems = scratch
    copies = Copies(sems)
    for source, target in ((small_in, small_v), (qkv_in, qkv_v), (proj_in, proj_v), (up_in, up_v), (down_in, down_v)):
        copies.start(source, target)
    copies.finish()
    rows_v[...] = jnp.zeros_like(rows_v)
    small = small_v[0] + small_v[1]
    parts = [small[2:3], small[3:4]]
    parts += [qkv_v[0:1, at : at + WIDTH] for at in range(0, 3 * WIDTH, WIDTH)]
    parts += [small[4:5], small[5:6], proj_v[0:1, :], small[0:1], small[1:2]]
    parts += [up_v[0:1, at : at + WIDTH] for at in range(0, HIDDEN, WIDTH)]
    parts += [down_v[0:1, :]]
    for index, part in enumerate(parts):
        rows_v[index : index + 1, :] = part
    half = SMALL_ROWS // 2
    low_v[...] = rows_v[:half, :].astype(bf16)
    high_v[...] = rows_v[half:, :].astype(bf16)
    copies.start(low_v, low_ref)
    copies.start(high_v, high_ref)
    copies.finish()


def small_call(small, qkv, proj, up, down):
    half = (SMALL_ROWS // 2, WIDTH)
    return pl.pallas_call(
        small_kernel,
        out_shape=[jax.ShapeDtypeStruct(half, bf16)] * 2,
        in_specs=[ANY] * 5,
        out_specs=[ANY] * 2,
        scratch_shapes=[
            vmem(MICRO, 8, WIDTH, dtype=f32), vmem(8, 3 * WIDTH, dtype=f32), vmem(8, WIDTH, dtype=f32),
            vmem(8, HIDDEN, dtype=f32), vmem(8, WIDTH, dtype=f32), vmem(SMALL_ROWS, WIDTH, dtype=f32),
            vmem(*half), vmem(*half), pltpu.SemaphoreType.DMA((8,)),
        ],
        name="small_grads",
    )(small, qkv, proj, up, down)


def send(value, source, target):
    return lax.ppermute(value, "section", [(source, target)])


def gathered(part, target, sections):
    pieces = [part if source == target else send(part, source, target) for source in range(sections)]
    return jnp.concatenate(pieces, axis=0)


def handed_out(output, grads, sections):
    section, last = lax.axis_index("section"), sections - 1
    share = output.shape[0] // sections

    def rows(whole, target):
        return whole[target * share : (target + 1) * share]

    output_share, grad_share = rows(output, last), rows(grads, 0)
    for target in range(last):
        mirror = last - target
        piece = jnp.where(section == last, rows(output, target), rows(grads, mirror))
        piece = lax.ppermute(piece, "section", [(last, target), (0, mirror)])
        output_share = jnp.where(section == target, piece, output_share)
        grad_share = jnp.where(section == mirror, piece, grad_share)
    return output_share, grad_share


def added(one, other):
    return (one.astype(f32) + other.astype(f32)).astype(bf16)


def both_cores(pairs):
    return [(2 * a + core, 2 * b + core) for a, b in pairs for core in range(2)]


def core_swap():
    return [(i, i ^ 1) for i in range(lax.axis_size("dp"))]


class Relay:
    def __init__(self):
        self.chunks, self.sums, self.totals = [], [], []
        self.flying, self.joined, self.clock = [], [], 0

    def start(self, value, pairs, then, keep, age, chunk=False):
        self.flying.append((self.clock + age, lax.ppermute(value, "dp", pairs), then, keep, chunk))

    def step(self, *gate, outer=0, inner=0, ahead=0):
        ready = [f for f in self.flying if f[0] <= self.clock + ahead]
        self.flying = [f for f in self.flying if f[0] > self.clock + ahead]
        fresh, self.chunks = self.chunks[:outer], self.chunks[outer:]
        arrays, keeps = [f[1] for f in ready], [f[3] for f in ready]
        new = [value for value, _ in fresh]
        joined, self.joined = self.joined, []
        results = [item.result for item in joined]
        arrays, keeps, new, gate, results = lax.optimization_barrier((arrays, keeps, new, gate, results))
        for item, result in zip(joined, results):
            item.result = result
        for (_, _, then, _, _), array, keep in zip(ready, arrays, keeps):
            then(array, keep)
        fresh = [(value, done) for value, (_, done) in zip(new, fresh)]
        for _ in range(outer):
            self.outer_start(fresh.pop(0) if fresh else None, self.totals.pop(0) if self.totals else None)
        for _ in range(min(inner, len(self.sums))):
            self.inner_start(*self.sums.pop(0))
        self.clock += 1
        return gate[0] if len(gate) == 1 else gate

    def inner_start(self, both, done):
        pairs = both_cores([(1, 2), (2, 1)])
        self.start(both, pairs, lambda array, keep: self.totals.append((added(keep, array), done)), both, 2)

    def outer_start(self, chunk, total):
        inward, outward = both_cores([(0, 1), (3, 2)]), both_cores([(1, 0), (2, 3)])
        chip = lax.axis_index("dp") // 2
        outer = (chip == 0) | (chip == 3)

        def inner_sum(array, own):
            self.sums.append((added(own, array), chunk[1]))

        def result(array, own):
            total[1](jnp.where(outer, array, own))

        if chunk and total and chunk[0].shape == total[0].shape:
            def land(array, keep):
                inner_sum(array, keep[0])
                result(array, keep[1])

            value = jnp.where(outer, chunk[0], total[0])
            self.start(value, inward + outward, land, (chunk[0], total[0]), 3, True)
        else:
            if total:
                self.start(total[0], outward, result, total[0], 3 if self.chunks or chunk else 8)
            if chunk:
                self.start(chunk[0], inward, inner_sum, chunk[0], 3, True)

    def finish(self):
        while self.chunks:
            self.pulse()
        while any(flight[0] > self.clock - 1 and flight[4] for flight in self.flying):
            self.step(outer=4, inner=4)
        while self.sums or self.totals or self.flying:
            self.step(outer=4, inner=4, ahead=9)

    def pulse(self, *gate):
        return self.step(*gate, inner=self.clock % 2, outer=1 - self.clock % 2)


class LineSum:
    def __init__(self, relay, axis):
        self.relay, self.axis, self.count = relay, axis, 0
        self.totals, self.result = {}, None

    def add(self, other, mine, ends):
        half = added(mine, lax.ppermute(other, "dp", core_swap()))
        for chunk in jnp.split(half, ends, axis=self.axis):
            self.relay.chunks.append((chunk, partial(self.landed, self.count)))
            self.count += 1

    def landed(self, index, total):
        self.totals[index] = total
        if len(self.totals) == self.count:
            mine = jnp.concatenate([self.totals[i] for i in range(self.count)], axis=self.axis)
            self.relay.start(mine, core_swap(), self.join, mine, 2)

    def join(self, other, mine):
        core = lax.axis_index("dp") % 2
        low, high = jnp.where(core == 0, mine, other), jnp.where(core == 0, other, mine)
        self.result = jnp.concatenate([low, high], axis=0).astype(f32)
        self.relay.joined.append(self)


def summed_by_compiler(part):
    count, rows = lax.axis_size("dp"), part.shape[0]
    part = jnp.pad(part, ((0, -rows % count), (0, 0)))
    own = lax.psum_scatter(part, "dp", scatter_dimension=0, tiled=True)
    return lax.all_gather(own, "dp", axis=0, tiled=True)[:rows].astype(f32)


def per_device(
    tokens,
    cotangent,
    image_kind,
    norm_one_gain,
    norm_one_bias,
    qkv_weight,
    qkv_bias,
    rotary_freq,
    proj_weight,
    proj_bias,
    norm_two_gain,
    norm_two_bias,
    up_weight,
    up_bias,
    down_weight,
    down_bias,
):
    sections = lax.axis_size("section")
    section = lax.axis_index("section")
    last = sections - 1
    by_line = lax.axis_size("dp") == 8
    scal = section.astype(jnp.int32).reshape(1)
    core = (lax.axis_index("dp") % 2).astype(jnp.int32).reshape(1)
    low = core[0] == 0
    common = tables(image_kind, rotary_freq)
    weights = (qkv_weight[0], proj_weight[0], up_weight[0], down_weight[0])
    vecs = (
        norm_one_gain, norm_one_bias, qkv_bias, proj_bias, norm_two_gain, norm_two_bias, up_bias, down_bias,
    )
    first_in = gathered(tokens, 0, sections)
    live_rows = live_rows_of(image_kind)
    last_in = gathered(cotangent, last, sections)
    last_in = jnp.where(live_rows > 0, last_in, bf16(0.0))

    def turn(layer, micro):
        return jnp.array([layer, micro], jnp.int32)

    states = None
    values = [first_in[m * ROWS : (m + 1) * ROWS] for m in range(MICRO)]
    backs, out_grads = None, None
    for layer in range(sections):
        for micro in range(MICRO):
            earlier = tokens
            if layer == last and micro == 1:
                fronts = dict(zip(STATES, states))
                turned, backs = back_call(scal, turn(last, 0), grads[0], common, weights, vecs, fronts, None)
                earlier = turned
            out, states = front_call(scal, turn(layer, micro), values[micro], common, weights, vecs, states, earlier)
            values[micro] = send(out, layer, layer + 1) if layer < last else out
        if layer == 1:
            values[0], last_in = lax.optimization_barrier((values[0], last_in))
            grads = [last_in[m * ROWS : (m + 1) * ROWS] for m in range(MICRO)]
            out_grads = list(grads)
    fronts = dict(zip(STATES, states))
    relay = Relay()
    sums = [LineSum(relay, axis) for axis in (1, 0, 1, 0)]
    plain = [[], [], [], []]

    def to_sum(index, other, mine, ends):
        if by_line:
            sums[index].add(other, mine, ends)
        else:
            plain[index].append((jnp.where(low, mine, other), jnp.where(low, other, mine)))

    for layer in reversed(range(sections)):
        if 0 < layer < last:
            out_grads = [jnp.where(section == layer, new, old) for new, old in zip(grads, out_grads)]
        if layer == 0:
            received = grads[0]
        for micro in range(MICRO):
            end = layer == 0 and micro == MICRO - 1
            if end:
                grads[0], grads[1], out_grads = lax.optimization_barrier((grads[0], grads[1], out_grads))
                out_grads = [jnp.where(section == 0, new, old) for new, old in zip((received, grads[1]), out_grads)]
                all_grads = jnp.concatenate(out_grads, axis=0)
                for offset in (0, 768):
                    other, mine, b_down = product_call(core, fronts["g"], all_grads, offset, 768)
                    to_sum(3, other, mine, [384])
                grads[1] = relay.step(grads[1], outer=2)
            if layer == last and micro == 0:
                dx = turned
            else:
                dx, backs = back_call(scal, turn(layer, micro), grads[micro], common, weights, vecs, fronts, backs)
            if end:
                values[0], values[1], dx, backs = relay.step(*values, dx, backs, outer=1, inner=1, ahead=9)
            grads[micro] = send(dx, layer, layer - 1) if layer > 0 else dx
    backs = dict(zip(BACKS, backs))
    other, mine, b_up = product_call(core, fronts["c"], backs["du"], 0, WIDTH // 2)
    to_sum(2, other, mine, [768, 1536, 2304])
    final = jnp.where(live_rows > 0, jnp.concatenate(values, axis=0), bf16(0.0))
    block_out, grad_tokens = handed_out(final, jnp.concatenate(grads, axis=0), sections)
    b_up, block_out, grad_tokens, dqkv = relay.step(
        b_up, block_out, grad_tokens, backs["dqkv"], outer=1, inner=1, ahead=9
    )
    other, mine, b_qkv = product_call(core, fronts["a"], dqkv, 0, WIDTH // 2)
    to_sum(0, other, mine, [768, 1536])
    other, mine, b_proj = product_call(core, fronts["o"], backs["dz"], 0, WIDTH // 2)
    lows, highs = small_call(backs["small"], b_qkv, b_proj, b_up, b_down)
    mine = jnp.concatenate([mine, jnp.where(low, lows, highs)], axis=0)
    other = jnp.concatenate([other, jnp.where(low, highs, lows)], axis=0)
    other, mine = relay.step(other, mine, outer=1, inner=1, ahead=9)
    to_sum(1, other, mine, [])
    relay.clock += relay.clock % 2
    relay.finish()
    if by_line:
        grad_qkv, grad_proj, grad_up, grad_down = (item.result for item in sums)
    else:
        grad_qkv, grad_proj, grad_up, grad_down = (
            summed_by_compiler(jnp.concatenate([part[side] for side in range(2) for part in parts], axis=0))
            for parts in plain
        )
    middle, half = WIDTH // 2, SMALL_ROWS // 2
    small = jnp.concatenate([grad_proj[middle : middle + half], grad_proj[middle + half + middle :]], axis=0)
    grad_proj = jnp.concatenate([grad_proj[:middle], grad_proj[middle + half : middle + half + middle]], axis=0)
    turns = small[5:7].reshape(2, HEADS, 2, 32)
    freq = (turns[:, :, 1] - turns[:, :, 0]).reshape(1, WIDTH)
    g_one, b_one, b_proj, g_two, b_two, b_down = (small[i : i + 1] for i in (0, 1, 7, 8, 9, 14))
    b_qkv, b_up = small[2:5].reshape(1, -1), small[10:14].reshape(1, -1)
    return (
        block_out, grad_tokens.astype(f32), g_one, b_one, grad_qkv[None], b_qkv, freq,
        grad_proj[None], b_proj, g_two, b_two, grad_up[None], b_up, grad_down[None], b_down,
    )


def solution(mesh):
    row = P(("dp", "section"), None)
    vector = P("section", None)
    matrix = P("section", None, None)
    params = (
        vector, vector, matrix, vector, vector, matrix, vector, vector, vector, matrix, vector, matrix, vector,
    )
    return jax.shard_map(
        per_device,
        mesh=mesh,
        in_specs=(row, row, P("dp")) + params,
        out_specs=(row, row) + params,
        check_vma=False,
    )
```

```python
from functools import partial
import math

import jax
import jax.numpy as jnp
import numpy as np
from jax import lax
from jax.experimental import pallas as pl
from jax.experimental.pallas import tpu as pltpu
from jax.sharding import PartitionSpec as P

HEADS = 12
SIDE_LARGE = 20
SIDE_MID = 16
SIDE_SMALL = 14
MICRO = 2
ROWS = 400
KEYS = 512
WIDTH = 768
HIDDEN = 3072
PAIRS = HEADS // 2
EPSILON = 1e-06
MASKED = -1e30
LOG2E = math.log2(math.e)
LN2 = math.log(2.0)
GELU_ONE = math.sqrt(2.0 / math.pi)
GELU_TWO = GELU_ONE * 0.044715

f32 = jnp.float32
bf16 = jnp.bfloat16
NT = (((1,), (1,)), ((), ()))
TN = (((0,), (0,)), ((), ()))

VEC_SIZES = (WIDTH, WIDTH, 3 * WIDTH, WIDTH, WIDTH, WIDTH, HIDDEN, WIDTH)
VEC_AT = tuple(int(v) for v in np.cumsum((0,) + VEC_SIZES))


def vec_part(vec_ref, index):
    return vec_ref[:, VEC_AT[index] : VEC_AT[index + 1]]


def swap_halves(values):
    lane = lax.broadcasted_iota(jnp.int32, values.shape, 1) % 64
    width = values.shape[1]
    return jnp.where(lane < 32, pltpu.roll(values, width - 32, 1), pltpu.roll(values, 32, 1))


def norm_parts(values):
    center = values - jnp.mean(values, axis=-1, keepdims=True)
    inverse = lax.rsqrt(jnp.mean(center * center, axis=-1, keepdims=True) + EPSILON)
    return center * inverse, inverse


def gelu_parts(pre):
    low = pre.astype(bf16)
    square = low * low
    tanh = jnp.tanh(low * (bf16(GELU_ONE) + bf16(GELU_TWO) * square))
    half = bf16(0.5) + bf16(0.5) * tanh
    value = low * half
    slope = half + (value - value * half) * (bf16(2 * GELU_ONE) + bf16(6 * GELU_TWO) * square)
    return value, slope


class Copies:
    def __init__(self, sems):
        self.sems = sems
        self.open = []
        self.used = 0

    def start(self, source, target):
        copy = pltpu.make_async_copy(source, target, self.sems.at[self.used])
        self.used += 1
        copy.start()
        self.open.append(copy)
        return copy

    def wait(self, *copies):
        for copy in copies:
            self.open = [other for other in self.open if other is not copy]
            copy.wait()

    def finish(self):
        self.wait(*list(self.open))


STATE_SHAPES = (
    ("x", (ROWS, WIDTH), bf16),
    ("a", (ROWS, WIDTH), bf16),
    ("qkv", (ROWS, 3 * WIDTH), bf16),
    ("e", (HEADS, ROWS, KEYS), bf16),
    ("linv", (ROWS, WIDTH), f32),
    ("o", (ROWS, WIDTH), bf16),
    ("n2", (ROWS, WIDTH), bf16),
    ("r2", (ROWS, 128), f32),
    ("c", (ROWS, WIDTH), bf16),
    ("g", (ROWS, HIDDEN), bf16),
    ("gp", (ROWS, HIDDEN), bf16),
)
STATES = tuple(name for name, _, _ in STATE_SHAPES)


def front_kernel(first, scal, layer, *refs):
    x_in, geo_in, cos_in, sin_in, wqkv_in, wp_in, wu_in, wd_in = refs[:8]
    vec_in, rest = refs[8:16], refs[17:]
    if not first:
        rest = rest[len(STATES) :]
    out_ref = rest[0]
    state = dict(zip(STATES, rest[1 : 1 + len(STATES)]))
    (
        x_v, vec_v, geo_v, cos_v, sin_v, wqkv_v, wp_v, wu_v, wd_v,
        a_v, qkv_v, e_v, s_v, li_v, o_v, m_v, n2_v, r2_v, c_v, g_v, gp_v, qcode_v, kcode_v, out_v, sems,
    ) = rest[1 + len(STATES) :]

    @pl.when(scal[0] == layer[0])
    def _():
        slot = layer[1]
        copies = Copies(sems)
        wait = copies.wait
        get_x = copies.start(x_in, x_v)
        get_vec = [
            copies.start(part, vec_v.at[:, pl.ds(at, size)]) for part, at, size in zip(vec_in, VEC_AT, VEC_SIZES)
        ]
        get_geo = copies.start(geo_in.at[slot], geo_v)
        get_qkv = [copies.start(wqkv_in.at[:, pl.ds(0, WIDTH)], wqkv_v.at[:, pl.ds(0, WIDTH)])]

        def put(source, name):
            copies.start(source, state[name].at[slot])

        qkv_v[ROWS:KEYS, :] = jnp.zeros((KEYS - ROWS, 3 * WIDTH), bf16)
        wait(get_x, *get_vec)
        get_cos = copies.start(cos_in.at[slot], cos_v)
        get_sin = copies.start(sin_in.at[slot], sin_v)
        for at in (WIDTH, 2 * WIDTH):
            get_qkv.append(copies.start(wqkv_in.at[:, pl.ds(at, WIDTH)], wqkv_v.at[:, pl.ds(at, WIDTH)]))
        normed, _ = norm_parts(x_v[...].astype(f32))
        a_v[...] = (normed * vec_part(vec_v, 0) + vec_part(vec_v, 1)).astype(bf16)
        wait(get_geo)
        segment = geo_v[:, 2:3]
        code = (lax.broadcasted_iota(jnp.int32, (KEYS, 128), 1) % 64).astype(f32)
        qcode_v[...] = jnp.where(segment[:ROWS] == code[:ROWS], 1.0, 0.0).astype(bf16)
        kcode_v[...] = jnp.where((segment != code) & (code < 4), MASKED, 0.0).astype(bf16)
        for part in range(3):
            at = part * WIDTH
            wait(get_qkv[part])
            if part == 0:
                wait(get_cos, get_sin)
                get_wp = copies.start(wp_in, wp_v)
                get_wu = copies.start(wu_in, wu_v)
                get_wd = copies.start(wd_in, wd_v)
            acc = jnp.dot(a_v[...], wqkv_v[:, at : at + WIDTH], preferred_element_type=f32)
            acc = acc + vec_v[:, VEC_AT[2] + at : VEC_AT[2] + at + WIDTH]
            if part < 2:
                acc = acc * cos_v[...] + swap_halves(acc) * sin_v[...]
            if part == 0:
                acc = acc * (LOG2E / 8.0)
            qkv_v[:ROWS, at : at + WIDTH] = acc.astype(bf16)

        lane_q = lax.broadcasted_iota(jnp.int32, (ROWS, 128), 1) // 64
        lane_k = lax.broadcasted_iota(jnp.int32, (KEYS, 128), 1) // 64

        def scores(index):
            pair, head = divmod(index, 2)
            q_one = jnp.where(lane_q == head, qkv_v[:ROWS, pair * 128 : pair * 128 + 128], qcode_v[...])
            k_at = WIDTH + pair * 128
            k_one = jnp.where(lane_k == head, qkv_v[:, k_at : k_at + 128], kcode_v[...])
            s_v[index % 4] = lax.dot_general(q_one, k_one, NT, preferred_element_type=f32)

        scores(0)
        sums = []
        for index in range(HEADS):
            pair, head = divmod(index, 2)
            if index + 1 < HEADS:
                scores(index + 1)
            v_at = 2 * WIDTH + pair * 128
            v_one = jnp.where(lane_k == head, qkv_v[:, v_at : v_at + 128], bf16(1.0))
            peak = jnp.max(s_v[index % 4], axis=1, keepdims=True)
            e_v[index] = jnp.exp2(s_v[index % 4] - peak).astype(bf16)
            sums.append(jnp.dot(e_v[index], v_one, preferred_element_type=f32))
            if head == 1:
                lanes = pl.ds(pair * 128, 128)
                inverse = 1.0 / pltpu.roll(jnp.where(lane_q == 0, sums[index], sums[index - 1]), 64, 1)
                li_v[:, lanes] = inverse
                o_v[:, lanes] = (jnp.where(lane_q == 0, sums[index - 1], sums[index]) * inverse).astype(bf16)
        put(x_v, "x")
        put(a_v, "a")
        put(qkv_v.at[pl.ds(0, ROWS)], "qkv")
        put(e_v, "e")
        put(li_v, "linv")
        put(o_v, "o")
        wait(get_wp)
        middle = (
            x_v[...].astype(f32)
            + jnp.dot(o_v[...], wp_v[...], preferred_element_type=f32)
            + vec_part(vec_v, 3)
        )
        m_v[...] = middle
        normed, inverse = norm_parts(middle)
        n2_v[...] = normed.astype(bf16)
        r2_v[...] = jnp.broadcast_to(inverse, (ROWS, 128))
        c_v[...] = (normed * vec_part(vec_v, 4) + vec_part(vec_v, 5)).astype(bf16)
        put(n2_v, "n2")
        put(r2_v, "r2")
        put(c_v, "c")
        wait(get_wu)
        chunk = 1024

        def up_step(step, carry):
            lanes = pl.ds(pl.multiple_of(step * chunk, chunk), chunk)
            blanes = pl.ds(pl.multiple_of(step * chunk + VEC_AT[6], 128), chunk)
            pre = jnp.dot(c_v[...], wu_v[:, lanes], preferred_element_type=f32) + vec_v[:, blanes]
            value, slope = gelu_parts(pre)
            g_v[:, lanes] = value
            gp_v[:, lanes] = slope
            return carry

        lax.fori_loop(0, HIDDEN // chunk, up_step, 0)
        put(gp_v, "gp")
        put(g_v, "g")
        wait(get_wd)
        for at in range(0, WIDTH, 256):
            part = pl.ds(at, 256)
            out = jnp.dot(g_v[...], wd_v[:, part], preferred_element_type=f32)
            out = out + m_v[:, part] + vec_v[:, VEC_AT[7] + at : VEC_AT[7] + at + 256]
            out_v[:, part] = out.astype(bf16)
            copies.start(out_v.at[:, part], out_ref.at[:, part])
        copies.finish()


ANY = pl.BlockSpec(memory_space=pl.ANY)
VMEM_LIMIT = 60 * 2**20


def vmem(*shape, dtype=bf16):
    return pltpu.VMEM(shape, dtype)


def call_states(kernel, first, operands, smem, states, plain_out, shapes, scratch, name):
    count = len(operands)
    state_out = [jax.ShapeDtypeStruct((MICRO,) + shape, dtype) for _, shape, dtype in shapes]
    operands = list(operands) + ([] if first else list(states))
    results = pl.pallas_call(
        partial(kernel, first),
        out_shape=list(plain_out) + state_out,
        in_specs=[pl.BlockSpec(memory_space=pltpu.SMEM)] * smem + [ANY] * (len(operands) - smem),
        out_specs=[ANY] * (len(plain_out) + len(shapes)),
        scratch_shapes=scratch,
        input_output_aliases={} if first else {count + i: len(plain_out) + i for i in range(len(shapes))},
        compiler_params=pltpu.CompilerParams(vmem_limit_bytes=VMEM_LIMIT),
        name=name,
    )(*operands)
    return results[0], tuple(results[1:])


def front_call(scal, layer, x, common, weights, vecs, states, earlier):
    scratch = [
        vmem(ROWS, WIDTH), vmem(1, VEC_AT[-1], dtype=f32), vmem(KEYS, 128, dtype=f32),
        vmem(ROWS, WIDTH, dtype=f32), vmem(ROWS, WIDTH, dtype=f32),
        vmem(WIDTH, 3 * WIDTH), vmem(WIDTH, WIDTH), vmem(WIDTH, HIDDEN), vmem(HIDDEN, WIDTH),
        vmem(ROWS, WIDTH), vmem(KEYS, 3 * WIDTH), vmem(HEADS, ROWS, KEYS), vmem(4, ROWS, KEYS, dtype=f32),
        vmem(ROWS, WIDTH, dtype=f32), vmem(ROWS, WIDTH), vmem(ROWS, WIDTH, dtype=f32),
        vmem(ROWS, WIDTH), vmem(ROWS, 128, dtype=f32), vmem(ROWS, WIDTH),
        vmem(ROWS, HIDDEN), vmem(ROWS, HIDDEN), vmem(ROWS, 128), vmem(KEYS, 128), vmem(ROWS, WIDTH),
        pltpu.SemaphoreType.DMA((36,)),
    ]
    operands = [scal, layer, x, *common, *weights, *vecs, earlier]
    out = jax.ShapeDtypeStruct((ROWS, WIDTH), bf16)
    return call_states(front_kernel, states is None, operands, 2, states, [out], STATE_SHAPES, scratch, "layer_front")


BACK_SHAPES = (
    ("du", (ROWS, HIDDEN), bf16),
    ("dz", (ROWS, WIDTH), bf16),
    ("dqkv", (ROWS, 3 * WIDTH), bf16),
    ("small", (8, WIDTH), f32),
)
BACKS = tuple(name for name, _, _ in BACK_SHAPES)


def back_kernel(first, scal, layer, *refs):
    dy_in, geo_in, cos_in, sin_in, wqkv_in, wp_in, wu_in, wd_in, gain_one_in, gain_two_in = refs[:10]
    saved = dict(zip(KEPT, refs[10 : 10 + len(KEPT)]))
    rest = refs[10 + len(KEPT) :]
    if not first:
        rest = rest[len(BACKS) :]
    dx_ref = rest[0]
    state = dict(zip(BACKS, rest[1 : 1 + len(BACKS)]))
    (
        dy_v, geo_v, cos_v, sin_v, wqkv_v, wp_v, wu_v, wd_v, gains_v,
        gp_v, n2_v, r2_v, li_v, qkv_v, e_v, o_v, x_v,
        du_v, dz_v, dm_v, dop_v, qt_v, dot_v, dq_v, dkt_v, dvt_v, dqkv_v, small_v, dx_v, sems,
    ) = rest[1 + len(BACKS) :]

    @pl.when(scal[0] == layer[0])
    def _():
        slot = layer[1]
        copies = Copies(sems)
        wait = copies.wait
        chunk = 1024
        steps = HIDDEN // chunk
        get_dy = copies.start(dy_in, dy_v)
        get_wd, get_gp = [], []
        for step in range(steps):
            part = pl.ds(step * chunk, chunk)
            get_wd.append(copies.start(wd_in.at[part], wd_v.at[part]))
            get_gp.append(copies.start(saved["gp"].at[slot, :, part], gp_v.at[:, part]))
        get_wu = copies.start(wu_in, wu_v)
        get_norm = [
            copies.start(saved["n2"].at[slot], n2_v),
            copies.start(saved["r2"].at[slot], r2_v),
            copies.start(gain_one_in, gains_v.at[pl.ds(0, 1)]),
            copies.start(gain_two_in, gains_v.at[pl.ds(8, 1)]),
        ]

        def put(source, name):
            copies.start(source, state[name].at[slot])

        qkv_v[ROWS:KEYS, :] = jnp.zeros((KEYS - ROWS, 3 * WIDTH), bf16)
        wait(get_dy)
        for step in range(steps):
            part = slice(step * chunk, (step + 1) * chunk)
            wait(get_wd[step], get_gp[step])
            act = lax.dot_general(dy_v[...], wd_v[part, :], NT, preferred_element_type=f32)
            du_v[:, part] = act.astype(bf16) * gp_v[:, part]
        get_wp = copies.start(wp_in, wp_v)
        get_li = copies.start(saved["linv"].at[slot], li_v)
        get_qkv = copies.start(saved["qkv"].at[slot], qkv_v.at[pl.ds(0, ROWS)])
        get_o = copies.start(saved["o"].at[slot], o_v)
        get_e = copies.start(saved["e"].at[slot], e_v)
        get_turn = [
            copies.start(cos_in.at[slot], cos_v),
            copies.start(sin_in.at[slot], sin_v),
            copies.start(geo_in.at[slot], geo_v),
        ]
        get_x = copies.start(saved["x"].at[slot], x_v)
        get_wqkv = copies.start(wqkv_in, wqkv_v)
        put(du_v, "du")
        wait(get_wu)
        dc = lax.dot_general(du_v[...], wu_v[...], NT, preferred_element_type=f32)
        wait(*get_norm)
        normed = n2_v[...].astype(f32)
        small_v[0:1, :] = jnp.sum(dc * normed, axis=0, keepdims=True)
        small_v[1:2, :] = jnp.sum(dc, axis=0, keepdims=True)
        hat = dc * gains_v[8:9, :]
        dm = dy_v[...].astype(f32) + r2_v[:, 0:1] * (
            hat
            - jnp.mean(hat, axis=-1, keepdims=True)
            - normed * jnp.mean(hat * normed, axis=-1, keepdims=True)
        )
        dm_v[...] = dm
        dz_v[...] = dm.astype(bf16)
        put(dz_v, "dz")
        wait(get_wp, get_li)
        do = lax.dot_general(dz_v[...], wp_v[...], NT, preferred_element_type=f32)
        dop_v[...] = (do * li_v[...]).astype(bf16)
        dot_v[...] = dop_v[...].T
        wait(get_qkv)
        qt_v[...] = qkv_v[:ROWS, :WIDTH].T
        wait(get_o, get_e)

        def pair_step(step, carry):
            for pair in [step * 2 + i for i in range(2)]:
                lanes = pl.ds(pl.multiple_of(pair * 128, 128), 128)
                klanes = pl.ds(pl.multiple_of(pair * 128 + WIDTH, 128), 128)
                vlanes = pl.ds(pl.multiple_of(pair * 128 + 2 * WIDTH, 128), 128)
                do_two = dop_v[:, lanes]
                k_two = qkv_v[:, klanes]
                v_two = qkv_v[:, vlanes]
                prod = do_two.astype(f32) * o_v[:, lanes].astype(f32)
                lane = lax.broadcasted_iota(jnp.int32, (ROWS, 128), 1) // 64
                dqs = []
                for head in range(2):
                    rows = pl.ds(pl.multiple_of(pair * 128 + head * 64, 64), 64)
                    do_one = jnp.where(lane == head, do_two, bf16(0.0))
                    dp = lax.dot_general(do_one, v_two, NT, preferred_element_type=f32)
                    delta = jnp.sum(jnp.where(lane == head, prod, 0.0), axis=1, keepdims=True)
                    probs = e_v[2 * pair + head]
                    ds = probs * (dp - delta).astype(bf16)
                    dqs.append(jnp.dot(ds, k_two, preferred_element_type=f32))
                    dkt_v[rows, :] = jnp.dot(qt_v[rows, :], ds, preferred_element_type=f32)
                    dvt_v[rows, :] = jnp.dot(dot_v[rows, :], probs, preferred_element_type=f32).astype(bf16)
                dq_v[:, lanes] = jnp.where(lane == 0, dqs[0], dqs[1])
            return carry

        lax.fori_loop(0, PAIRS // 2, pair_step, 0)
        wait(*get_turn)
        dqkv_v[:, 2 * WIDTH :] = dvt_v[...].T[:ROWS]
        dk = dkt_v[...].T[:ROWS]
        dq = dq_v[...]
        turn = dq * swap_halves(qkv_v[:ROWS, :WIDTH].astype(f32)) + dk * swap_halves(
            qkv_v[:ROWS, WIDTH : 2 * WIDTH].astype(f32)
        )
        small_v[4:5, :] = LN2 * jnp.sum(turn * geo_v[:ROWS, 0:1], axis=0, keepdims=True)
        small_v[5:6, :] = LN2 * jnp.sum(turn * geo_v[:ROWS, 1:2], axis=0, keepdims=True)
        dqkv_v[:, :WIDTH] = (0.125 * (dq * cos_v[...] - swap_halves(dq) * sin_v[...])).astype(bf16)
        dqkv_v[:, WIDTH : 2 * WIDTH] = (LN2 * (dk * cos_v[...] - swap_halves(dk) * sin_v[...])).astype(bf16)
        put(dqkv_v, "dqkv")
        wait(get_x)
        normed, inverse = norm_parts(x_v[...].astype(f32))
        wait(get_wqkv)
        da = lax.dot_general(dqkv_v[...], wqkv_v[...], NT, preferred_element_type=f32)
        small_v[2:3, :] = jnp.sum(da * normed, axis=0, keepdims=True)
        small_v[3:4, :] = jnp.sum(da, axis=0, keepdims=True)
        put(small_v, "small")
        hat = da * gains_v[0:1, :]
        dx = dm_v[...] + inverse * (
            hat
            - jnp.mean(hat, axis=-1, keepdims=True)
            - normed * jnp.mean(hat * normed, axis=-1, keepdims=True)
        )
        dx_v[...] = dx.astype(bf16)
        copies.start(dx_v, dx_ref)
        copies.finish()


KEPT = ("gp", "n2", "r2", "linv", "qkv", "e", "o", "x")


def back_call(scal, layer, dy, common, weights, vecs, fronts, backs):
    scratch = [
        vmem(ROWS, WIDTH), vmem(KEYS, 128, dtype=f32), vmem(ROWS, WIDTH, dtype=f32), vmem(ROWS, WIDTH, dtype=f32),
        vmem(WIDTH, 3 * WIDTH), vmem(WIDTH, WIDTH), vmem(WIDTH, HIDDEN), vmem(HIDDEN, WIDTH), vmem(16, WIDTH, dtype=f32),
        vmem(ROWS, HIDDEN), vmem(ROWS, WIDTH), vmem(ROWS, 128, dtype=f32), vmem(ROWS, WIDTH, dtype=f32),
        vmem(KEYS, 3 * WIDTH), vmem(HEADS, ROWS, KEYS), vmem(ROWS, WIDTH), vmem(ROWS, WIDTH),
        vmem(ROWS, HIDDEN), vmem(ROWS, WIDTH), vmem(ROWS, WIDTH, dtype=f32), vmem(ROWS, WIDTH),
        vmem(WIDTH, ROWS), vmem(WIDTH, ROWS), vmem(ROWS, WIDTH, dtype=f32),
        vmem(WIDTH, KEYS, dtype=f32), vmem(WIDTH, KEYS), vmem(ROWS, 3 * WIDTH), vmem(8, WIDTH, dtype=f32), vmem(ROWS, WIDTH),
        pltpu.SemaphoreType.DMA((36,)),
    ]
    operands = [scal, layer, dy, *common, *weights, vecs[0], vecs[4], *(fronts[name] for name in KEPT)]
    out = jax.ShapeDtypeStruct((ROWS, WIDTH), bf16)
    return call_states(back_kernel, backs is None, operands, 2, backs, [out], BACK_SHAPES, scratch, "layer_back")


def side_of(kind):
    return jnp.where(kind == 0, float(SIDE_LARGE), jnp.where(kind == 1, float(SIDE_MID), float(SIDE_SMALL)))


def places(kind, rows):
    side = side_of(kind)
    area = side * side
    images = jnp.where(kind == 2, 2.0, 1.0)
    image = (rows >= area).astype(f32) + (rows >= 2 * area).astype(f32)
    live = (image < images) & (rows < ROWS)
    local = rows - image * area
    patch_row = jnp.floor((local + 0.5) / side)
    patch_col = local - patch_row * side
    zero = jnp.zeros_like(rows)
    segment = jnp.where(live, image, jnp.where(rows < ROWS, 3.0, 2.0))
    return jnp.where(live, patch_row, zero), jnp.where(live, patch_col, zero), segment, live


def split_low(values):
    high = values.astype(bf16)
    return jnp.concatenate([high, (values - high.astype(f32)).astype(bf16)], axis=0)


def tables_kernel(kind_ref, freq_in, geo_ref, cos_ref, sin_ref, freq_v, geo_v, cos_v, sin_v, sems):
    copies = Copies(sems)
    copies.wait(copies.start(freq_in, freq_v))
    step = lax.broadcasted_iota(jnp.int32, (32, WIDTH // 2), 0).astype(f32)
    angles = [step * freq_v[:, at : at + WIDTH // 2] for at in (0, WIDTH // 2)]
    waves = [split_low(jnp.concatenate([jnp.cos(angle), jnp.sin(angle)], axis=1)) for angle in angles]
    sixteen = lax.broadcasted_iota(jnp.int32, (ROWS, 64), 1) % 32
    for micro in range(MICRO):
        rows = lax.broadcasted_iota(jnp.int32, (KEYS, 128), 0).astype(f32)
        lane = lax.broadcasted_iota(jnp.int32, (KEYS, 128), 1)
        patch_row, patch_col, segment, _ = places(kind_ref[micro], rows)
        geo_v[micro] = jnp.where(lane == 0, patch_row, jnp.where(lane == 1, patch_col, segment))
        picks = [
            jnp.where(sixteen.astype(f32) == patch[:ROWS, :64], 1.0, 0.0).astype(bf16)
            for patch in (patch_row, patch_col)
        ]
        row_wave, col_wave = (
            jnp.dot(pick, wave, preferred_element_type=f32) for pick, wave in zip(picks, waves)
        )
        half = WIDTH // 2
        row_cos, row_sin = row_wave[:, :half], row_wave[:, half:]
        col_cos, col_sin = col_wave[:, :half], col_wave[:, half:]
        cosine = row_cos * col_cos - row_sin * col_sin
        sine = row_sin * col_cos + row_cos * col_sin
        lane = lax.broadcasted_iota(jnp.int32, (ROWS, 128), 1)
        for part in range(half // 128):
            for pair in range(2):
                at = (2 * part + pair) * 128
                cos_v[micro, :, at : at + 128] = spread(cosine[:, part * 128 : part * 128 + 128], pair, lane)
                values = spread(sine[:, part * 128 : part * 128 + 128], pair, lane)
                sin_v[micro, :, at : at + 128] = jnp.where(lane % 64 < 32, -values, values)
        copies.start(geo_v.at[micro], geo_ref.at[micro])
        copies.start(cos_v.at[micro], cos_ref.at[micro])
        copies.start(sin_v.at[micro], sin_ref.at[micro])
    copies.finish()


def spread(values, pair, lane):
    base = values if pair == 0 else pltpu.roll(values, 64, 1)
    by_one = pltpu.roll(base, 32, 1)
    by_two = pltpu.roll(base, 64, 1)
    return jnp.where(lane < 32, base, jnp.where(lane < 96, by_one, by_two))


def tables(kinds, frequency):
    shapes = [(MICRO, KEYS, 128), (MICRO, ROWS, WIDTH), (MICRO, ROWS, WIDTH)]
    return pl.pallas_call(
        tables_kernel,
        out_shape=[jax.ShapeDtypeStruct(shape, f32) for shape in shapes],
        in_specs=[pl.BlockSpec(memory_space=pltpu.SMEM), ANY],
        out_specs=[ANY] * 3,
        scratch_shapes=[vmem(1, WIDTH, dtype=f32)]
        + [vmem(*shape, dtype=f32) for shape in shapes]
        + [pltpu.SemaphoreType.DMA((8,))],
        compiler_params=pltpu.CompilerParams(vmem_limit_bytes=VMEM_LIMIT),
        name="tables",
    )(kinds, frequency)


def live_rows_of(kinds):
    rows = jnp.broadcast_to(jnp.arange(ROWS, dtype=jnp.int32).astype(f32)[None, :], (MICRO, ROWS))
    return places(kinds[:, None], rows)[3].reshape(-1, 1)


def product_kernel(
    offset, block, core_ref, left_in, right_in, other_ref, own_ref, sums_ref,
    other_v, own_v, right_v, other_out, own_out, sums_out, sems,
):
    copies = Copies(sems)
    core = core_ref[0]
    half = left_in.shape[1] // 2
    rows = other_v.shape[1]
    get_right = copies.start(right_in, right_v)
    get_other = copies.start(left_in.at[:, pl.ds(pl.multiple_of((1 - core) * half + offset, 128), rows)], other_v)
    get_own = copies.start(left_in.at[:, pl.ds(pl.multiple_of(core * half + offset, 128), rows)], own_v)
    copies.wait(get_right)
    for get, part_v, part_out, ref in (
        (get_other, other_v, other_out, other_ref),
        (get_own, own_v, own_out, own_ref),
    ):
        copies.wait(get)

        for at in range(0, rows, block):
            lanes = pl.ds(at, block)
            part_out[lanes, :] = lax.dot_general(
                part_v[:, lanes], right_v[...], TN, preferred_element_type=f32
            ).astype(bf16)
            copies.start(part_out.at[lanes], ref.at[lanes])
    sums_out[...] = jnp.dot(jnp.ones((16, right_v.shape[0]), bf16), right_v[...], preferred_element_type=f32)[:8]
    copies.start(sums_out, sums_ref)
    copies.finish()


def product_call(core, left, right, offset, rows):
    left = left.reshape(MICRO * ROWS, left.shape[-1])
    right = right.reshape(MICRO * ROWS, right.shape[-1])
    count, width = right.shape
    block = 512 if rows % 512 == 0 else 384
    return pl.pallas_call(
        partial(product_kernel, offset, block),
        out_shape=[jax.ShapeDtypeStruct((rows, width), bf16)] * 2 + [jax.ShapeDtypeStruct((8, width), f32)],
        in_specs=[pl.BlockSpec(memory_space=pltpu.SMEM), ANY, ANY],
        out_specs=[ANY] * 3,
        scratch_shapes=[
            vmem(count, rows), vmem(count, rows), vmem(count, width), vmem(rows, width), vmem(rows, width),
            vmem(8, width, dtype=f32), pltpu.SemaphoreType.DMA((16,)),
        ],
        compiler_params=pltpu.CompilerParams(vmem_limit_bytes=VMEM_LIMIT),
        name="weight_grad",
    )(core, left, right)


SMALL_AT = (WIDTH, WIDTH, 3 * WIDTH, WIDTH, WIDTH, WIDTH, WIDTH, WIDTH, HIDDEN, WIDTH)
SMALL_ROWS = 32


def small_kernel(small_in, qkv_in, proj_in, up_in, down_in, low_ref, high_ref, *scratch):
    small_v, qkv_v, proj_v, up_v, down_v, rows_v, low_v, high_v, sems = scratch
    copies = Copies(sems)
    for source, target in ((small_in, small_v), (qkv_in, qkv_v), (proj_in, proj_v), (up_in, up_v), (down_in, down_v)):
        copies.start(source, target)
    copies.finish()
    rows_v[...] = jnp.zeros_like(rows_v)
    small = small_v[0] + small_v[1]
    parts = [small[2:3], small[3:4]]
    parts += [qkv_v[0:1, at : at + WIDTH] for at in range(0, 3 * WIDTH, WIDTH)]
    parts += [small[4:5], small[5:6], proj_v[0:1, :], small[0:1], small[1:2]]
    parts += [up_v[0:1, at : at + WIDTH] for at in range(0, HIDDEN, WIDTH)]
    parts += [down_v[0:1, :]]
    for index, part in enumerate(parts):
        rows_v[index : index + 1, :] = part
    half = SMALL_ROWS // 2
    low_v[...] = rows_v[:half, :].astype(bf16)
    high_v[...] = rows_v[half:, :].astype(bf16)
    copies.start(low_v, low_ref)
    copies.start(high_v, high_ref)
    copies.finish()


def small_call(small, qkv, proj, up, down):
    half = (SMALL_ROWS // 2, WIDTH)
    return pl.pallas_call(
        small_kernel,
        out_shape=[jax.ShapeDtypeStruct(half, bf16)] * 2,
        in_specs=[ANY] * 5,
        out_specs=[ANY] * 2,
        scratch_shapes=[
            vmem(MICRO, 8, WIDTH, dtype=f32), vmem(8, 3 * WIDTH, dtype=f32), vmem(8, WIDTH, dtype=f32),
            vmem(8, HIDDEN, dtype=f32), vmem(8, WIDTH, dtype=f32), vmem(SMALL_ROWS, WIDTH, dtype=f32),
            vmem(*half), vmem(*half), pltpu.SemaphoreType.DMA((8,)),
        ],
        name="small_grads",
    )(small, qkv, proj, up, down)


def send(value, source, target):
    return lax.ppermute(value, "section", [(source, target)])


def gathered(part, target, sections):
    pieces = [part if source == target else send(part, source, target) for source in range(sections)]
    return jnp.concatenate(pieces, axis=0)


def handed_out(output, grads, sections):
    section, last = lax.axis_index("section"), sections - 1
    share = output.shape[0] // sections

    def rows(whole, target):
        return whole[target * share : (target + 1) * share]

    output_share, grad_share = rows(output, last), rows(grads, 0)
    for target in range(last):
        mirror = last - target
        piece = jnp.where(section == last, rows(output, target), rows(grads, mirror))
        piece = lax.ppermute(piece, "section", [(last, target), (0, mirror)])
        output_share = jnp.where(section == target, piece, output_share)
        grad_share = jnp.where(section == mirror, piece, grad_share)
    return output_share, grad_share


def added(one, other):
    return (one.astype(f32) + other.astype(f32)).astype(bf16)


def both_cores(pairs):
    return [(2 * a + core, 2 * b + core) for a, b in pairs for core in range(2)]


def core_swap():
    return [(i, i ^ 1) for i in range(lax.axis_size("dp"))]


class Relay:
    def __init__(self):
        self.chunks, self.sums, self.totals = [], [], []
        self.flying, self.joined, self.clock = [], [], 0

    def start(self, value, pairs, then, keep, age, chunk=False):
        self.flying.append((self.clock + age, lax.ppermute(value, "dp", pairs), then, keep, chunk))

    def step(self, *gate, outer=0, inner=0, ahead=0):
        ready = [f for f in self.flying if f[0] <= self.clock + ahead]
        self.flying = [f for f in self.flying if f[0] > self.clock + ahead]
        fresh, self.chunks = self.chunks[:outer], self.chunks[outer:]
        arrays, keeps = [f[1] for f in ready], [f[3] for f in ready]
        new = [value for value, _ in fresh]
        joined, self.joined = self.joined, []
        results = [item.result for item in joined]
        arrays, keeps, new, gate, results = lax.optimization_barrier((arrays, keeps, new, gate, results))
        for item, result in zip(joined, results):
            item.result = result
        for (_, _, then, _, _), array, keep in zip(ready, arrays, keeps):
            then(array, keep)
        fresh = [(value, done) for value, (_, done) in zip(new, fresh)]
        for _ in range(outer):
            self.outer_start(fresh.pop(0) if fresh else None, self.totals.pop(0) if self.totals else None)
        for _ in range(min(inner, len(self.sums))):
            self.inner_start(*self.sums.pop(0))
        self.clock += 1
        return gate[0] if len(gate) == 1 else gate

    def inner_start(self, both, done):
        pairs = both_cores([(1, 2), (2, 1)])
        self.start(both, pairs, lambda array, keep: self.totals.append((added(keep, array), done)), both, 2)

    def outer_start(self, chunk, total):
        inward, outward = both_cores([(0, 1), (3, 2)]), both_cores([(1, 0), (2, 3)])
        chip = lax.axis_index("dp") // 2
        outer = (chip == 0) | (chip == 3)

        def inner_sum(array, own):
            self.sums.append((added(own, array), chunk[1]))

        def result(array, own):
            total[1](jnp.where(outer, array, own))

        if chunk and total and chunk[0].shape == total[0].shape:
            def land(array, keep):
                inner_sum(array, keep[0])
                result(array, keep[1])

            value = jnp.where(outer, chunk[0], total[0])
            self.start(value, inward + outward, land, (chunk[0], total[0]), 3, True)
        else:
            if total:
                self.start(total[0], outward, result, total[0], 3 if self.chunks or chunk else 8)
            if chunk:
                self.start(chunk[0], inward, inner_sum, chunk[0], 3, True)

    def finish(self):
        while self.chunks:
            self.pulse()
        while any(flight[0] > self.clock - 1 and flight[4] for flight in self.flying):
            self.step(outer=4, inner=4)
        while self.sums or self.totals or self.flying:
            self.step(outer=4, inner=4, ahead=9)
            self.step(outer=4, inner=4, ahead=2)

    def pulse(self, *gate):
        return self.step(*gate, inner=self.clock % 2, outer=1 - self.clock % 2)


class LineSum:
    def __init__(self, relay, axis):
        self.relay, self.axis, self.count = relay, axis, 0
        self.totals, self.result = {}, None

    def add(self, other, mine, ends):
        half = added(mine, lax.ppermute(other, "dp", core_swap()))
        for chunk in jnp.split(half, ends, axis=self.axis):
            self.relay.chunks.append((chunk, partial(self.landed, self.count)))
            self.count += 1

    def landed(self, index, total):
        self.totals[index] = total
        if len(self.totals) == self.count:
            mine = jnp.concatenate([self.totals[i] for i in range(self.count)], axis=self.axis)
            self.relay.start(mine, core_swap(), self.join, mine, 2)

    def join(self, other, mine):
        core = lax.axis_index("dp") % 2
        low, high = jnp.where(core == 0, mine, other), jnp.where(core == 0, other, mine)
        self.result = jnp.concatenate([low, high], axis=0).astype(f32)
        self.relay.joined.append(self)


def summed_by_compiler(part):
    count, rows = lax.axis_size("dp"), part.shape[0]
    part = jnp.pad(part, ((0, -rows % count), (0, 0)))
    own = lax.psum_scatter(part, "dp", scatter_dimension=0, tiled=True)
    return lax.all_gather(own, "dp", axis=0, tiled=True)[:rows].astype(f32)


def per_device(
    tokens,
    cotangent,
    image_kind,
    norm_one_gain,
    norm_one_bias,
    qkv_weight,
    qkv_bias,
    rotary_freq,
    proj_weight,
    proj_bias,
    norm_two_gain,
    norm_two_bias,
    up_weight,
    up_bias,
    down_weight,
    down_bias,
):
    sections = lax.axis_size("section")
    section = lax.axis_index("section")
    last = sections - 1
    by_line = lax.axis_size("dp") == 8
    scal = section.astype(jnp.int32).reshape(1)
    core = (lax.axis_index("dp") % 2).astype(jnp.int32).reshape(1)
    low = core[0] == 0
    common = tables(image_kind, rotary_freq)
    weights = (qkv_weight[0], proj_weight[0], up_weight[0], down_weight[0])
    vecs = (
        norm_one_gain, norm_one_bias, qkv_bias, proj_bias, norm_two_gain, norm_two_bias, up_bias, down_bias,
    )
    first_in = gathered(tokens, 0, sections)
    live_rows = live_rows_of(image_kind)
    last_in = gathered(cotangent, last, sections)
    last_in = jnp.where(live_rows > 0, last_in, bf16(0.0))

    def turn(layer, micro):
        return jnp.array([layer, micro], jnp.int32)

    states = None
    values = [first_in[m * ROWS : (m + 1) * ROWS] for m in range(MICRO)]
    backs, out_grads = None, None
    for layer in range(sections):
        for micro in range(MICRO):
            earlier = tokens
            if layer == last and micro == 1:
                fronts = dict(zip(STATES, states))
                turned, backs = back_call(scal, turn(last, 0), grads[0], common, weights, vecs, fronts, None)
                earlier = turned
            out, states = front_call(scal, turn(layer, micro), values[micro], common, weights, vecs, states, earlier)
            values[micro] = send(out, layer, layer + 1) if layer < last else out
        if layer == 1:
            values[0], last_in = lax.optimization_barrier((values[0], last_in))
            grads = [last_in[m * ROWS : (m + 1) * ROWS] for m in range(MICRO)]
            out_grads = list(grads)
    fronts = dict(zip(STATES, states))
    relay = Relay()
    sums = [LineSum(relay, axis) for axis in (1, 0, 1, 0)]
    plain = [[], [], [], []]

    def to_sum(index, other, mine, ends):
        if by_line:
            sums[index].add(other, mine, ends)
        else:
            plain[index].append((jnp.where(low, mine, other), jnp.where(low, other, mine)))

    for layer in reversed(range(sections)):
        if 0 < layer < last:
            out_grads = [jnp.where(section == layer, new, old) for new, old in zip(grads, out_grads)]
        if layer == 0:
            received = grads[0]
        for micro in range(MICRO):
            end = layer == 0 and micro == MICRO - 1
            if end:
                grads[0], grads[1], out_grads = lax.optimization_barrier((grads[0], grads[1], out_grads))
                out_grads = [jnp.where(section == 0, new, old) for new, old in zip((received, grads[1]), out_grads)]
                all_grads = jnp.concatenate(out_grads, axis=0)
                for offset in (0, 768):
                    other, mine, b_down = product_call(core, fronts["g"], all_grads, offset, 768)
                    to_sum(3, other, mine, [384])
                grads[1] = relay.step(grads[1], outer=2)
            if layer == last and micro == 0:
                dx = turned
            else:
                dx, backs = back_call(scal, turn(layer, micro), grads[micro], common, weights, vecs, fronts, backs)
            if end:
                values[0], values[1], dx, backs = relay.step(*values, dx, backs, outer=1, inner=1, ahead=9)
            grads[micro] = send(dx, layer, layer - 1) if layer > 0 else dx
    backs = dict(zip(BACKS, backs))
    other, mine, b_up = product_call(core, fronts["c"], backs["du"], 0, WIDTH // 2)
    to_sum(2, other, mine, [768, 1536, 2304])
    final = jnp.where(live_rows > 0, jnp.concatenate(values, axis=0), bf16(0.0))
    block_out, grad_tokens = handed_out(final, jnp.concatenate(grads, axis=0), sections)
    b_up, block_out, grad_tokens, dqkv = relay.step(
        b_up, block_out, grad_tokens, backs["dqkv"], outer=1, inner=1, ahead=9
    )
    other, mine, b_qkv = product_call(core, fronts["a"], dqkv, 0, WIDTH // 2)
    to_sum(0, other, mine, [768, 1536])
    other, mine, b_proj = product_call(core, fronts["o"], backs["dz"], 0, WIDTH // 2)
    lows, highs = small_call(backs["small"], b_qkv, b_proj, b_up, b_down)
    mine = jnp.concatenate([mine, jnp.where(low, lows, highs)], axis=0)
    other = jnp.concatenate([other, jnp.where(low, highs, lows)], axis=0)
    other, mine = relay.step(other, mine, outer=1, inner=1, ahead=9)
    to_sum(1, other, mine, [])
    relay.clock += relay.clock % 2
    relay.finish()
    if by_line:
        grad_qkv, grad_proj, grad_up, grad_down = (item.result for item in sums)
    else:
        grad_qkv, grad_proj, grad_up, grad_down = (
            summed_by_compiler(jnp.concatenate([part[side] for side in range(2) for part in parts], axis=0))
            for parts in plain
        )
    middle, half = WIDTH // 2, SMALL_ROWS // 2
    small = jnp.concatenate([grad_proj[middle : middle + half], grad_proj[middle + half + middle :]], axis=0)
    grad_proj = jnp.concatenate([grad_proj[:middle], grad_proj[middle + half : middle + half + middle]], axis=0)
    turns = small[5:7].reshape(2, HEADS, 2, 32)
    freq = (turns[:, :, 1] - turns[:, :, 0]).reshape(1, WIDTH)
    g_one, b_one, b_proj, g_two, b_two, b_down = (small[i : i + 1] for i in (0, 1, 7, 8, 9, 14))
    b_qkv, b_up = small[2:5].reshape(1, -1), small[10:14].reshape(1, -1)
    return (
        block_out, grad_tokens.astype(f32), g_one, b_one, grad_qkv[None], b_qkv, freq,
        grad_proj[None], b_proj, g_two, b_two, grad_up[None], b_up, grad_down[None], b_down,
    )


def solution(mesh):
    row = P(("dp", "section"), None)
    vector = P("section", None)
    matrix = P("section", None, None)
    params = (
        vector, vector, matrix, vector, vector, matrix, vector, vector, vector, matrix, vector, matrix, vector,
    )
    return jax.shard_map(
        per_device,
        mesh=mesh,
        in_specs=(row, row, P("dp")) + params,
        out_specs=(row, row) + params,
        check_vma=False,
    )
```

```python
from functools import partial
import math

import jax
import jax.numpy as jnp
import numpy as np
from jax import lax
from jax.experimental import pallas as pl
from jax.experimental.pallas import tpu as pltpu
from jax.sharding import PartitionSpec as P

HEADS = 12
SIDE_LARGE = 20
SIDE_MID = 16
SIDE_SMALL = 14
MICRO = 2
ROWS = 400
KEYS = 512
WIDTH = 768
HIDDEN = 3072
PAIRS = HEADS // 2
EPSILON = 1e-06
MASKED = -1e30
LOG2E = math.log2(math.e)
LN2 = math.log(2.0)
GELU_ONE = math.sqrt(2.0 / math.pi)
GELU_TWO = GELU_ONE * 0.044715

f32 = jnp.float32
bf16 = jnp.bfloat16
NT = (((1,), (1,)), ((), ()))
TN = (((0,), (0,)), ((), ()))

VEC_SIZES = (WIDTH, WIDTH, 3 * WIDTH, WIDTH, WIDTH, WIDTH, HIDDEN, WIDTH)
VEC_AT = tuple(int(v) for v in np.cumsum((0,) + VEC_SIZES))


def vec_part(vec_ref, index):
    return vec_ref[:, VEC_AT[index] : VEC_AT[index + 1]]


def swap_halves(values):
    lane = lax.broadcasted_iota(jnp.int32, values.shape, 1) % 64
    width = values.shape[1]
    return jnp.where(lane < 32, pltpu.roll(values, width - 32, 1), pltpu.roll(values, 32, 1))


def norm_parts(values):
    center = values - jnp.mean(values, axis=-1, keepdims=True)
    inverse = lax.rsqrt(jnp.mean(center * center, axis=-1, keepdims=True) + EPSILON)
    return center * inverse, inverse


def gelu_parts(pre):
    low = pre.astype(bf16)
    square = low * low
    tanh = jnp.tanh(low * (bf16(GELU_ONE) + bf16(GELU_TWO) * square))
    half = bf16(0.5) + bf16(0.5) * tanh
    value = low * half
    slope = half + (value - value * half) * (bf16(2 * GELU_ONE) + bf16(6 * GELU_TWO) * square)
    return value, slope


class Copies:
    def __init__(self, sems):
        self.sems = sems
        self.open = []
        self.used = 0

    def start(self, source, target):
        copy = pltpu.make_async_copy(source, target, self.sems.at[self.used])
        self.used += 1
        copy.start()
        self.open.append(copy)
        return copy

    def wait(self, *copies):
        for copy in copies:
            self.open = [other for other in self.open if other is not copy]
            copy.wait()

    def finish(self):
        self.wait(*list(self.open))


STATE_SHAPES = (
    ("x", (ROWS, WIDTH), bf16),
    ("a", (ROWS, WIDTH), bf16),
    ("qkv", (ROWS, 3 * WIDTH), bf16),
    ("e", (HEADS, ROWS, KEYS), bf16),
    ("linv", (ROWS, WIDTH), f32),
    ("o", (ROWS, WIDTH), bf16),
    ("n2", (ROWS, WIDTH), bf16),
    ("r2", (ROWS, 128), f32),
    ("c", (ROWS, WIDTH), bf16),
    ("g", (ROWS, HIDDEN), bf16),
    ("gp", (ROWS, HIDDEN), bf16),
)
STATES = tuple(name for name, _, _ in STATE_SHAPES)


def front_kernel(first, scal, layer, *refs):
    x_in, geo_in, cos_in, sin_in, wqkv_in, wp_in, wu_in, wd_in = refs[:8]
    vec_in, rest = refs[8:16], refs[17:]
    if not first:
        rest = rest[len(STATES) :]
    out_ref = rest[0]
    state = dict(zip(STATES, rest[1 : 1 + len(STATES)]))
    (
        x_v, vec_v, geo_v, cos_v, sin_v, wqkv_v, wp_v, wu_v, wd_v,
        a_v, qkv_v, e_v, s_v, li_v, o_v, m_v, n2_v, r2_v, c_v, g_v, gp_v, qcode_v, kcode_v, out_v, sems,
    ) = rest[1 + len(STATES) :]

    @pl.when(scal[0] == layer[0])
    def _():
        slot = layer[1]
        copies = Copies(sems)
        wait = copies.wait
        get_x = copies.start(x_in, x_v)
        get_vec = [
            copies.start(part, vec_v.at[:, pl.ds(at, size)]) for part, at, size in zip(vec_in, VEC_AT, VEC_SIZES)
        ]
        get_geo = copies.start(geo_in.at[slot], geo_v)
        get_qkv = [copies.start(wqkv_in.at[:, pl.ds(0, WIDTH)], wqkv_v.at[:, pl.ds(0, WIDTH)])]

        def put(source, name):
            copies.start(source, state[name].at[slot])

        qkv_v[ROWS:KEYS, :] = jnp.zeros((KEYS - ROWS, 3 * WIDTH), bf16)
        wait(get_x, *get_vec)
        get_cos = copies.start(cos_in.at[slot], cos_v)
        get_sin = copies.start(sin_in.at[slot], sin_v)
        for at in (WIDTH, 2 * WIDTH):
            get_qkv.append(copies.start(wqkv_in.at[:, pl.ds(at, WIDTH)], wqkv_v.at[:, pl.ds(at, WIDTH)]))
        normed, _ = norm_parts(x_v[...].astype(f32))
        a_v[...] = (normed * vec_part(vec_v, 0) + vec_part(vec_v, 1)).astype(bf16)
        wait(get_geo)
        segment = geo_v[:, 2:3]
        code = (lax.broadcasted_iota(jnp.int32, (KEYS, 128), 1) % 64).astype(f32)
        qcode_v[...] = jnp.where(segment[:ROWS] == code[:ROWS], 1.0, 0.0).astype(bf16)
        kcode_v[...] = jnp.where((segment != code) & (code < 4), MASKED, 0.0).astype(bf16)
        for part in range(3):
            at = part * WIDTH
            wait(get_qkv[part])
            if part == 0:
                wait(get_cos, get_sin)
                get_wp = copies.start(wp_in, wp_v)
                get_wu = copies.start(wu_in, wu_v)
                get_wd = copies.start(wd_in, wd_v)
            acc = jnp.dot(a_v[...], wqkv_v[:, at : at + WIDTH], preferred_element_type=f32)
            acc = acc + vec_v[:, VEC_AT[2] + at : VEC_AT[2] + at + WIDTH]
            if part < 2:
                acc = acc * cos_v[...] + swap_halves(acc) * sin_v[...]
            if part == 0:
                acc = acc * (LOG2E / 8.0)
            qkv_v[:ROWS, at : at + WIDTH] = acc.astype(bf16)

        lane_q = lax.broadcasted_iota(jnp.int32, (ROWS, 128), 1) // 64
        lane_k = lax.broadcasted_iota(jnp.int32, (KEYS, 128), 1) // 64

        def scores(index):
            pair, head = divmod(index, 2)
            q_one = jnp.where(lane_q == head, qkv_v[:ROWS, pair * 128 : pair * 128 + 128], qcode_v[...])
            k_at = WIDTH + pair * 128
            k_one = jnp.where(lane_k == head, qkv_v[:, k_at : k_at + 128], kcode_v[...])
            s_v[index % 4] = lax.dot_general(q_one, k_one, NT, preferred_element_type=f32)

        scores(0)
        sums = []
        for index in range(HEADS):
            pair, head = divmod(index, 2)
            if index + 1 < HEADS:
                scores(index + 1)
            v_at = 2 * WIDTH + pair * 128
            v_one = jnp.where(lane_k == head, qkv_v[:, v_at : v_at + 128], bf16(1.0))
            peak = jnp.max(s_v[index % 4], axis=1, keepdims=True)
            e_v[index] = jnp.exp2(s_v[index % 4] - peak).astype(bf16)
            sums.append(jnp.dot(e_v[index], v_one, preferred_element_type=f32))
            if head == 1:
                lanes = pl.ds(pair * 128, 128)
                inverse = 1.0 / pltpu.roll(jnp.where(lane_q == 0, sums[index], sums[index - 1]), 64, 1)
                li_v[:, lanes] = inverse
                o_v[:, lanes] = (jnp.where(lane_q == 0, sums[index - 1], sums[index]) * inverse).astype(bf16)
        put(x_v, "x")
        put(a_v, "a")
        put(qkv_v.at[pl.ds(0, ROWS)], "qkv")
        put(e_v, "e")
        put(li_v, "linv")
        put(o_v, "o")
        wait(get_wp)
        middle = (
            x_v[...].astype(f32)
            + jnp.dot(o_v[...], wp_v[...], preferred_element_type=f32)
            + vec_part(vec_v, 3)
        )
        m_v[...] = middle
        normed, inverse = norm_parts(middle)
        n2_v[...] = normed.astype(bf16)
        r2_v[...] = jnp.broadcast_to(inverse, (ROWS, 128))
        c_v[...] = (normed * vec_part(vec_v, 4) + vec_part(vec_v, 5)).astype(bf16)
        put(n2_v, "n2")
        put(r2_v, "r2")
        put(c_v, "c")
        wait(get_wu)
        chunk = 1024

        def up_step(step, carry):
            lanes = pl.ds(pl.multiple_of(step * chunk, chunk), chunk)
            blanes = pl.ds(pl.multiple_of(step * chunk + VEC_AT[6], 128), chunk)
            pre = jnp.dot(c_v[...], wu_v[:, lanes], preferred_element_type=f32) + vec_v[:, blanes]
            value, slope = gelu_parts(pre)
            g_v[:, lanes] = value
            gp_v[:, lanes] = slope
            return carry

        lax.fori_loop(0, HIDDEN // chunk, up_step, 0)
        put(gp_v, "gp")
        put(g_v, "g")
        wait(get_wd)
        for at in range(0, WIDTH, 256):
            part = pl.ds(at, 256)
            out = jnp.dot(g_v[...], wd_v[:, part], preferred_element_type=f32)
            out = out + m_v[:, part] + vec_v[:, VEC_AT[7] + at : VEC_AT[7] + at + 256]
            out_v[:, part] = out.astype(bf16)
            copies.start(out_v.at[:, part], out_ref.at[:, part])
        copies.finish()


ANY = pl.BlockSpec(memory_space=pl.ANY)
VMEM_LIMIT = 60 * 2**20


def vmem(*shape, dtype=bf16):
    return pltpu.VMEM(shape, dtype)


def call_states(kernel, first, operands, smem, states, plain_out, shapes, scratch, name):
    count = len(operands)
    state_out = [jax.ShapeDtypeStruct((MICRO,) + shape, dtype) for _, shape, dtype in shapes]
    operands = list(operands) + ([] if first else list(states))
    results = pl.pallas_call(
        partial(kernel, first),
        out_shape=list(plain_out) + state_out,
        in_specs=[pl.BlockSpec(memory_space=pltpu.SMEM)] * smem + [ANY] * (len(operands) - smem),
        out_specs=[ANY] * (len(plain_out) + len(shapes)),
        scratch_shapes=scratch,
        input_output_aliases={} if first else {count + i: len(plain_out) + i for i in range(len(shapes))},
        compiler_params=pltpu.CompilerParams(vmem_limit_bytes=VMEM_LIMIT),
        name=name,
    )(*operands)
    return results[0], tuple(results[1:])


def front_call(scal, layer, x, common, weights, vecs, states, earlier):
    scratch = [
        vmem(ROWS, WIDTH), vmem(1, VEC_AT[-1], dtype=f32), vmem(KEYS, 128, dtype=f32),
        vmem(ROWS, WIDTH, dtype=f32), vmem(ROWS, WIDTH, dtype=f32),
        vmem(WIDTH, 3 * WIDTH), vmem(WIDTH, WIDTH), vmem(WIDTH, HIDDEN), vmem(HIDDEN, WIDTH),
        vmem(ROWS, WIDTH), vmem(KEYS, 3 * WIDTH), vmem(HEADS, ROWS, KEYS), vmem(4, ROWS, KEYS, dtype=f32),
        vmem(ROWS, WIDTH, dtype=f32), vmem(ROWS, WIDTH), vmem(ROWS, WIDTH, dtype=f32),
        vmem(ROWS, WIDTH), vmem(ROWS, 128, dtype=f32), vmem(ROWS, WIDTH),
        vmem(ROWS, HIDDEN), vmem(ROWS, HIDDEN), vmem(ROWS, 128), vmem(KEYS, 128), vmem(ROWS, WIDTH),
        pltpu.SemaphoreType.DMA((36,)),
    ]
    operands = [scal, layer, x, *common, *weights, *vecs, earlier]
    out = jax.ShapeDtypeStruct((ROWS, WIDTH), bf16)
    return call_states(front_kernel, states is None, operands, 2, states, [out], STATE_SHAPES, scratch, "layer_front")


BACK_SHAPES = (
    ("du", (ROWS, HIDDEN), bf16),
    ("dz", (ROWS, WIDTH), bf16),
    ("dqkv", (ROWS, 3 * WIDTH), bf16),
    ("small", (8, WIDTH), f32),
)
BACKS = tuple(name for name, _, _ in BACK_SHAPES)


def back_kernel(first, scal, layer, *refs):
    dy_in, geo_in, cos_in, sin_in, wqkv_in, wp_in, wu_in, wd_in, gain_one_in, gain_two_in = refs[:10]
    saved = dict(zip(KEPT, refs[10 : 10 + len(KEPT)]))
    rest = refs[10 + len(KEPT) :]
    if not first:
        rest = rest[len(BACKS) :]
    dx_ref = rest[0]
    state = dict(zip(BACKS, rest[1 : 1 + len(BACKS)]))
    (
        dy_v, geo_v, cos_v, sin_v, wqkv_v, wp_v, wu_v, wd_v, gains_v,
        gp_v, n2_v, r2_v, li_v, qkv_v, e_v, o_v, x_v,
        du_v, dz_v, dm_v, dop_v, qt_v, dot_v, dq_v, dkt_v, dvt_v, dqkv_v, small_v, dx_v, sems,
    ) = rest[1 + len(BACKS) :]

    @pl.when(scal[0] == layer[0])
    def _():
        slot = layer[1]
        copies = Copies(sems)
        wait = copies.wait
        chunk = 1024
        steps = HIDDEN // chunk
        get_dy = copies.start(dy_in, dy_v)
        get_wd, get_gp = [], []

        def get_chunk(step):
            part = pl.ds(step * chunk, chunk)
            get_wd.append(copies.start(wd_in.at[part], wd_v.at[part]))
            get_gp.append(copies.start(saved["gp"].at[slot, :, part], gp_v.at[:, part]))

        get_chunk(0)
        get_chunk(1)

        def put(source, name):
            copies.start(source, state[name].at[slot])

        qkv_v[ROWS:KEYS, :] = jnp.zeros((KEYS - ROWS, 3 * WIDTH), bf16)
        wait(get_dy)
        for step in range(steps):
            part = slice(step * chunk, (step + 1) * chunk)
            wait(get_wd[step], get_gp[step])
            if step == 0:
                for later in range(2, steps):
                    get_chunk(later)
                get_wu = copies.start(wu_in, wu_v)
                get_norm = [
                    copies.start(saved["n2"].at[slot], n2_v),
                    copies.start(saved["r2"].at[slot], r2_v),
                    copies.start(gain_one_in, gains_v.at[pl.ds(0, 1)]),
                    copies.start(gain_two_in, gains_v.at[pl.ds(8, 1)]),
                ]
            act = lax.dot_general(dy_v[...], wd_v[part, :], NT, preferred_element_type=f32)
            du_v[:, part] = act.astype(bf16) * gp_v[:, part]
        get_wp = copies.start(wp_in, wp_v)
        get_li = copies.start(saved["linv"].at[slot], li_v)
        get_qkv = copies.start(saved["qkv"].at[slot], qkv_v.at[pl.ds(0, ROWS)])
        get_o = copies.start(saved["o"].at[slot], o_v)
        get_e = copies.start(saved["e"].at[slot], e_v)
        get_turn = [
            copies.start(cos_in.at[slot], cos_v),
            copies.start(sin_in.at[slot], sin_v),
            copies.start(geo_in.at[slot], geo_v),
        ]
        get_x = copies.start(saved["x"].at[slot], x_v)
        get_wqkv = copies.start(wqkv_in, wqkv_v)
        put(du_v, "du")
        wait(get_wu)
        dc = lax.dot_general(du_v[...], wu_v[...], NT, preferred_element_type=f32)
        wait(*get_norm)
        normed = n2_v[...].astype(f32)
        small_v[0:1, :] = jnp.sum(dc * normed, axis=0, keepdims=True)
        small_v[1:2, :] = jnp.sum(dc, axis=0, keepdims=True)
        hat = dc * gains_v[8:9, :]
        dm = dy_v[...].astype(f32) + r2_v[:, 0:1] * (
            hat
            - jnp.mean(hat, axis=-1, keepdims=True)
            - normed * jnp.mean(hat * normed, axis=-1, keepdims=True)
        )
        dm_v[...] = dm
        dz_v[...] = dm.astype(bf16)
        put(dz_v, "dz")
        wait(get_wp, get_li)
        do = lax.dot_general(dz_v[...], wp_v[...], NT, preferred_element_type=f32)
        dop_v[...] = (do * li_v[...]).astype(bf16)
        dot_v[...] = dop_v[...].T
        wait(get_qkv)
        qt_v[...] = qkv_v[:ROWS, :WIDTH].T
        wait(get_o, get_e)

        def pair_step(step, carry):
            for pair in [step * 2 + i for i in range(2)]:
                lanes = pl.ds(pl.multiple_of(pair * 128, 128), 128)
                klanes = pl.ds(pl.multiple_of(pair * 128 + WIDTH, 128), 128)
                vlanes = pl.ds(pl.multiple_of(pair * 128 + 2 * WIDTH, 128), 128)
                do_two = dop_v[:, lanes]
                k_two = qkv_v[:, klanes]
                v_two = qkv_v[:, vlanes]
                prod = do_two.astype(f32) * o_v[:, lanes].astype(f32)
                lane = lax.broadcasted_iota(jnp.int32, (ROWS, 128), 1) // 64
                dqs = []
                for head in range(2):
                    rows = pl.ds(pl.multiple_of(pair * 128 + head * 64, 64), 64)
                    do_one = jnp.where(lane == head, do_two, bf16(0.0))
                    dp = lax.dot_general(do_one, v_two, NT, preferred_element_type=f32)
                    delta = jnp.sum(jnp.where(lane == head, prod, 0.0), axis=1, keepdims=True)
                    probs = e_v[2 * pair + head]
                    ds = probs * (dp - delta).astype(bf16)
                    dqs.append(jnp.dot(ds, k_two, preferred_element_type=f32))
                    dkt_v[rows, :] = jnp.dot(qt_v[rows, :], ds, preferred_element_type=f32)
                    dvt_v[rows, :] = jnp.dot(dot_v[rows, :], probs, preferred_element_type=f32).astype(bf16)
                dq_v[:, lanes] = jnp.where(lane == 0, dqs[0], dqs[1])
            return carry

        lax.fori_loop(0, PAIRS // 2, pair_step, 0)
        wait(*get_turn)
        dqkv_v[:, 2 * WIDTH :] = dvt_v[...].T[:ROWS]
        dk = dkt_v[...].T[:ROWS]
        dq = dq_v[...]
        turn = dq * swap_halves(qkv_v[:ROWS, :WIDTH].astype(f32)) + dk * swap_halves(
            qkv_v[:ROWS, WIDTH : 2 * WIDTH].astype(f32)
        )
        small_v[4:5, :] = LN2 * jnp.sum(turn * geo_v[:ROWS, 0:1], axis=0, keepdims=True)
        small_v[5:6, :] = LN2 * jnp.sum(turn * geo_v[:ROWS, 1:2], axis=0, keepdims=True)
        dqkv_v[:, :WIDTH] = (0.125 * (dq * cos_v[...] - swap_halves(dq) * sin_v[...])).astype(bf16)
        dqkv_v[:, WIDTH : 2 * WIDTH] = (LN2 * (dk * cos_v[...] - swap_halves(dk) * sin_v[...])).astype(bf16)
        put(dqkv_v, "dqkv")
        wait(get_x)
        normed, inverse = norm_parts(x_v[...].astype(f32))
        wait(get_wqkv)
        da = lax.dot_general(dqkv_v[...], wqkv_v[...], NT, preferred_element_type=f32)
        small_v[2:3, :] = jnp.sum(da * normed, axis=0, keepdims=True)
        small_v[3:4, :] = jnp.sum(da, axis=0, keepdims=True)
        put(small_v, "small")
        hat = da * gains_v[0:1, :]
        dx = dm_v[...] + inverse * (
            hat
            - jnp.mean(hat, axis=-1, keepdims=True)
            - normed * jnp.mean(hat * normed, axis=-1, keepdims=True)
        )
        dx_v[...] = dx.astype(bf16)
        copies.start(dx_v, dx_ref)
        copies.finish()


KEPT = ("gp", "n2", "r2", "linv", "qkv", "e", "o", "x")


def back_call(scal, layer, dy, common, weights, vecs, fronts, backs):
    scratch = [
        vmem(ROWS, WIDTH), vmem(KEYS, 128, dtype=f32), vmem(ROWS, WIDTH, dtype=f32), vmem(ROWS, WIDTH, dtype=f32),
        vmem(WIDTH, 3 * WIDTH), vmem(WIDTH, WIDTH), vmem(WIDTH, HIDDEN), vmem(HIDDEN, WIDTH), vmem(16, WIDTH, dtype=f32),
        vmem(ROWS, HIDDEN), vmem(ROWS, WIDTH), vmem(ROWS, 128, dtype=f32), vmem(ROWS, WIDTH, dtype=f32),
        vmem(KEYS, 3 * WIDTH), vmem(HEADS, ROWS, KEYS), vmem(ROWS, WIDTH), vmem(ROWS, WIDTH),
        vmem(ROWS, HIDDEN), vmem(ROWS, WIDTH), vmem(ROWS, WIDTH, dtype=f32), vmem(ROWS, WIDTH),
        vmem(WIDTH, ROWS), vmem(WIDTH, ROWS), vmem(ROWS, WIDTH, dtype=f32),
        vmem(WIDTH, KEYS, dtype=f32), vmem(WIDTH, KEYS), vmem(ROWS, 3 * WIDTH), vmem(8, WIDTH, dtype=f32), vmem(ROWS, WIDTH),
        pltpu.SemaphoreType.DMA((36,)),
    ]
    operands = [scal, layer, dy, *common, *weights, vecs[0], vecs[4], *(fronts[name] for name in KEPT)]
    out = jax.ShapeDtypeStruct((ROWS, WIDTH), bf16)
    return call_states(back_kernel, backs is None, operands, 2, backs, [out], BACK_SHAPES, scratch, "layer_back")


def side_of(kind):
    return jnp.where(kind == 0, float(SIDE_LARGE), jnp.where(kind == 1, float(SIDE_MID), float(SIDE_SMALL)))


def places(kind, rows):
    side = side_of(kind)
    area = side * side
    images = jnp.where(kind == 2, 2.0, 1.0)
    image = (rows >= area).astype(f32) + (rows >= 2 * area).astype(f32)
    live = (image < images) & (rows < ROWS)
    local = rows - image * area
    patch_row = jnp.floor((local + 0.5) / side)
    patch_col = local - patch_row * side
    zero = jnp.zeros_like(rows)
    segment = jnp.where(live, image, jnp.where(rows < ROWS, 3.0, 2.0))
    return jnp.where(live, patch_row, zero), jnp.where(live, patch_col, zero), segment, live


def split_low(values):
    high = values.astype(bf16)
    return jnp.concatenate([high, (values - high.astype(f32)).astype(bf16)], axis=0)


def tables_kernel(kind_ref, freq_in, geo_ref, cos_ref, sin_ref, freq_v, geo_v, cos_v, sin_v, sems):
    copies = Copies(sems)
    copies.wait(copies.start(freq_in, freq_v))
    step = lax.broadcasted_iota(jnp.int32, (32, WIDTH // 2), 0).astype(f32)
    angles = [step * freq_v[:, at : at + WIDTH // 2] for at in (0, WIDTH // 2)]
    waves = [split_low(jnp.concatenate([jnp.cos(angle), jnp.sin(angle)], axis=1)) for angle in angles]
    sixteen = lax.broadcasted_iota(jnp.int32, (ROWS, 64), 1) % 32
    for micro in range(MICRO):
        rows = lax.broadcasted_iota(jnp.int32, (KEYS, 128), 0).astype(f32)
        lane = lax.broadcasted_iota(jnp.int32, (KEYS, 128), 1)
        patch_row, patch_col, segment, _ = places(kind_ref[micro], rows)
        geo_v[micro] = jnp.where(lane == 0, patch_row, jnp.where(lane == 1, patch_col, segment))
        picks = [
            jnp.where(sixteen.astype(f32) == patch[:ROWS, :64], 1.0, 0.0).astype(bf16)
            for patch in (patch_row, patch_col)
        ]
        row_wave, col_wave = (
            jnp.dot(pick, wave, preferred_element_type=f32) for pick, wave in zip(picks, waves)
        )
        half = WIDTH // 2
        row_cos, row_sin = row_wave[:, :half], row_wave[:, half:]
        col_cos, col_sin = col_wave[:, :half], col_wave[:, half:]
        cosine = row_cos * col_cos - row_sin * col_sin
        sine = row_sin * col_cos + row_cos * col_sin
        lane = lax.broadcasted_iota(jnp.int32, (ROWS, 128), 1)
        for part in range(half // 128):
            for pair in range(2):
                at = (2 * part + pair) * 128
                cos_v[micro, :, at : at + 128] = spread(cosine[:, part * 128 : part * 128 + 128], pair, lane)
                values = spread(sine[:, part * 128 : part * 128 + 128], pair, lane)
                sin_v[micro, :, at : at + 128] = jnp.where(lane % 64 < 32, -values, values)
        copies.start(geo_v.at[micro], geo_ref.at[micro])
        copies.start(cos_v.at[micro], cos_ref.at[micro])
        copies.start(sin_v.at[micro], sin_ref.at[micro])
    copies.finish()


def spread(values, pair, lane):
    base = values if pair == 0 else pltpu.roll(values, 64, 1)
    by_one = pltpu.roll(base, 32, 1)
    by_two = pltpu.roll(base, 64, 1)
    return jnp.where(lane < 32, base, jnp.where(lane < 96, by_one, by_two))


def tables(kinds, frequency):
    shapes = [(MICRO, KEYS, 128), (MICRO, ROWS, WIDTH), (MICRO, ROWS, WIDTH)]
    return pl.pallas_call(
        tables_kernel,
        out_shape=[jax.ShapeDtypeStruct(shape, f32) for shape in shapes],
        in_specs=[pl.BlockSpec(memory_space=pltpu.SMEM), ANY],
        out_specs=[ANY] * 3,
        scratch_shapes=[vmem(1, WIDTH, dtype=f32)]
        + [vmem(*shape, dtype=f32) for shape in shapes]
        + [pltpu.SemaphoreType.DMA((8,))],
        compiler_params=pltpu.CompilerParams(vmem_limit_bytes=VMEM_LIMIT),
        name="tables",
    )(kinds, frequency)


def live_rows_of(kinds):
    rows = jnp.broadcast_to(jnp.arange(ROWS, dtype=jnp.int32).astype(f32)[None, :], (MICRO, ROWS))
    return places(kinds[:, None], rows)[3].reshape(-1, 1)


def product_kernel(
    offset, block, core_ref, left_in, right_in, other_ref, own_ref, sums_ref,
    other_v, own_v, right_v, other_out, own_out, sums_out, sems,
):
    copies = Copies(sems)
    core = core_ref[0]
    half = left_in.shape[1] // 2
    rows = other_v.shape[1]
    get_right = copies.start(right_in, right_v)
    get_other = copies.start(left_in.at[:, pl.ds(pl.multiple_of((1 - core) * half + offset, 128), rows)], other_v)
    get_own = copies.start(left_in.at[:, pl.ds(pl.multiple_of(core * half + offset, 128), rows)], own_v)
    copies.wait(get_right)
    for get, part_v, part_out, ref in (
        (get_other, other_v, other_out, other_ref),
        (get_own, own_v, own_out, own_ref),
    ):
        copies.wait(get)

        for at in range(0, rows, block):
            lanes = pl.ds(at, block)
            part_out[lanes, :] = lax.dot_general(
                part_v[:, lanes], right_v[...], TN, preferred_element_type=f32
            ).astype(bf16)
            copies.start(part_out.at[lanes], ref.at[lanes])
    sums_out[...] = jnp.dot(jnp.ones((16, right_v.shape[0]), bf16), right_v[...], preferred_element_type=f32)[:8]
    copies.start(sums_out, sums_ref)
    copies.finish()


def product_call(core, left, right, offset, rows):
    left = left.reshape(MICRO * ROWS, left.shape[-1])
    right = right.reshape(MICRO * ROWS, right.shape[-1])
    count, width = right.shape
    block = 512 if rows % 512 == 0 else 384
    return pl.pallas_call(
        partial(product_kernel, offset, block),
        out_shape=[jax.ShapeDtypeStruct((rows, width), bf16)] * 2 + [jax.ShapeDtypeStruct((8, width), f32)],
        in_specs=[pl.BlockSpec(memory_space=pltpu.SMEM), ANY, ANY],
        out_specs=[ANY] * 3,
        scratch_shapes=[
            vmem(count, rows), vmem(count, rows), vmem(count, width), vmem(rows, width), vmem(rows, width),
            vmem(8, width, dtype=f32), pltpu.SemaphoreType.DMA((16,)),
        ],
        compiler_params=pltpu.CompilerParams(vmem_limit_bytes=VMEM_LIMIT),
        name="weight_grad",
    )(core, left, right)


SMALL_AT = (WIDTH, WIDTH, 3 * WIDTH, WIDTH, WIDTH, WIDTH, WIDTH, WIDTH, HIDDEN, WIDTH)
SMALL_ROWS = 32


def small_kernel(small_in, qkv_in, proj_in, up_in, down_in, low_ref, high_ref, *scratch):
    small_v, qkv_v, proj_v, up_v, down_v, rows_v, low_v, high_v, sems = scratch
    copies = Copies(sems)
    for source, target in ((small_in, small_v), (qkv_in, qkv_v), (proj_in, proj_v), (up_in, up_v), (down_in, down_v)):
        copies.start(source, target)
    copies.finish()
    rows_v[...] = jnp.zeros_like(rows_v)
    small = small_v[0] + small_v[1]
    parts = [small[2:3], small[3:4]]
    parts += [qkv_v[0:1, at : at + WIDTH] for at in range(0, 3 * WIDTH, WIDTH)]
    parts += [small[4:5], small[5:6], proj_v[0:1, :], small[0:1], small[1:2]]
    parts += [up_v[0:1, at : at + WIDTH] for at in range(0, HIDDEN, WIDTH)]
    parts += [down_v[0:1, :]]
    for index, part in enumerate(parts):
        rows_v[index : index + 1, :] = part
    half = SMALL_ROWS // 2
    low_v[...] = rows_v[:half, :].astype(bf16)
    high_v[...] = rows_v[half:, :].astype(bf16)
    copies.start(low_v, low_ref)
    copies.start(high_v, high_ref)
    copies.finish()


def small_call(small, qkv, proj, up, down):
    half = (SMALL_ROWS // 2, WIDTH)
    return pl.pallas_call(
        small_kernel,
        out_shape=[jax.ShapeDtypeStruct(half, bf16)] * 2,
        in_specs=[ANY] * 5,
        out_specs=[ANY] * 2,
        scratch_shapes=[
            vmem(MICRO, 8, WIDTH, dtype=f32), vmem(8, 3 * WIDTH, dtype=f32), vmem(8, WIDTH, dtype=f32),
            vmem(8, HIDDEN, dtype=f32), vmem(8, WIDTH, dtype=f32), vmem(SMALL_ROWS, WIDTH, dtype=f32),
            vmem(*half), vmem(*half), pltpu.SemaphoreType.DMA((8,)),
        ],
        name="small_grads",
    )(small, qkv, proj, up, down)


def send(value, source, target):
    return lax.ppermute(value, "section", [(source, target)])


def gathered(part, target, sections):
    pieces = [part if source == target else send(part, source, target) for source in range(sections)]
    return jnp.concatenate(pieces, axis=0)


def handed_out(output, grads, sections):
    section, last = lax.axis_index("section"), sections - 1
    share = output.shape[0] // sections

    def rows(whole, target):
        return whole[target * share : (target + 1) * share]

    output_share, grad_share = rows(output, last), rows(grads, 0)
    for target in range(last):
        mirror = last - target
        piece = jnp.where(section == last, rows(output, target), rows(grads, mirror))
        piece = lax.ppermute(piece, "section", [(last, target), (0, mirror)])
        output_share = jnp.where(section == target, piece, output_share)
        grad_share = jnp.where(section == mirror, piece, grad_share)
    return output_share, grad_share


def added(one, other):
    return (one.astype(f32) + other.astype(f32)).astype(bf16)


def both_cores(pairs):
    return [(2 * a + core, 2 * b + core) for a, b in pairs for core in range(2)]


def core_swap():
    return [(i, i ^ 1) for i in range(lax.axis_size("dp"))]


class Relay:
    def __init__(self):
        self.chunks, self.sums, self.totals = [], [], []
        self.flying, self.joined, self.clock = [], [], 0

    def start(self, value, pairs, then, keep, age, chunk=False):
        self.flying.append((self.clock + age, lax.ppermute(value, "dp", pairs), then, keep, chunk))

    def step(self, *gate, outer=0, inner=0, ahead=0):
        ready = [f for f in self.flying if f[0] <= self.clock + ahead]
        self.flying = [f for f in self.flying if f[0] > self.clock + ahead]
        fresh, self.chunks = self.chunks[:outer], self.chunks[outer:]
        arrays, keeps = [f[1] for f in ready], [f[3] for f in ready]
        new = [value for value, _ in fresh]
        joined, self.joined = self.joined, []
        results = [item.result for item in joined]
        arrays, keeps, new, gate, results = lax.optimization_barrier((arrays, keeps, new, gate, results))
        for item, result in zip(joined, results):
            item.result = result
        for (_, _, then, _, _), array, keep in zip(ready, arrays, keeps):
            then(array, keep)
        fresh = [(value, done) for value, (_, done) in zip(new, fresh)]
        for _ in range(outer):
            self.outer_start(fresh.pop(0) if fresh else None, self.totals.pop(0) if self.totals else None)
        for _ in range(min(inner, len(self.sums))):
            self.inner_start(*self.sums.pop(0))
        self.clock += 1
        return gate[0] if len(gate) == 1 else gate

    def inner_start(self, both, done):
        pairs = both_cores([(1, 2), (2, 1)])
        self.start(both, pairs, lambda array, keep: self.totals.append((added(keep, array), done)), both, 2)

    def outer_start(self, chunk, total):
        inward, outward = both_cores([(0, 1), (3, 2)]), both_cores([(1, 0), (2, 3)])
        chip = lax.axis_index("dp") // 2
        outer = (chip == 0) | (chip == 3)

        def inner_sum(array, own):
            self.sums.append((added(own, array), chunk[1]))

        def result(array, own):
            total[1](jnp.where(outer, array, own))

        if chunk and total and chunk[0].shape == total[0].shape:
            def land(array, keep):
                inner_sum(array, keep[0])
                result(array, keep[1])

            value = jnp.where(outer, chunk[0], total[0])
            self.start(value, inward + outward, land, (chunk[0], total[0]), 3, True)
        else:
            if total:
                self.start(total[0], outward, result, total[0], 3 if self.chunks or chunk else 8)
            if chunk:
                self.start(chunk[0], inward, inner_sum, chunk[0], 3, True)

    def finish(self):
        while self.chunks:
            self.pulse()
        while any(flight[0] > self.clock - 1 and flight[4] for flight in self.flying):
            self.step(outer=4, inner=4)
        while self.sums or self.totals or self.flying:
            self.step(outer=4, inner=4, ahead=9)
            self.step(outer=4, inner=4, ahead=2)

    def pulse(self, *gate):
        return self.step(*gate, inner=self.clock % 2, outer=1 - self.clock % 2)


class LineSum:
    def __init__(self, relay, axis):
        self.relay, self.axis, self.count = relay, axis, 0
        self.totals, self.result = {}, None

    def add(self, other, mine, ends):
        half = added(mine, lax.ppermute(other, "dp", core_swap()))
        for chunk in jnp.split(half, ends, axis=self.axis):
            self.relay.chunks.append((chunk, partial(self.landed, self.count)))
            self.count += 1

    def landed(self, index, total):
        self.totals[index] = total
        if len(self.totals) == self.count:
            mine = jnp.concatenate([self.totals[i] for i in range(self.count)], axis=self.axis)
            self.relay.start(mine, core_swap(), self.join, mine, 2)

    def join(self, other, mine):
        core = lax.axis_index("dp") % 2
        low, high = jnp.where(core == 0, mine, other), jnp.where(core == 0, other, mine)
        self.result = jnp.concatenate([low, high], axis=0).astype(f32)
        self.relay.joined.append(self)


def summed_by_compiler(part):
    count, rows = lax.axis_size("dp"), part.shape[0]
    part = jnp.pad(part, ((0, -rows % count), (0, 0)))
    own = lax.psum_scatter(part, "dp", scatter_dimension=0, tiled=True)
    return lax.all_gather(own, "dp", axis=0, tiled=True)[:rows].astype(f32)


def per_device(
    tokens,
    cotangent,
    image_kind,
    norm_one_gain,
    norm_one_bias,
    qkv_weight,
    qkv_bias,
    rotary_freq,
    proj_weight,
    proj_bias,
    norm_two_gain,
    norm_two_bias,
    up_weight,
    up_bias,
    down_weight,
    down_bias,
):
    sections = lax.axis_size("section")
    section = lax.axis_index("section")
    last = sections - 1
    by_line = lax.axis_size("dp") == 8
    scal = section.astype(jnp.int32).reshape(1)
    core = (lax.axis_index("dp") % 2).astype(jnp.int32).reshape(1)
    low = core[0] == 0
    common = tables(image_kind, rotary_freq)
    weights = (qkv_weight[0], proj_weight[0], up_weight[0], down_weight[0])
    vecs = (
        norm_one_gain, norm_one_bias, qkv_bias, proj_bias, norm_two_gain, norm_two_bias, up_bias, down_bias,
    )
    first_in = gathered(tokens, 0, sections)
    live_rows = live_rows_of(image_kind)
    last_in = gathered(cotangent, last, sections)
    last_in = jnp.where(live_rows > 0, last_in, bf16(0.0))

    def turn(layer, micro):
        return jnp.array([layer, micro], jnp.int32)

    states = None
    values = [first_in[m * ROWS : (m + 1) * ROWS] for m in range(MICRO)]
    backs, out_grads = None, None
    for layer in range(sections):
        for micro in range(MICRO):
            earlier = tokens
            if layer == last and micro == 1:
                fronts = dict(zip(STATES, states))
                turned, backs = back_call(scal, turn(last, 0), grads[0], common, weights, vecs, fronts, None)
                earlier = turned
            out, states = front_call(scal, turn(layer, micro), values[micro], common, weights, vecs, states, earlier)
            values[micro] = send(out, layer, layer + 1) if layer < last else out
        if layer == 1:
            values[0], last_in = lax.optimization_barrier((values[0], last_in))
            grads = [last_in[m * ROWS : (m + 1) * ROWS] for m in range(MICRO)]
            out_grads = list(grads)
    fronts = dict(zip(STATES, states))
    relay = Relay()
    sums = [LineSum(relay, axis) for axis in (1, 0, 1, 0)]
    plain = [[], [], [], []]

    def to_sum(index, other, mine, ends):
        if by_line:
            sums[index].add(other, mine, ends)
        else:
            plain[index].append((jnp.where(low, mine, other), jnp.where(low, other, mine)))

    for layer in reversed(range(sections)):
        if 0 < layer < last:
            out_grads = [jnp.where(section == layer, new, old) for new, old in zip(grads, out_grads)]
        if layer == 0:
            received = grads[0]
        for micro in range(MICRO):
            end = layer == 0 and micro == MICRO - 1
            if end:
                grads[0], grads[1], out_grads = lax.optimization_barrier((grads[0], grads[1], out_grads))
                out_grads = [jnp.where(section == 0, new, old) for new, old in zip((received, grads[1]), out_grads)]
                all_grads = jnp.concatenate(out_grads, axis=0)
                for offset in (0, 768):
                    other, mine, b_down = product_call(core, fronts["g"], all_grads, offset, 768)
                    to_sum(3, other, mine, [384])
                grads[1] = relay.step(grads[1], outer=2)
            if layer == last and micro == 0:
                dx = turned
            else:
                dx, backs = back_call(scal, turn(layer, micro), grads[micro], common, weights, vecs, fronts, backs)
            if end:
                values[0], values[1], dx, backs = relay.step(*values, dx, backs, outer=1, inner=1, ahead=9)
            grads[micro] = send(dx, layer, layer - 1) if layer > 0 else dx
    backs = dict(zip(BACKS, backs))
    other, mine, b_up = product_call(core, fronts["c"], backs["du"], 0, WIDTH // 2)
    to_sum(2, other, mine, [768, 1536, 2304])
    final = jnp.where(live_rows > 0, jnp.concatenate(values, axis=0), bf16(0.0))
    block_out, grad_tokens = handed_out(final, jnp.concatenate(grads, axis=0), sections)
    b_up, block_out, grad_tokens, dqkv = relay.step(
        b_up, block_out, grad_tokens, backs["dqkv"], outer=1, inner=1, ahead=9
    )
    other, mine, b_qkv = product_call(core, fronts["a"], dqkv, 0, WIDTH // 2)
    to_sum(0, other, mine, [768, 1536])
    other, mine, b_proj = product_call(core, fronts["o"], backs["dz"], 0, WIDTH // 2)
    lows, highs = small_call(backs["small"], b_qkv, b_proj, b_up, b_down)
    mine = jnp.concatenate([mine, jnp.where(low, lows, highs)], axis=0)
    other = jnp.concatenate([other, jnp.where(low, highs, lows)], axis=0)
    other, mine = relay.step(other, mine, outer=1, inner=1, ahead=9)
    to_sum(1, other, mine, [])
    relay.clock += relay.clock % 2
    relay.finish()
    if by_line:
        grad_qkv, grad_proj, grad_up, grad_down = (item.result for item in sums)
    else:
        grad_qkv, grad_proj, grad_up, grad_down = (
            summed_by_compiler(jnp.concatenate([part[side] for side in range(2) for part in parts], axis=0))
            for parts in plain
        )
    middle, half = WIDTH // 2, SMALL_ROWS // 2
    small = jnp.concatenate([grad_proj[middle : middle + half], grad_proj[middle + half + middle :]], axis=0)
    grad_proj = jnp.concatenate([grad_proj[:middle], grad_proj[middle + half : middle + half + middle]], axis=0)
    turns = small[5:7].reshape(2, HEADS, 2, 32)
    freq = (turns[:, :, 1] - turns[:, :, 0]).reshape(1, WIDTH)
    g_one, b_one, b_proj, g_two, b_two, b_down = (small[i : i + 1] for i in (0, 1, 7, 8, 9, 14))
    b_qkv, b_up = small[2:5].reshape(1, -1), small[10:14].reshape(1, -1)
    return (
        block_out, grad_tokens.astype(f32), g_one, b_one, grad_qkv[None], b_qkv, freq,
        grad_proj[None], b_proj, g_two, b_two, grad_up[None], b_up, grad_down[None], b_down,
    )


def solution(mesh):
    row = P(("dp", "section"), None)
    vector = P("section", None)
    matrix = P("section", None, None)
    params = (
        vector, vector, matrix, vector, vector, matrix, vector, vector, vector, matrix, vector, matrix, vector,
    )
    return jax.shard_map(
        per_device,
        mesh=mesh,
        in_specs=(row, row, P("dp")) + params,
        out_specs=(row, row) + params,
        check_vma=False,
    )
```
